128 devices in a mesh: gx: 8 (over z, core), gy: 16 (over x, y).
Axes of the slice: x: 4, y: 4, z: 4, core: 2. Of those that a mesh axis runs over, the one named last changes fastest.
Arguments:
- state: float32 [22, 4, 512, 2048], P(None, None, 'gx', 'gy')
- chemical_masses_per_mole: float32 [21], replicated, may hold values from 2 to 32
- pairwise_transport_reciprocals: float32 [21, 21], replicated, may hold values from 1 to 4
- rate_scale: float32 [84], replicated, may hold values from 10 to 3000
- arrhenius_energy: float32 [84], replicated, may hold values from 0.5 to 4
- reactants: int32 [84, 21], replicated, may hold values from 0 to 1, as said below
- products: int32 [84, 21], replicated, may hold values from 0 to 1, as said below
- heat_release: float32 [21], replicated, may hold values from -16 to 16
- box_cost: int32 [16, 64], P('gx', 'gy'), may hold values from 1 to 6, as said below
- box_owner: int32 [16, 64], P('gx', 'gy'), may hold values from 0 to 15, as said below
- flame_flag: int32 [16, 64], P('gx', 'gy'), may hold values from 0 to 1, as said below
Outputs:
- new_state: float32 [22, 4, 512, 2048], P(None, None, 'gx', 'gy')
- chemistry_load: float32 [8, 16], P('gx', 'gy')
The draws below stay inside these ranges and needn't reach their ends.
Inputs may be any that keep to these rules, and one draw needn't show every extreme that they name: `reactants`: every row has exactly two ones, in different columns. `products`: every row has exactly two ones, in different columns. `flame_flag`: in every row of boxes along x the flame boxes are 4 boxes in a row along y, counted cyclically. `box_cost`: flame boxes take 4 to 6 iterations, the others 1 or 2. `box_owner`: a box's owner lies in the box's own index along gx; the boxes of one device have distinct owners, and every owner receives exactly 8 boxes.
All inputs are finite; a program needn't handle non-finite values.
Results may differ from the reference program's by a relative error of at most 0.0003.
Values sent between devices are 32-bit elements; how exact they have to be, the bound alone decides.
No kernel may reach another device: no remote copies, remote signals or barrier semaphores. Data moves between devices by JAX's collectives and lax.ppermute only.
A program may use at most 128 MiB of HBM per device.

```python
import math
import jax
import jax.numpy as jnp
from jax import lax

NSP = 21
R = 84
BOX = 32
NZ = 4
CX = 64
CY = 128
CMAX = 6
NX = 512
NY = 2048
N_GX = 8
N_GY = 16


def flame_offset(key):
    centre = jax.random.randint(key, (NX // BOX, 1), 0, NY // BOX)
    return (jnp.arange(NY // BOX, dtype=jnp.int32)[None, :] - centre) % (NY // BOX)


def pair_table(key):
    key_first, key_second = jax.random.split(key)
    initial_outcome = jax.random.randint(key_first, (R,), 0, NSP)
    second = (initial_outcome + 1 + jax.random.randint(key_second, (R,), 0, NSP - 1)) % NSP
    columns = jnp.arange(NSP, dtype=jnp.int32)
    return ((columns[None, :] == initial_outcome[:, None]) | (columns[None, :] == second[:, None])).astype(jnp.int32)


def draw_state(key, part):
    key = jax.random.fold_in(key, 11)
    key_species, key_heat = jax.random.split(key)
    shape = (NSP, NZ, NX, NY)
    raw = jnp.exp(jax.random.uniform(key_species, shape, jnp.float32, jnp.log(0.05), 0.0))
    heated = jax.random.uniform(key_heat, shape[1:], jnp.float32, 1.0, 2.2)
    composition_shares = raw / jnp.sum(raw, axis=0, keepdims=True)
    return jnp.concatenate([composition_shares, heated[None]], 0)


def draw_reactants(key, part):
    key = jax.random.fold_in(key, 13)
    return pair_table(key)


def draw_products(key, part):
    key = jax.random.fold_in(key, 17)
    return pair_table(key)


def draw_flame_flag(key, part):
    offset = flame_offset(key)
    return (offset < CY // BOX).astype(jnp.int32)


def draw_box_cost(key, part):
    offset = flame_offset(key)
    key = jax.random.fold_in(key, 7)
    marked_blocks = offset < CY // BOX
    spread = jax.random.randint(key, offset.shape, 0, 3)
    marker = (offset == 0) & (jnp.arange(NX // BOX, dtype=jnp.int32)[:, None] == 0)
    spread = jnp.where(marker, 0, spread)
    return jnp.where(marked_blocks, CMAX - spread, 1 + spread % 2).astype(jnp.int32)


def draw_box_owner(key, part):
    key = jax.random.fold_in(key, 9)
    per_x = CX // BOX
    per_y = CY // BOX
    keys = jax.random.split(key, N_GX)
    offsets = jax.vmap(lambda single: jax.random.permutation(single, N_GY)[:per_x * per_y])(keys)
    offsets = offsets.reshape(N_GX, per_x, 1, per_y)
    senders = jnp.arange(N_GY, dtype=jnp.int32).reshape(1, 1, N_GY, 1)
    owners = (senders + offsets) % N_GY
    return owners.reshape(NX // BOX, NY // BOX).astype(jnp.int32)


def normal_values(own_key, dims, scale, most, held_as=jnp.bfloat16):
    drawn = jax.random.normal(own_key, dims, jnp.float32) * scale
    return jnp.minimum(jnp.maximum(drawn, -most), most).astype(held_as)


def setup_inputs(seed: int = 0) -> dict:
    key_list = jax.random.split(jax.random.key(seed), 12)
    state = draw_state(jax.random.fold_in(key_list[11], 71), 0)
    chemical_masses_per_mole = jnp.clip(jnp.exp(jax.random.uniform(key_list[1], (NSP,), jnp.float32, math.log(2.0), math.log(32.0))), 2.0, 32.0)
    pairwise_transport_reciprocals = jnp.clip(jnp.exp(jax.random.uniform(key_list[2], (NSP, NSP), jnp.float32, math.log(1.0), math.log(4.0))), 1.0, 4.0)
    rate_scale = jnp.clip(jnp.exp(jax.random.uniform(key_list[3], (R,), jnp.float32, math.log(10.0), math.log(3000.0))), 10.0, 3000.0)
    arrhenius_energy = jnp.clip(jnp.exp(jax.random.uniform(key_list[4], (R,), jnp.float32, math.log(0.5), math.log(4.0))), 0.5, 4.0)
    reactants = draw_reactants(jax.random.fold_in(key_list[11], 71), 0)
    products = draw_products(jax.random.fold_in(key_list[11], 71), 0)
    heat_release = normal_values(key_list[7], (NSP,), 4.0, 16.0, jnp.float32)
    box_cost = draw_box_cost(jax.random.fold_in(key_list[11], 71), 0)
    box_owner = draw_box_owner(jax.random.fold_in(key_list[11], 71), 0)
    flame_flag = draw_flame_flag(jax.random.fold_in(key_list[11], 71), 0)
    return dict(state=state, chemical_masses_per_mole=chemical_masses_per_mole, pairwise_transport_reciprocals=pairwise_transport_reciprocals, rate_scale=rate_scale, arrhenius_energy=arrhenius_energy, reactants=reactants, products=products, heat_release=heat_release, box_cost=box_cost, box_owner=box_owner, flame_flag=flame_flag)


HIGHEST = lax.Precision.HIGHEST
CFL_SAFE = 0.5
Z_WEIGHT = 0.25
DT_CHEM = 0.5


def blend_transport_factor(composition_shares, local_thermal_state, chemical_masses_per_mole, pairwise_transport_reciprocals):
    amounts = composition_shares / chemical_masses_per_mole[:, None, None, None]
    amount_sum = jnp.sum(amounts, axis=0)
    fractions = amounts / amount_sum
    cross_table = pairwise_transport_reciprocals * (1.0 - jnp.eye(pairwise_transport_reciprocals.shape[0], dtype=pairwise_transport_reciprocals.dtype))
    transport_impedance = jnp.einsum('jk,jzab->kzab', cross_table, fractions, precision=HIGHEST)
    return (1.0 - composition_shares) * local_thermal_state ** 1.5 / transport_impedance


def face_term(centre, centre_coef, beside, beside_coef):
    return 0.5 * (centre_coef + beside_coef) * (beside - centre)


def divergence(field, neighbour_weighting):
    centre = field[:, :, 1:-1, 1:-1]
    centre_coef = neighbour_weighting[:, :, 1:-1, 1:-1]
    result = face_term(centre, centre_coef, field[:, :, 2:, 1:-1], neighbour_weighting[:, :, 2:, 1:-1])
    result = result + face_term(centre, centre_coef, field[:, :, :-2, 1:-1], neighbour_weighting[:, :, :-2, 1:-1])
    result = result + face_term(centre, centre_coef, field[:, :, 1:-1, 2:], neighbour_weighting[:, :, 1:-1, 2:])
    result = result + face_term(centre, centre_coef, field[:, :, 1:-1, :-2], neighbour_weighting[:, :, 1:-1, :-2])
    upward = face_term(centre[:, :-1], centre_coef[:, :-1], centre[:, 1:], centre_coef[:, 1:])
    closed = jnp.zeros_like(centre[:, :1])
    return result + Z_WEIGHT * (jnp.concatenate([upward, closed], 1) - jnp.concatenate([closed, upward], 1))


def matched_segments(composition_shares, local_thermal_state, neighbour_weighting, clock_delta, chemical_masses_per_mole, pairwise_transport_reciprocals):
    initial_outcome = composition_shares[:, :, 1:-1, 1:-1] + clock_delta * divergence(composition_shares, neighbour_weighting)
    prefactor_value = blend_transport_factor(initial_outcome, local_thermal_state[:, 1:-1, 1:-1], chemical_masses_per_mole, pairwise_transport_reciprocals)
    return initial_outcome[:, :, 1:-1, 1:-1] + clock_delta * divergence(initial_outcome, prefactor_value)


def chemistry(grid_quantities, iterations, marked_blocks, chemical_masses_per_mole, natural_log_prefactor, arrhenius_energy, react_table, react_back, make_back, heat_release):
    component_number = chemical_masses_per_mole.shape[0]
    composition_shares = grid_quantities[:component_number]
    local_thermal_state = grid_quantities[component_number]
    start = composition_shares / chemical_masses_per_mole[:, None]
    natural_log_speed = natural_log_prefactor[:, None] - arrhenius_energy[:, None] / local_thermal_state[None, :]

    def sweep(index, conc):
        progress = jnp.exp(natural_log_speed + jnp.dot(react_table, jnp.log(conc), precision=HIGHEST, preferred_element_type=jnp.float32))
        gained = jnp.dot(make_back, progress, precision=HIGHEST, preferred_element_type=jnp.float32)
        lost = jnp.dot(react_back, progress, precision=HIGHEST, preferred_element_type=jnp.float32)
        return (start + DT_CHEM * gained) / (1.0 + DT_CHEM * lost / conc)

    conc = lax.fori_loop(jnp.int32(0), iterations.astype(jnp.int32), sweep, start)
    advanced_composition = conc * chemical_masses_per_mole[:, None]
    enthalpy_source = jnp.sum(heat_release[:, None] * (advanced_composition - composition_shares), axis=0)
    revised_thermal_state = local_thermal_state + marked_blocks.astype(grid_quantities.dtype) * enthalpy_source
    return jnp.concatenate([advanced_composition, revised_thermal_state[None]], 0)


def to_boxes(grid_quantities):
    components, planes, rows, columns = grid_quantities.shape
    pieces = grid_quantities.reshape(components, planes, rows // BOX, BOX, columns // BOX, BOX)
    return pieces.transpose(2, 4, 0, 1, 3, 5).reshape((rows // BOX) * (columns // BOX), components, planes * BOX * BOX)


def from_boxes(boxes, planes, rows, columns):
    components = boxes.shape[1]
    pieces = boxes.reshape(rows // BOX, columns // BOX, components, planes, BOX, BOX)
    return pieces.transpose(2, 3, 0, 4, 1, 5).reshape(components, planes, rows, columns)


def reference(state, chemical_masses_per_mole, pairwise_transport_reciprocals, rate_scale, arrhenius_energy, reactants, products, heat_release, box_cost, box_owner, flame_flag):
    component_number = chemical_masses_per_mole.shape[0]
    haloed_grid_values = jnp.pad(state, ((0, 0), (0, 0), (2, 2), (2, 2)), mode='wrap')
    composition_shares = haloed_grid_values[:component_number]
    local_thermal_state = haloed_grid_values[component_number]
    neighbour_weighting = blend_transport_factor(composition_shares, local_thermal_state, chemical_masses_per_mole, pairwise_transport_reciprocals)
    peak = jnp.max(neighbour_weighting[:, :, 2:-2, 2:-2])
    clock_delta = CFL_SAFE / ((4.0 + 2.0 * Z_WEIGHT) * peak)
    spread_mass_shares = matched_segments(composition_shares, local_thermal_state, neighbour_weighting, clock_delta, chemical_masses_per_mole, pairwise_transport_reciprocals)
    grid_quantities = jnp.concatenate([spread_mass_shares, state[component_number:]], 0)
    boxes = to_boxes(grid_quantities)
    react_table = reactants.astype(state.dtype)
    react_back = react_table.T
    make_back = products.astype(state.dtype).T
    natural_log_prefactor = jnp.log(rate_scale)

    def integrate(member):
        return chemistry(member[0], member[1], member[2], chemical_masses_per_mole, natural_log_prefactor, arrhenius_energy, react_table, react_back, make_back, heat_release)

    worked = lax.map(integrate, (boxes, box_cost.reshape(-1), flame_flag.reshape(-1)))
    new_state = from_boxes(worked, state.shape[1], state.shape[2], state.shape[3])
    slot_ids = jnp.arange(N_GY, dtype=jnp.int32)
    chosen = (box_owner[:, :, None] == slot_ids[None, None, :]).astype(state.dtype) * box_cost[:, :, None].astype(state.dtype)
    per_row = jnp.sum(chosen, axis=1).reshape(N_GX, CX // BOX, N_GY).sum(axis=1)
    chemistry_load = per_row / (jnp.sum(per_row, axis=1, keepdims=True) / N_GY)
    return new_state, chemistry_load
```

```python
import functools

import jax
import jax.numpy as jnp
from jax import lax
from jax.experimental import pallas as pl
from jax.experimental.pallas import tpu as pltpu
from jax.sharding import PartitionSpec as P

SPECIES = 21
FIELDS = 22
SUB = 24
LANES = 128
PLANES = 4
ROWS = 64
HROWS = ROWS + 4
BOX = 32
REACTIONS = 84
RPAD = 88
CHUNK = 4
BOX_CHUNK = 4
Z_WEIGHT = 0.25
CFL_SAFE = 0.5
HALF = 0.5
VMEM_BYTES = 56 * 1024 * 1024

f32 = jnp.float32
bf16 = jnp.bfloat16


def coarse(x):
    return x.astype(bf16).astype(f32)


def diffusivity(rows, inv_mass, table, live):
    amounts = jnp.concatenate([row * inv_mass for row in rows], axis=1)
    high = coarse(amounts)
    low = amounts - high
    blank = jnp.zeros((8, amounts.shape[1]), f32)
    stacked = jnp.concatenate([high, low, high, blank], axis=0).astype(bf16)
    sums = jnp.dot(table, stacked, preferred_element_type=f32)
    result = []
    for i, row in enumerate(rows):
        lanes = slice(i * LANES, (i + 1) * LANES)
        heat = row[SPECIES : SPECIES + 1, :]
        scale = (HALF * heat * jnp.sqrt(heat)) * sums[SUB : SUB + 8, lanes]
        scale = jnp.concatenate([scale] * 3, axis=0)
        result.append(live * (1.0 - row) * scale / sums[:SUB, lanes])
    return result


def peak_kernel(state, inv_mass_ref, live_ref, table_ref, peak):
    flat = state.reshape(FIELDS * ROWS, LANES)
    inv_mass = inv_mass_ref[...]
    live = live_ref[...]
    table = table_ref[...]
    ones = jnp.ones((SUB - FIELDS, LANES), f32)

    def body(step, best):
        rows = [
            jnp.concatenate([flat[pl.ds(step * CHUNK + i, FIELDS, stride=ROWS), :], ones], axis=0)
            for i in range(CHUNK)
        ]
        for value in diffusivity(rows, inv_mass, table, live):
            best = jnp.maximum(best, value)
        return best

    best = lax.fori_loop(0, ROWS // CHUNK, body, jnp.zeros((SUB, LANES), f32), unroll=2)

    @pl.when(pl.program_id(0) == 0)
    def _():
        peak[...] = best

    @pl.when(pl.program_id(0) > 0)
    def _():
        peak[...] = jnp.maximum(peak[...], best)


def local_peak(state, inv_mass, live, table):
    whole = lambda z: (0, 0)
    return pl.pallas_call(
        peak_kernel,
        grid=(PLANES,),
        in_specs=[
            pl.BlockSpec((FIELDS, None, ROWS, LANES), lambda z: (0, z, 0, 0)),
            pl.BlockSpec((SUB, LANES), whole),
            pl.BlockSpec((SUB, LANES), whole),
            pl.BlockSpec((SUB + 8, 3 * SUB + 8), whole),
        ],
        out_specs=pl.BlockSpec((SUB, LANES), whole),
        out_shape=jax.ShapeDtypeStruct((SUB, LANES), f32),
        compiler_params=pltpu.CompilerParams(vmem_limit_bytes=VMEM_BYTES),
    )(state, inv_mass, live, table)


def edge_rows_kernel(first, last, low, high):
    for k in range(FIELDS):
        for z in range(PLANES):
            at = (k * PLANES + z) * 2
            low[at : at + 2, :] = first[k, z, 0:2, :]
            high[at : at + 2, :] = last[k, z, 6:8, :]


def edge_rows(state):
    shape = jax.ShapeDtypeStruct((FIELDS * PLANES * 2, LANES), f32)
    return pl.pallas_call(
        edge_rows_kernel,
        grid=(1,),
        in_specs=[
            pl.BlockSpec((FIELDS, PLANES, 8, LANES), lambda i: (0, 0, 0, 0)),
            pl.BlockSpec((FIELDS, PLANES, 8, LANES), lambda i: (0, 0, ROWS // 8 - 1, 0)),
        ],
        out_specs=[pl.BlockSpec(shape.shape, lambda i: (0, 0))] * 2,
        out_shape=[shape, shape],
        compiler_params=pltpu.CompilerParams(vmem_limit_bytes=VMEM_BYTES),
    )(state, state)


def strips_kernel(state, below, above, own, to_left, to_right):
    lane = lax.broadcasted_iota(jnp.int32, (8, LANES), 1)
    sub = lax.broadcasted_iota(jnp.int32, (8, LANES), 0)
    pairs = FIELDS * PLANES
    for group in range(3):
        count = min(32, pairs - group * 32)

        def body(index, held):
            pair = group * 32 + index
            blocks = [state[pl.ds(pl.multiple_of(pair * ROWS + i * 8, 8), 8), :] for i in range(8)]
            after = jnp.broadcast_to(above[pl.ds(pair * 2, 1), :], (8, LANES))
            before = jnp.broadcast_to(below[pl.ds(pair * 2 + 1, 1), :], (8, LANES))
            blocks.append(jnp.where(sub == 0, after, before))
            mine = (lane >> 2) == index
            return tuple(
                jnp.where(mine, pltpu.roll(block, 4 * index + 2, 1), old)
                for block, old in zip(blocks, held)
            )

        held = lax.fori_loop(0, count, body, (jnp.ones((8, LANES), f32),) * 9, unroll=4)
        block = jnp.concatenate(list(held[:8]) + [held[8]] * 8, axis=0)
        turned = block.T
        own[group * 128 : group * 128 + 4 * count, :] = turned[: 4 * count, :]
    for c in range(2):
        to_right[pl.ds(c, pairs, stride=2), :] = own[pl.ds(c, pairs, stride=4), :]
        to_left[pl.ds(c, pairs, stride=2), :] = own[pl.ds(2 + c, pairs, stride=4), :]


def strips(flat_state, below, above):
    pairs = FIELDS * PLANES
    return pl.pallas_call(
        strips_kernel,
        out_shape=[
            jax.ShapeDtypeStruct((pairs * 4, LANES), f32),
            jax.ShapeDtypeStruct((pairs * 2, LANES), f32),
            jax.ShapeDtypeStruct((pairs * 2, LANES), f32),
        ],
        compiler_params=pltpu.CompilerParams(vmem_limit_bytes=VMEM_BYTES),
    )(flat_state, below, above)


def swap_quarters(planes, lane):
    low_half = lane < 64
    even = ((lane >> 5) & 1) == 0
    a, b, c, d = planes
    a, c = (
        jnp.where(low_half, a, pltpu.roll(c, 64, 1)),
        jnp.where(low_half, pltpu.roll(a, 64, 1), c),
    )
    b, d = (
        jnp.where(low_half, b, pltpu.roll(d, 64, 1)),
        jnp.where(low_half, pltpu.roll(b, 64, 1), d),
    )
    a, b = (
        jnp.where(even, a, pltpu.roll(b, 32, 1)),
        jnp.where(even, pltpu.roll(a, 96, 1), b),
    )
    c, d = (
        jnp.where(even, c, pltpu.roll(d, 32, 1)),
        jnp.where(even, pltpu.roll(c, 96, 1), d),
    )
    return [a, b, c, d]


def substep_kernel(
    box_cost,
    flame_flag,
    state,
    below,
    above,
    left,
    right,
    own,
    gathered,
    inv_mass_ref,
    mass_ref,
    live_ref,
    heat_ref,
    table_ref,
    log_table_ref,
    sum_table_ref,
    out,
    load_out,
    field,
    coef,
    first,
    strip_field,
    strip_coef,
    strip_first,
    flux_left,
    flux_right,
    packed,
    start_ref,
    conc_ref,
    ext_ref,
):
    inv_mass = inv_mass_ref[...]
    live = live_ref[...]
    table = table_ref[...]
    lane = lax.broadcasted_iota(jnp.int32, (8, LANES), 1)
    ones2 = jnp.ones((SUB - FIELDS, LANES), f32)

    received = gathered[...]
    columns = lax.broadcasted_iota(jnp.int32, received.shape, 1)
    peak = jnp.max(jnp.where(columns == 0, received, 0.0), keepdims=True)
    step = CFL_SAFE / ((4.0 + 2.0 * Z_WEIGHT) * peak)
    mine = jnp.sum(jnp.where(columns == 1, received, 0.0))
    everyone = jnp.sum(jnp.where(columns == 2, received, 0.0))
    load_out[0, 0] = mine / (everyone / 16.0)
    step = jnp.broadcast_to(step, (8, LANES))

    def row24(value):
        return jnp.concatenate([value, ones2], axis=0)

    for z in range(PLANES):
        for layer in range(2):
            field[z * HROWS + layer] = row24(below[pl.ds(z * 2 + layer, FIELDS, stride=8), :])
            field[z * HROWS + ROWS + 2 + layer] = row24(
                above[pl.ds(z * 2 + layer, FIELDS, stride=8), :]
            )

        def bring(x, carry):
            field[z * HROWS + 2 + x] = row24(
                state[pl.ds(z * ROWS + x, FIELDS, stride=PLANES * ROWS), :]
            )
            return carry

        lax.fori_loop(0, ROWS, bring, 0, unroll=8)
        for c in range(2):
            strip_field[z * 8 + c] = row24(left[pl.ds(z * 2 + c, FIELDS, stride=8), :])
            strip_field[z * 8 + 2 + c] = row24(own[pl.ds(z * 4 + 2 + c, FIELDS, stride=16), :])
            strip_field[z * 8 + 4 + c] = row24(own[pl.ds(z * 4 + c, FIELDS, stride=16), :])
            strip_field[z * 8 + 6 + c] = row24(right[pl.ds(z * 2 + c, FIELDS, stride=8), :])

    def coefficients(source, target, count):
        def body(index, carry):
            rows = [source[index * CHUNK + i] for i in range(CHUNK)]
            for i, value in enumerate(diffusivity(rows, inv_mass, table, live)):
                target[index * CHUNK + i] = value
            return carry

        lax.fori_loop(0, count // CHUNK, body, 0, unroll=2)

    def face(source, weight, here, there, part):
        return (weight[here, part, :] + weight[there, part, :]) * (
            source[there, part, :] - source[here, part, :]
        )

    parts = [slice(0, 8), slice(8, 16), slice(16, 24)]

    def side_fluxes(source, weight):
        for z in range(PLANES):
            for part in parts:
                flux_left[z, part, :] = face(source, weight, z * 8 + 1, z * 8 + 2, part)
                flux_right[z, part, :] = face(source, weight, z * 8 + 5, z * 8 + 6, part)

    def strip_update():
        for r in (1, 2, 5, 6):
            for part in parts:
                above_flux = None
                for z in range(PLANES):
                    at = z * 8 + r
                    here = strip_field[at, part, :]
                    weight = strip_coef[at, part, :]
                    total = face(strip_field, strip_coef, at, at + 1, part)
                    total = total - face(strip_field, strip_coef, at - 1, at, part)
                    onward = (weight + pltpu.roll(weight, LANES - 1, 1)) * (
                        pltpu.roll(here, LANES - 1, 1) - here
                    )
                    total = total + (onward - pltpu.roll(onward, 1, 1))
                    if above_flux is not None:
                        total = total - Z_WEIGHT * above_flux
                    if z < PLANES - 1:
                        above_flux = face(strip_field, strip_coef, at, at + 8, part)
                        total = total + Z_WEIGHT * above_flux
                    strip_first[at, part, :] = here + step * total

    def updated(source, weight, x, part):
        result = []
        above_flux = None
        for z in range(PLANES):
            at = z * HROWS + x + 2
            here = source[at, part, :]
            coefs = weight[at, part, :]
            total = (coefs + weight[at + 1, part, :]) * (source[at + 1, part, :] - here)
            total = total + (coefs + weight[at - 1, part, :]) * (source[at - 1, part, :] - here)
            onward = (coefs + pltpu.roll(coefs, LANES - 1, 1)) * (
                pltpu.roll(here, LANES - 1, 1) - here
            )
            shift = (2 * LANES - x) & (LANES - 1)
            entering = pltpu.roll(flux_left[z, part, :], shift, 1)
            leaving = pltpu.roll(flux_right[z, part, :], (shift + LANES - 1) & (LANES - 1), 1)
            onward = jnp.where(lane == LANES - 1, leaving, onward)
            total = total + (onward - jnp.where(lane == 0, entering, pltpu.roll(onward, 1, 1)))
            if above_flux is not None:
                total = total - Z_WEIGHT * above_flux
            if z < PLANES - 1:
                over = at + HROWS
                above_flux = (coefs + weight[over, part, :]) * (source[over, part, :] - here)
                total = total + Z_WEIGHT * above_flux
            result.append(here + step * total)
        return result

    coefficients(field, coef, PLANES * HROWS)
    coefficients(strip_field, strip_coef, PLANES * 8)
    side_fluxes(strip_field, strip_coef)
    strip_update()

    def first_rows(x, carry):
        for part in parts:
            for z, value in enumerate(updated(field, coef, x - 1, part)):
                first[z * HROWS + x + 1, part, :] = value
        return carry

    lax.fori_loop(0, ROWS + 2, first_rows, 0)
    for z in range(PLANES):
        first[z * HROWS] = field[z * HROWS]
        first[z * HROWS + HROWS - 1] = field[z * HROWS + HROWS - 1]
        for r in (0, 3, 4, 7):
            strip_first[z * 8 + r] = strip_field[z * 8 + r]
    coefficients(first, coef, PLANES * HROWS)
    coefficients(strip_first, strip_coef, PLANES * 8)
    side_fluxes(strip_first, strip_coef)

    def second_rows(x, carry):
        for part in parts:
            planes = swap_quarters(updated(first, coef, x, part), lane)
            for j in range(4):
                packed[j * ROWS + x, part, :] = planes[j]
        return carry

    lax.fori_loop(0, ROWS, second_rows, 0)

    log_table = log_table_ref[...]
    sum_table = sum_table_ref[...]
    ext_row = lax.broadcasted_iota(jnp.int32, (16, LANES), 0)
    is_high = (ext_row == 0) | (ext_row == 2) | (ext_row == 5)
    is_middle = (ext_row == 1) | (ext_row == 3)
    is_one = (ext_row >= 6) & (ext_row < 9)
    mass = mass_ref[...]
    heat = heat_ref[...]
    sub24 = lax.broadcasted_iota(jnp.int32, (SUB, LANES), 0)

    def box(index, carry):
        p = index // 4
        j = index - p * 4
        base = j * ROWS + p * BOX

        def prepare(i, inner):
            row = packed[base + i]
            beginning = row * inv_mass
            start_ref[i] = beginning
            conc_ref[i] = beginning
            inverse = 1.0 / row[SPECIES : SPECIES + 1, :]
            high = coarse(inverse)
            middle = coarse(inverse - high)
            rest = (inverse - high) - middle
            ext = jnp.where(
                is_high,
                jnp.broadcast_to(high, (16, LANES)),
                jnp.where(
                    is_middle,
                    jnp.broadcast_to(middle, (16, LANES)),
                    jnp.where(ext_row == 4, jnp.broadcast_to(rest, (16, LANES)), 0.0),
                ),
            )
            ext_ref[i] = jnp.where(is_one, 1.0, ext)
            return inner

        lax.fori_loop(0, BOX, prepare, 0, unroll=4)

        def sweep(number, inner):
            for chunk in range(BOX // BOX_CHUNK):
                at = [chunk * BOX_CHUNK + i for i in range(BOX_CHUNK)]
                conc = jnp.concatenate([conc_ref[i] for i in at], axis=1)
                ext = jnp.concatenate([ext_ref[i] for i in at], axis=1)
                logs = jnp.log(conc)
                high = coarse(logs)
                stacked = jnp.concatenate([high, logs - high, ext], axis=0).astype(bf16)
                progress = jnp.exp(jnp.dot(log_table, stacked, preferred_element_type=f32))
                high = coarse(progress)
                stacked = jnp.concatenate([high, progress - high], axis=0).astype(bf16)
                sums = jnp.dot(sum_table, stacked, preferred_element_type=f32)
                start = jnp.concatenate([start_ref[i] for i in at], axis=1)
                conc = (start + sums[:SUB, :]) * (conc / (conc + sums[SUB:, :]))
                for n, i in enumerate(at):
                    conc_ref[i] = conc[:, n * LANES : (n + 1) * LANES]
            return inner

        lax.fori_loop(0, box_cost[p, j], sweep, 0)
        flag = flame_flag[p, j].astype(f32)

        def finish(i, inner):
            row = packed[base + i]
            advanced = conc_ref[i] * mass
            source = jnp.sum(heat * (advanced - row), axis=0, keepdims=True)
            temperature = row[SPECIES : SPECIES + 1, :] + flag * source
            packed[base + i] = jnp.where(
                sub24 == SPECIES, jnp.broadcast_to(temperature, (SUB, LANES)), advanced
            )
            return inner

        lax.fori_loop(0, BOX, finish, 0, unroll=4)
        return carry

    lax.fori_loop(0, 8, box, 0)

    lane24 = lax.broadcasted_iota(jnp.int32, (SUB, LANES), 1)

    def give(x, carry):
        planes = swap_quarters([packed[j * ROWS + x] for j in range(4)], lane24)
        for z in range(PLANES):
            out[pl.ds(z * ROWS + x, FIELDS, stride=PLANES * ROWS), :] = planes[z][:FIELDS]
        return carry

    lax.fori_loop(0, ROWS, give, 0, unroll=2)


def substep(box_cost, flame_flag, *operands):
    vmem = pl.BlockSpec(memory_space=pltpu.VMEM)
    smem = pl.BlockSpec(memory_space=pltpu.SMEM)
    rows = lambda n: pltpu.VMEM((n, SUB, LANES), f32)
    return pl.pallas_call(
        substep_kernel,
        in_specs=[smem, smem] + [vmem] * len(operands),
        out_specs=[vmem, smem],
        out_shape=[
            jax.ShapeDtypeStruct((FIELDS * PLANES * ROWS, LANES), f32),
            jax.ShapeDtypeStruct((1, 1), f32),
        ],
        scratch_shapes=[
            rows(PLANES * HROWS),
            rows(PLANES * HROWS),
            rows(PLANES * HROWS),
            rows(32),
            rows(32),
            rows(32),
            rows(4),
            rows(4),
            rows(PLANES * ROWS),
            rows(BOX),
            rows(BOX),
            pltpu.VMEM((BOX, 16, LANES), f32),
        ],
        compiler_params=pltpu.CompilerParams(vmem_limit_bytes=VMEM_BYTES),
    )(box_cost, flame_flag, *operands)


def rounded(x):
    return lax.reduce_precision(x, 8, 7)


def split3(x):
    high = rounded(x)
    middle = rounded(x - high)
    return high, middle, rounded((x - high) - middle)


def tables(masses, reciprocals, rate_scale, energy, reactants, products, heat_release):
    fill = lambda x, value: jnp.broadcast_to(
        jnp.pad(x, (0, SUB - SPECIES), constant_values=value)[:, None], (SUB, LANES)
    )
    inv_mass = fill(1.0 / masses, 1.0)
    mass = fill(masses, 1.0)
    live = fill(jnp.ones_like(masses), 0.0)
    heat = fill(heat_release, 0.0)
    cross = (reciprocals * (1.0 - jnp.eye(SPECIES, dtype=f32))).T
    full = jnp.concatenate([cross, jnp.ones((SUB + 8 - SPECIES, SPECIES), f32)], axis=0)
    full = jnp.pad(full, ((0, 0), (0, SUB - SPECIES)))
    high = rounded(full)
    table = jnp.concatenate(
        [high, high, full - high, jnp.zeros((SUB + 8, 8), f32)], axis=1
    ).astype(bf16)
    react = jnp.pad(reactants.astype(f32), ((0, RPAD - REACTIONS), (0, SUB - SPECIES)))
    make = jnp.pad(products.astype(f32), ((0, RPAD - REACTIONS), (0, SUB - SPECIES)))
    eh, em, el = split3(-energy)
    ah, am, al = split3(jnp.log(rate_scale))
    ext = jnp.stack([eh, eh, em, em, eh, el, ah, am, al], axis=1)
    ext = jnp.pad(ext, ((0, RPAD - REACTIONS), (0, 7)))
    log_table = jnp.concatenate([react, react, ext], axis=1).astype(bf16)
    sums = HALF * jnp.concatenate([make.T, react.T], axis=0)
    sum_table = jnp.concatenate([sums, sums], axis=1).astype(bf16)
    return inv_mass, mass, live, heat, table, log_table, sum_table


def shifted(x, axis, by):
    count = lax.axis_size(axis)
    return lax.ppermute(x, axis, [(i, (i + by) % count) for i in range(count)])


def per_device(
    state,
    masses,
    reciprocals,
    rate_scale,
    energy,
    reactants,
    products,
    heat_release,
    box_cost,
    box_owner,
    flame_flag,
):
    inv_mass, mass, live, heat, table, log_table, sum_table = tables(
        masses, reciprocals, rate_scale, energy, reactants, products, heat_release
    )
    flat = state.reshape(FIELDS * PLANES * ROWS, LANES)
    low, high = edge_rows(state)
    below = shifted(high, "gx", 1)
    above = shifted(low, "gx", -1)
    peak = local_peak(state, inv_mass, live, table)
    own, to_left, to_right = strips(flat, below, above)
    left = shifted(to_right, "gy", 1)
    right = shifted(to_left, "gy", -1)

    nx, ny = lax.axis_size("gx"), lax.axis_size("gy")
    cost = box_cost.reshape(-1).astype(f32)
    target = jnp.arange(nx * ny, dtype=jnp.int32)
    same = (target // ny == lax.axis_index("gx")).astype(f32)
    charged = (box_owner.reshape(1, -1) == (target % ny)[:, None]).astype(f32)
    charged = jnp.sum(charged * cost[None, :], axis=1) * same
    column = jnp.arange(LANES, dtype=jnp.int32)[None, :]
    message = jnp.where(
        column == 0,
        2.0 * jnp.max(peak),
        jnp.where(
            column == 1,
            charged[:, None],
            jnp.where(column == 2, (same * jnp.sum(cost))[:, None], 0.0),
        ),
    )
    gathered = lax.all_to_all(message, ("gx", "gy"), 0, 0, tiled=True)

    new_state, load = substep(
        box_cost,
        flame_flag,
        flat,
        below,
        above,
        left,
        right,
        own,
        gathered,
        inv_mass,
        mass,
        live,
        heat,
        table,
        log_table,
        sum_table,
    )
    return new_state.reshape(state.shape), load


def solution(mesh):
    split = P("gx", "gy")
    whole = P(None, None, "gx", "gy")
    return jax.shard_map(
        per_device,
        mesh=mesh,
        in_specs=(whole, P(), P(), P(), P(), P(), P(), P(), split, split, split),
        out_specs=(whole, split),
        check_vma=False,
    )
```

```python
import functools

import jax
import jax.numpy as jnp
from jax import lax
from jax.experimental import pallas as pl
from jax.experimental.pallas import tpu as pltpu
from jax.sharding import PartitionSpec as P

SPECIES = 21
FIELDS = 22
SUB = 24
LANES = 128
PLANES = 4
ROWS = 64
HROWS = ROWS + 4
BOX = 32
REACTIONS = 84
RPAD = 88
CHUNK = 4
BOX_CHUNK = 4
GROUP = 2
LOG2E = 1.4426950408889634
Z_WEIGHT = 0.25
CFL_SAFE = 0.5
HALF = 0.5
VMEM_BYTES = 56 * 1024 * 1024

f32 = jnp.float32
bf16 = jnp.bfloat16


def live_rows():
    return (lax.broadcasted_iota(jnp.int32, (SUB, LANES), 0) < SPECIES).astype(f32)


def fill_spare(rows, count):
    def body(i, carry):
        rows[i, FIELDS:SUB, :] = jnp.ones((SUB - FIELDS, LANES), f32)
        return carry

    lax.fori_loop(0, count, body, 0, unroll=8)


def coarse(x):
    return x.astype(bf16).astype(f32)


def diffusivity(rows, inv_mass, table, live):
    amounts = jnp.concatenate([row * inv_mass for row in rows], axis=1)
    high = coarse(amounts)
    low = amounts - high
    blank = jnp.zeros((8, amounts.shape[1]), f32)
    stacked = jnp.concatenate([high, low, high, blank], axis=0).astype(bf16)
    sums = jnp.dot(table, stacked, preferred_element_type=f32)
    result = []
    for i, row in enumerate(rows):
        lanes = slice(i * LANES, (i + 1) * LANES)
        heat = row[SPECIES : SPECIES + 1, :]
        scale = (HALF * heat * jnp.sqrt(heat)) * sums[SUB : SUB + 8, lanes]
        scale = jnp.concatenate([scale] * 3, axis=0)
        result.append(live * (1.0 - row) * scale / sums[:SUB, lanes])
    return result


def peak_kernel(box_cost, box_owner, state, inv_mass_ref, table_ref, message, coef_out, field, coef, in_sem, out_sem):
    inv_mass = inv_mass_ref[...]
    live = live_rows()
    table = table_ref[...]

    def fetch(z, k):
        return pltpu.make_async_copy(
            state.at[k, pl.ds(z * ROWS, ROWS)], field.at[pl.ds(z * ROWS, ROWS), k], in_sem.at[z]
        )

    def keep(z):
        rows = pl.ds(z * ROWS, ROWS)
        return pltpu.make_async_copy(coef.at[rows], coef_out.at[rows], out_sem.at[z])

    for z in range(PLANES):
        for k in range(FIELDS):
            fetch(z, k).start()
    fill_spare(field, PLANES * ROWS)
    best = jnp.zeros((SUB, LANES), f32)
    for z in range(PLANES):
        for k in range(FIELDS):
            fetch(z, k).wait()

        def body(index, best):
            at = [z * ROWS + index * CHUNK + i for i in range(CHUNK)]
            rows = [field[i] for i in at]
            for i, value in zip(at, diffusivity(rows, inv_mass, table, live)):
                coef[i] = value
                best = jnp.maximum(best, value)
            return best

        best = lax.fori_loop(0, ROWS // CHUNK, body, best, unroll=4)
        keep(z).start()
    top = 2.0 * jnp.max(best)
    device = lax.broadcasted_iota(jnp.int32, (LANES, LANES), 0)
    column = lax.broadcasted_iota(jnp.int32, (LANES, LANES), 1)
    count = lax.axis_size("gy")
    same = device // count == lax.axis_index("gx")
    place = device % count
    charged = jnp.zeros((LANES, LANES), f32)
    total = 0.0
    for p in range(2):
        for j in range(4):
            cost = box_cost[p, j].astype(f32)
            total = total + cost
            charged = charged + jnp.where(place == box_owner[p, j], cost, 0.0)
    tally = jnp.where(column == 1, charged, jnp.where(column == 2, total, 0.0))
    message[...] = jnp.where(column == 0, top, jnp.where(same, tally, 0.0))
    for z in range(PLANES):
        keep(z).wait()


def local_peak(box_cost, box_owner, state, inv_mass, table):
    vmem = pl.BlockSpec(memory_space=pltpu.VMEM)
    smem = pl.BlockSpec(memory_space=pltpu.SMEM)
    hbm = pl.BlockSpec(memory_space=pl.ANY)
    held = jax.ShapeDtypeStruct((PLANES * ROWS, SUB, LANES), f32)
    devices = lax.axis_size("gx") * lax.axis_size("gy")
    assert devices == LANES or devices == 1
    return pl.pallas_call(
        peak_kernel,
        in_specs=[smem, smem, hbm, vmem, vmem],
        out_specs=[vmem, hbm],
        out_shape=[jax.ShapeDtypeStruct((LANES, LANES), f32), held],
        scratch_shapes=[
            pltpu.VMEM(held.shape, f32),
            pltpu.VMEM(held.shape, f32),
            pltpu.SemaphoreType.DMA((PLANES,)),
            pltpu.SemaphoreType.DMA((PLANES,)),
        ],
        compiler_params=pltpu.CompilerParams(vmem_limit_bytes=VMEM_BYTES),
    )(box_cost, box_owner, state, inv_mass, table)


def edge_rows_kernel(first, last, low, high):
    for k in range(FIELDS):
        for z in range(PLANES):
            at = (k * PLANES + z) * 2
            low[at : at + 2, :] = first[k, z, 0:2, :]
            high[at : at + 2, :] = last[k, z, 6:8, :]


def edge_rows(state):
    shape = jax.ShapeDtypeStruct((FIELDS * PLANES * 2, LANES), f32)
    return pl.pallas_call(
        edge_rows_kernel,
        grid=(1,),
        in_specs=[
            pl.BlockSpec((FIELDS, PLANES, 8, LANES), lambda i: (0, 0, 0, 0)),
            pl.BlockSpec((FIELDS, PLANES, 8, LANES), lambda i: (0, 0, ROWS // 8 - 1, 0)),
        ],
        out_specs=[pl.BlockSpec(shape.shape, lambda i: (0, 0))] * 2,
        out_shape=[shape, shape],
        compiler_params=pltpu.CompilerParams(vmem_limit_bytes=VMEM_BYTES),
    )(state, state)


def strips_kernel(state, below, above, own, to_left, to_right):
    lane = lax.broadcasted_iota(jnp.int32, (8, LANES), 1)
    sub = lax.broadcasted_iota(jnp.int32, (8, LANES), 0)
    pairs = FIELDS * PLANES
    for group in range(3):
        count = min(32, pairs - group * 32)

        def body(index, held):
            pair = group * 32 + index
            blocks = [state[pl.ds(pl.multiple_of(pair * ROWS + i * 8, 8), 8), :] for i in range(8)]
            after = jnp.broadcast_to(above[pl.ds(pair * 2, 1), :], (8, LANES))
            before = jnp.broadcast_to(below[pl.ds(pair * 2 + 1, 1), :], (8, LANES))
            blocks.append(jnp.where(sub == 0, after, before))
            mine = (lane >> 2) == index
            return tuple(
                jnp.where(mine, pltpu.roll(block, 4 * index + 2, 1), old)
                for block, old in zip(blocks, held)
            )

        held = lax.fori_loop(0, count, body, (jnp.ones((8, LANES), f32),) * 9, unroll=4)
        block = jnp.concatenate(list(held[:8]) + [held[8]] * 8, axis=0)
        turned = block.T
        own[group * 128 : group * 128 + 4 * count, :] = turned[: 4 * count, :]
    for c in range(2):
        to_right[pl.ds(c, pairs, stride=2), :] = own[pl.ds(c, pairs, stride=4), :]
        to_left[pl.ds(c, pairs, stride=2), :] = own[pl.ds(2 + c, pairs, stride=4), :]


def strips(flat_state, below, above):
    pairs = FIELDS * PLANES
    return pl.pallas_call(
        strips_kernel,
        out_shape=[
            jax.ShapeDtypeStruct((pairs * 4, LANES), f32),
            jax.ShapeDtypeStruct((pairs * 2, LANES), f32),
            jax.ShapeDtypeStruct((pairs * 2, LANES), f32),
        ],
        compiler_params=pltpu.CompilerParams(vmem_limit_bytes=VMEM_BYTES),
    )(flat_state, below, above)


def swap_quarters(planes, lane):
    low_half = lane < 64
    even = ((lane >> 5) & 1) == 0
    a, b, c, d = planes
    a, c = (
        jnp.where(low_half, a, pltpu.roll(c, 64, 1)),
        jnp.where(low_half, pltpu.roll(a, 64, 1), c),
    )
    b, d = (
        jnp.where(low_half, b, pltpu.roll(d, 64, 1)),
        jnp.where(low_half, pltpu.roll(b, 64, 1), d),
    )
    a, b = (
        jnp.where(even, a, pltpu.roll(b, 32, 1)),
        jnp.where(even, pltpu.roll(a, 96, 1), b),
    )
    c, d = (
        jnp.where(even, c, pltpu.roll(d, 32, 1)),
        jnp.where(even, pltpu.roll(c, 96, 1), d),
    )
    return [a, b, c, d]


def substep_kernel(
    box_cost,
    flame_flag,
    state,
    coef_in,
    below,
    above,
    left,
    right,
    own,
    gathered,
    inv_mass_ref,
    mass_ref,
    heat_ref,
    table_ref,
    log_table_ref,
    sum_table_ref,
    out,
    load_out,
    field,
    coef,
    first,
    strip_field,
    strip_coef,
    strip_first,
    flux_left,
    flux_right,
    flux_both,
    packed,
    start_ref,
    conc_ref,
    ext_ref,
    out_rows,
    in_sem,
    out_sem,
):
    def fetch(z):
        rows = pl.ds(z * HROWS + 2, ROWS)
        copies = [
            pltpu.make_async_copy(
                state.at[k, pl.ds(z * ROWS, ROWS)], field.at[rows, k], in_sem.at[z]
            )
            for k in range(FIELDS)
        ]
        copies.append(
            pltpu.make_async_copy(
                coef_in.at[pl.ds(z * ROWS, ROWS)], coef.at[rows], in_sem.at[z]
            )
        )
        return copies

    for z in range(PLANES):
        for copy in fetch(z):
            copy.start()
    fill_spare(field, PLANES * HROWS)
    inv_mass = inv_mass_ref[...]
    live = live_rows()
    table = table_ref[...]
    lane = lax.broadcasted_iota(jnp.int32, (8, LANES), 1)
    ones2 = jnp.ones((SUB - FIELDS, LANES), f32)

    received = gathered[...]
    columns = lax.broadcasted_iota(jnp.int32, received.shape, 1)
    peak = jnp.max(jnp.where(columns == 0, received, 0.0), keepdims=True)
    step = CFL_SAFE / ((4.0 + 2.0 * Z_WEIGHT) * peak)
    mine = jnp.sum(jnp.where(columns == 1, received, 0.0))
    everyone = jnp.sum(jnp.where(columns == 2, received, 0.0))
    load_out[0, 0] = mine / (everyone / 16.0)
    step = jnp.broadcast_to(step, (8, LANES))

    def row24(value):
        return jnp.concatenate([value, ones2], axis=0)

    for z in range(PLANES):
        for layer in range(2):
            field[z * HROWS + layer] = row24(below[pl.ds(z * 2 + layer, FIELDS, stride=8), :])
            field[z * HROWS + ROWS + 2 + layer] = row24(
                above[pl.ds(z * 2 + layer, FIELDS, stride=8), :]
            )

        for c in range(2):
            strip_field[z * 8 + c] = row24(left[pl.ds(z * 2 + c, FIELDS, stride=8), :])
            strip_field[z * 8 + 2 + c] = row24(own[pl.ds(z * 4 + 2 + c, FIELDS, stride=16), :])
            strip_field[z * 8 + 4 + c] = row24(own[pl.ds(z * 4 + c, FIELDS, stride=16), :])
            strip_field[z * 8 + 6 + c] = row24(right[pl.ds(z * 2 + c, FIELDS, stride=8), :])

    def coefficients(source, target, base, count):
        def body(index, carry):
            at = [base + index * CHUNK + i for i in range(CHUNK)]
            rows = [source[i] for i in at]
            for i, value in zip(at, diffusivity(rows, inv_mass, table, live)):
                target[i] = value
            return carry

        lax.fori_loop(0, count // CHUNK, body, 0, unroll=4)

    def face(source, weight, here, there, part):
        return (weight[here, part, :] + weight[there, part, :]) * (
            source[there, part, :] - source[here, part, :]
        )

    parts = [slice(0, 8), slice(8, 16), slice(16, 24)]

    def side_fluxes(source, weight):
        for z in range(PLANES):
            for part in parts:
                flux_left[z, part, :] = face(source, weight, z * 8 + 1, z * 8 + 2, part)
                flux_right[z, part, :] = face(source, weight, z * 8 + 5, z * 8 + 6, part)
                flux_both[z, part, :] = jnp.where(
                    lane < ROWS, flux_left[z, part, :], pltpu.roll(flux_right[z, part, :], ROWS, 1)
                )

    def strip_update():
        for r in (1, 2, 5, 6):
            for part in parts:
                above_flux = None
                for z in range(PLANES):
                    at = z * 8 + r
                    here = strip_field[at, part, :]
                    weight = strip_coef[at, part, :]
                    total = face(strip_field, strip_coef, at, at + 1, part)
                    total = total - face(strip_field, strip_coef, at - 1, at, part)
                    onward = (weight + pltpu.roll(weight, LANES - 1, 1)) * (
                        pltpu.roll(here, LANES - 1, 1) - here
                    )
                    total = total + (onward - pltpu.roll(onward, 1, 1))
                    if above_flux is not None:
                        total = total - Z_WEIGHT * above_flux
                    if z < PLANES - 1:
                        above_flux = face(strip_field, strip_coef, at, at + 8, part)
                        total = total + Z_WEIGHT * above_flux
                    strip_first[at, part, :] = here + step * total

    def updated(source, weight, x0, count, part, ends):
        result = [[] for _ in range(count)]
        above_flux = [None] * count
        for z in range(PLANES):
            base = z * HROWS + x0 + 1
            here = [source[base + i, part, :] for i in range(count + 2)]
            coefs = [weight[base + i, part, :] for i in range(count + 2)]
            along = [
                (coefs[i] + coefs[i + 1]) * (here[i + 1] - here[i]) for i in range(count + 1)
            ]
            for i in range(count):
                c, d = here[i + 1], coefs[i + 1]
                onward = (d + pltpu.roll(d, LANES - 1, 1)) * (pltpu.roll(c, LANES - 1, 1) - c)
                entering, leaving = ends(z, x0 + i, part)
                onward = jnp.where(lane == LANES - 1, leaving, onward)
                back = jnp.where(lane == 0, entering, pltpu.roll(onward, 1, 1))
                total = (along[i + 1] - along[i]) + (onward - back)
                if z < PLANES - 1:
                    over = base + i + 1 + HROWS
                    flux = Z_WEIGHT * (
                        (d + weight[over, part, :]) * (source[over, part, :] - c)
                    )
                    total = total + flux
                if z > 0:
                    total = total - above_flux[i]
                if z < PLANES - 1:
                    above_flux[i] = flux
                result[i].append(c + step * total)
        return result

    def outer_ends(z, x, part):
        shift = -x % LANES
        entering = pltpu.roll(flux_left[z, part, :], shift, 1)
        leaving = pltpu.roll(flux_right[z, part, :], (shift + LANES - 1) % LANES, 1)
        return entering, leaving

    def inner_ends(z, x, part):
        index = jnp.where(lane == 0, x, x + ROWS)
        both = jnp.take_along_axis(flux_both[z, part, :], index, axis=1, mode="promise_in_bounds")
        return both, both

    coefficients(strip_field, strip_coef, 0, PLANES * 8)
    side_fluxes(strip_field, strip_coef)
    strip_update()
    for z in range(PLANES):
        for copy in fetch(z):
            copy.wait()
    halo = [z * HROWS + x for z in range(PLANES) for x in (0, 1, ROWS + 2, ROWS + 3)]
    for n in range(0, len(halo), CHUNK):
        at = halo[n : n + CHUNK]
        for i, value in zip(at, diffusivity([field[i] for i in at], inv_mass, table, live)):
            coef[i] = value

    for x in (-1, ROWS):
        for part in parts:
            for z, value in enumerate(updated(field, coef, x, 1, part, outer_ends)[0]):
                first[z * HROWS + x + 2, part, :] = value

    def first_rows(index, carry):
        x = index * GROUP
        for part in parts:
            for i, planes in enumerate(updated(field, coef, x, GROUP, part, inner_ends)):
                for z, value in enumerate(planes):
                    first[z * HROWS + x + i + 2, part, :] = value
        return carry

    lax.fori_loop(0, ROWS // GROUP, first_rows, 0)
    for z in range(PLANES):
        first[z * HROWS] = field[z * HROWS]
        first[z * HROWS + HROWS - 1] = field[z * HROWS + HROWS - 1]
        for r in (0, 3, 4, 7):
            strip_first[z * 8 + r] = strip_field[z * 8 + r]
    coefficients(strip_first, strip_coef, 0, PLANES * 8)
    side_fluxes(strip_first, strip_coef)
    coefficients(first, coef, 0, PLANES * HROWS)

    def second_rows(index, carry):
        x = index * GROUP
        for part in parts:
            for i, planes in enumerate(updated(first, coef, x, GROUP, part, inner_ends)):
                planes = swap_quarters(planes, lane)
                for j in range(4):
                    packed[j * ROWS + x + i, part, :] = planes[j]
        return carry

    lax.fori_loop(0, ROWS // GROUP, second_rows, 0)

    log_table = log_table_ref[...]
    sum_table = sum_table_ref[...]
    ext_row = lax.broadcasted_iota(jnp.int32, (16, LANES), 0)
    is_high = (ext_row == 0) | (ext_row == 2) | (ext_row == 5)
    is_middle = (ext_row == 1) | (ext_row == 3)
    is_one = (ext_row >= 6) & (ext_row < 9)
    mass = mass_ref[...]
    heat = heat_ref[...]
    sub24 = lax.broadcasted_iota(jnp.int32, (SUB, LANES), 0)

    def box(p, j, carry):
        base = j * ROWS + p * BOX

        def prepare(i, inner):
            row = packed[base + i]
            beginning = row * inv_mass
            start_ref[i] = beginning
            conc_ref[i] = beginning
            inverse = 1.0 / row[SPECIES : SPECIES + 1, :]
            high = coarse(inverse)
            middle = coarse(inverse - high)
            rest = (inverse - high) - middle
            ext = jnp.where(
                is_high,
                jnp.broadcast_to(high, (16, LANES)),
                jnp.where(
                    is_middle,
                    jnp.broadcast_to(middle, (16, LANES)),
                    jnp.where(ext_row == 4, jnp.broadcast_to(rest, (16, LANES)), 0.0),
                ),
            )
            ext_ref[i] = jnp.where(is_one, 1.0, ext)
            return inner

        lax.fori_loop(0, BOX, prepare, 0, unroll=8)

        chunks = BOX // BOX_CHUNK

        def rates(chunk):
            at = [chunk * BOX_CHUNK + i for i in range(BOX_CHUNK)]
            conc = jnp.concatenate([conc_ref[i] for i in at], axis=1)
            ext = jnp.concatenate([ext_ref[i] for i in at], axis=1)
            logs = jnp.log2(conc)
            high = coarse(logs)
            stacked = jnp.concatenate([high, logs - high, ext], axis=0).astype(bf16)
            return jnp.dot(log_table, stacked, preferred_element_type=f32)

        def advance(chunk, exponent):
            at = [chunk * BOX_CHUNK + i for i in range(BOX_CHUNK)]
            progress = jnp.exp2(exponent)
            high = coarse(progress)
            stacked = jnp.concatenate([high, progress - high], axis=0).astype(bf16)
            sums = jnp.dot(sum_table, stacked, preferred_element_type=f32)
            conc = jnp.concatenate([conc_ref[i] for i in at], axis=1)
            start = jnp.concatenate([start_ref[i] for i in at], axis=1)
            conc = (start + sums[:SUB, :]) * (conc / (conc + sums[SUB:, :]))
            for n, i in enumerate(at):
                conc_ref[i] = conc[:, n * LANES : (n + 1) * LANES]

        def sweep(number, inner):
            ahead = rates(0)
            for chunk in range(chunks):
                exponent = ahead
                if chunk + 1 < chunks:
                    ahead = rates(chunk + 1)
                advance(chunk, exponent)
            return inner

        lax.fori_loop(0, box_cost[p, j], sweep, 0)
        flag = flame_flag[p, j].astype(f32)

        def finish(i, inner):
            row = packed[base + i]
            advanced = conc_ref[i] * mass
            source = jnp.sum(heat * (advanced - row), axis=0, keepdims=True)
            temperature = row[SPECIES : SPECIES + 1, :] + flag * source
            packed[base + i] = jnp.where(
                sub24 == SPECIES, jnp.broadcast_to(temperature, (SUB, LANES)), advanced
            )
            return inner

        lax.fori_loop(0, BOX, finish, 0, unroll=8)
        return carry

    def give(x, carry):
        for part in parts:
            planes = swap_quarters([packed[j * ROWS + x, part, :] for j in range(4)], lane)
            for z in range(PLANES):
                out_rows[z * ROWS + x, part, :] = planes[z]
        return carry

    def deliver(p):
        return [
            pltpu.make_async_copy(
                out_rows.at[pl.ds(z * ROWS + p * BOX, BOX), k],
                out.at[k, pl.ds(z * ROWS + p * BOX, BOX)],
                out_sem.at[p],
            )
            for z in range(PLANES)
            for k in range(FIELDS)
        ]

    for p in range(2):
        lax.fori_loop(0, 4, functools.partial(box, p), 0)
        lax.fori_loop(p * BOX, (p + 1) * BOX, give, 0, unroll=4)
        for copy in deliver(p):
            copy.start()
    for p in range(2):
        for copy in deliver(p):
            copy.wait()


def substep(box_cost, flame_flag, *operands):
    vmem = pl.BlockSpec(memory_space=pltpu.VMEM)
    smem = pl.BlockSpec(memory_space=pltpu.SMEM)
    hbm = pl.BlockSpec(memory_space=pl.ANY)
    rows = lambda n: pltpu.VMEM((n, SUB, LANES), f32)
    return pl.pallas_call(
        substep_kernel,
        in_specs=[smem, smem, hbm, hbm] + [vmem] * (len(operands) - 2),
        out_specs=[hbm, smem],
        out_shape=[
            jax.ShapeDtypeStruct((FIELDS, PLANES * ROWS, LANES), f32),
            jax.ShapeDtypeStruct((1, 1), f32),
        ],
        scratch_shapes=[
            rows(PLANES * HROWS),
            rows(PLANES * HROWS),
            rows(PLANES * HROWS),
            rows(32),
            rows(32),
            rows(32),
            rows(4),
            rows(4),
            rows(4),
            rows(PLANES * ROWS),
            rows(BOX),
            rows(BOX),
            pltpu.VMEM((BOX, 16, LANES), f32),
            rows(PLANES * ROWS),
            pltpu.SemaphoreType.DMA((PLANES,)),
            pltpu.SemaphoreType.DMA((2,)),
        ],
        compiler_params=pltpu.CompilerParams(vmem_limit_bytes=VMEM_BYTES),
    )(box_cost, flame_flag, *operands)


def rounded(x):
    return lax.reduce_precision(x, 8, 7)


def split3(x):
    high = rounded(x)
    middle = rounded(x - high)
    return high, middle, rounded((x - high) - middle)


def tables(masses, reciprocals, rate_scale, energy, reactants, products, heat_release):
    fill = lambda x, value: jnp.broadcast_to(
        jnp.pad(x, (0, SUB - SPECIES), constant_values=value)[:, None], (SUB, LANES)
    )
    inv_mass = fill(1.0 / masses, 1.0)
    mass = fill(masses, 1.0)
    heat = fill(heat_release, 0.0)
    cross = (reciprocals * (1.0 - jnp.eye(SPECIES, dtype=f32))).T
    full = jnp.concatenate([cross, jnp.ones((SUB + 8 - SPECIES, SPECIES), f32)], axis=0)
    full = jnp.pad(full, ((0, 0), (0, SUB - SPECIES)))
    high = rounded(full)
    table = jnp.concatenate(
        [high, high, full - high, jnp.zeros((SUB + 8, 8), f32)], axis=1
    ).astype(bf16)
    react = jnp.pad(reactants.astype(f32), ((0, RPAD - REACTIONS), (0, SUB - SPECIES)))
    make = jnp.pad(products.astype(f32), ((0, RPAD - REACTIONS), (0, SUB - SPECIES)))
    eh, em, el = split3(-LOG2E * energy)
    ah, am, al = split3(jnp.log2(rate_scale))
    ext = jnp.stack([eh, eh, em, em, eh, el, ah, am, al], axis=1)
    ext = jnp.pad(ext, ((0, RPAD - REACTIONS), (0, 7)))
    log_table = jnp.concatenate([react, react, ext], axis=1).astype(bf16)
    sums = HALF * jnp.concatenate([make.T, react.T], axis=0)
    sum_table = jnp.concatenate([sums, sums], axis=1).astype(bf16)
    return inv_mass, mass, heat, table, log_table, sum_table


def shifted(x, axis, by):
    count = lax.axis_size(axis)
    return lax.ppermute(x, axis, [(i, (i + by) % count) for i in range(count)])


def per_device(
    state,
    masses,
    reciprocals,
    rate_scale,
    energy,
    reactants,
    products,
    heat_release,
    box_cost,
    box_owner,
    flame_flag,
):
    inv_mass, mass, heat, table, log_table, sum_table = tables(
        masses, reciprocals, rate_scale, energy, reactants, products, heat_release
    )
    flat = state.reshape(FIELDS * PLANES * ROWS, LANES)
    low, high = edge_rows(state)
    below = shifted(high, "gx", 1)
    above = shifted(low, "gx", -1)
    message, coef = local_peak(
        box_cost, box_owner, state.reshape(FIELDS, PLANES * ROWS, LANES), inv_mass, table
    )
    own, to_left, to_right = strips(flat, below, above)
    left = shifted(to_right, "gy", 1)
    right = shifted(to_left, "gy", -1)

    gathered = lax.all_to_all(message, ("gx", "gy"), 0, 0, tiled=True)

    new_state, load = substep(
        box_cost,
        flame_flag,
        state.reshape(FIELDS, PLANES * ROWS, LANES),
        coef,
        below,
        above,
        left,
        right,
        own,
        gathered,
        inv_mass,
        mass,
        heat,
        table,
        log_table,
        sum_table,
    )
    return new_state.reshape(state.shape), load


def solution(mesh):
    split = P("gx", "gy")
    whole = P(None, None, "gx", "gy")
    return jax.shard_map(
        per_device,
        mesh=mesh,
        in_specs=(whole, P(), P(), P(), P(), P(), P(), P(), split, split, split),
        out_specs=(whole, split),
        check_vma=False,
    )
```

```python
import functools

import jax
import jax.numpy as jnp
from jax import lax
from jax.experimental import pallas as pl
from jax.experimental.pallas import tpu as pltpu
from jax.sharding import PartitionSpec as P

SPECIES = 21
FIELDS = 22
SUB = 24
LANES = 128
PLANES = 4
ROWS = 64
HROWS = ROWS + 4
BOX = 32
REACTIONS = 84
RPAD = 88
CHUNK = 4
BOX_CHUNK = 4
GROUP = 2
LOG2E = 1.4426950408889634
Z_WEIGHT = 0.25
CFL_SAFE = 0.5
HALF = 0.5
VMEM_BYTES = 56 * 1024 * 1024

PARTS = [slice(0, 8), slice(8, 16), slice(16, 24)]

f32 = jnp.float32
bf16 = jnp.bfloat16


def live_rows():
    return (lax.broadcasted_iota(jnp.int32, (SUB, LANES), 0) < SPECIES).astype(f32)


def fill_spare(rows, count):
    def body(i, carry):
        rows[i, FIELDS:SUB, :] = jnp.ones((SUB - FIELDS, LANES), f32)
        return carry

    lax.fori_loop(0, count, body, 0, unroll=8)


def coarse(x):
    return x.astype(bf16).astype(f32)


def diffusivity(rows, inv_mass, table, live):
    amounts = jnp.concatenate([row * inv_mass for row in rows], axis=1)
    high = coarse(amounts)
    low = amounts - high
    blank = jnp.zeros((8, amounts.shape[1]), f32)
    stacked = jnp.concatenate([high, low, high, blank], axis=0).astype(bf16)
    sums = jnp.dot(table, stacked, preferred_element_type=f32)
    result = []
    for i, row in enumerate(rows):
        lanes = slice(i * LANES, (i + 1) * LANES)
        heat = row[SPECIES : SPECIES + 1, :]
        scale = (HALF * heat * jnp.sqrt(heat)) * sums[SUB : SUB + 8, lanes]
        scale = jnp.concatenate([scale] * 3, axis=0)
        result.append(live * (1.0 - row) * scale / sums[:SUB, lanes])
    return result


def split3(x):
    high = coarse(x)
    middle = coarse(x - high)
    return high, middle, coarse((x - high) - middle)


def fill_tables(
    masses,
    reciprocals,
    rate_scale,
    energy,
    reactants,
    products,
    heat_release,
    scales,
    table,
    log_table,
    sum_table,
    square,
):
    lane = lax.broadcasted_iota(jnp.int32, (LANES, LANES), 1)
    row = lax.broadcasted_iota(jnp.int32, (LANES, LANES), 0)

    def padded(value, filler=0.0):
        square[...] = jnp.full((LANES, LANES), filler, f32)
        square[: value.shape[0], : value.shape[1]] = value
        return square[...]

    def column(ref, filler):
        return jnp.broadcast_to(padded(ref[...], filler)[:1], (LANES, LANES)).T

    mass = column(masses, 1.0)[:SUB]
    scales[0] = 1.0 / mass
    scales[1] = mass
    scales[2] = column(heat_release, 0.0)[:SUB]

    cross = padded(reciprocals[...])
    cross = jnp.where(row == lane, 0.0, cross).T
    cross = jnp.where(lane < SPECIES, jnp.where(row < SPECIES, cross, 1.0), 0.0)[: SUB + 8]
    high = coarse(cross)
    table[...] = high + pltpu.roll(high, SUB, 1) + pltpu.roll(cross - high, 2 * SUB, 1)

    react_back = padded(reactants[...].astype(f32))
    react = react_back.T
    eh, em, el = split3((-LOG2E) * column(energy, 0.0)[:RPAD])
    ah, am, al = split3(jnp.log2(column(rate_scale, 1.0)[:RPAD]))
    place = lane[:RPAD]
    ext = jnp.zeros((RPAD, LANES), f32)
    for n, value in enumerate((eh, eh, em, em, eh, el, ah, am, al)):
        ext = jnp.where(place == 2 * SUB + n, value, ext)
    log_table[...] = react[:RPAD] + pltpu.roll(react[:RPAD], SUB, 1) + ext

    make = padded(products[...].astype(f32))[:SUB]
    sums = HALF * jnp.concatenate([make, react_back[:SUB]], axis=0)
    moved = pltpu.roll(sums, RPAD, 1)
    place = lane[: 2 * SUB]
    sum_table[:, :LANES] = jnp.where(place < RPAD, sums, moved)
    sum_table[:, LANES:] = jnp.where(place < 2 * RPAD - LANES, moved, 0.0)


def peak_kernel(
    box_cost,
    box_owner,
    state,
    masses,
    reciprocals,
    rate_scale,
    energy,
    reactants,
    products,
    heat_release,
    message,
    field_out,
    coef_out,
    low,
    high,
    own,
    scales,
    table_out,
    log_table,
    sum_table,
    field,
    coef,
    square,
    in_sem,
    out_sem,
):
    def fetch(half, k):
        rows = pl.ds(half * 2 * ROWS, 2 * ROWS)
        return pltpu.make_async_copy(state.at[k, rows], field.at[rows, k], in_sem.at[half])

    def fetched(half):
        rows = pl.ds(half * 2 * ROWS, 2 * ROWS)
        whole = state.at[:, rows]
        return pltpu.make_async_copy(whole, whole, in_sem.at[half])

    def keep(held, target, half, n):
        rows = pl.ds(half * 2 * ROWS, 2 * ROWS)
        return pltpu.make_async_copy(held.at[rows], target.at[rows], out_sem.at[half, n])

    for half in range(2):
        for k in range(FIELDS):
            fetch(half, k).start()
    fill_spare(field, PLANES * ROWS)
    fill_tables(
        masses,
        reciprocals,
        rate_scale,
        energy,
        reactants,
        products,
        heat_release,
        scales,
        table_out,
        log_table,
        sum_table,
        square,
    )
    inv_mass = scales[0]
    live = live_rows()
    table = table_out[:, : 3 * SUB + 8].astype(bf16)
    best = jnp.zeros((SUB, LANES), f32)
    for half in range(2):
        fetched(half).wait()
        keep(field, field_out, half, 0).start()

        def body(index, best):
            at = [half * 2 * ROWS + index * CHUNK + i for i in range(CHUNK)]
            rows = [field[i] for i in at]
            for i, value in zip(at, diffusivity(rows, inv_mass, table, live)):
                coef[i] = value
                best = jnp.maximum(best, value)
            return best

        best = lax.fori_loop(0, 2 * ROWS // CHUNK, body, best, unroll=4)
        keep(coef, coef_out, half, 1).start()
    top = 2.0 * jnp.max(best)
    device = lax.broadcasted_iota(jnp.int32, (LANES, LANES), 0)
    column = lax.broadcasted_iota(jnp.int32, (LANES, LANES), 1)
    count = lax.axis_size("gy")
    same = device // count == lax.axis_index("gx")
    place = device % count
    charged = jnp.zeros((LANES, LANES), f32)
    total = 0.0
    for p in range(2):
        for j in range(4):
            cost = box_cost[p, j].astype(f32)
            total = total + cost
            charged = charged + jnp.where(place == box_owner[p, j], cost, 0.0)
    tally = jnp.where(column == 1, charged, jnp.where(column == 2, total, 0.0))
    message[...] = jnp.where(column == 0, top, jnp.where(same, tally, 0.0))

    for z in range(PLANES):
        for layer in range(2):
            low[z * 2 + layer] = field[z * ROWS + layer]
            high[z * 2 + layer] = field[z * ROWS + ROWS - 2 + layer]
    lane = lax.broadcasted_iota(jnp.int32, (8, LANES), 1)

    def gather(index, held):
        mine = (lane >> 2) == index
        result = []
        for z in range(PLANES):
            for group in range(2):
                for n, part in enumerate(PARTS):
                    row = field[z * ROWS + group * 32 + index, part, :]
                    turned = pltpu.roll(row, 4 * index + 2, 1)
                    result.append(jnp.where(mine, turned, held[(z * 2 + group) * 3 + n]))
        return tuple(result)

    held = lax.fori_loop(0, 32, gather, (jnp.ones((8, LANES), f32),) * 24)
    for z in range(PLANES):
        for n, part in enumerate(PARTS):
            for c in range(4):
                index = (4 * lane + c) & (LANES - 1)
                pick = lambda v: jnp.take_along_axis(v, index, axis=1, mode="promise_in_bounds")
                own[z * 4 + c, part, :] = jnp.where(
                    lane < 32, pick(held[z * 6 + n]), pick(held[z * 6 + 3 + n])
                )
    for half in range(2):
        keep(field, field_out, half, 0).wait()
        keep(coef, coef_out, half, 1).wait()


def local_peak(box_cost, box_owner, *operands):
    vmem = pl.BlockSpec(memory_space=pltpu.VMEM)
    smem = pl.BlockSpec(memory_space=pltpu.SMEM)
    hbm = pl.BlockSpec(memory_space=pl.ANY)
    rows = lambda n: jax.ShapeDtypeStruct((n, SUB, LANES), f32)
    devices = lax.axis_size("gx") * lax.axis_size("gy")
    assert devices == LANES or devices == 1
    return pl.pallas_call(
        peak_kernel,
        in_specs=[smem, smem, hbm] + [vmem] * 7,
        out_specs=[vmem, hbm, hbm] + [vmem] * 7,
        out_shape=[
            jax.ShapeDtypeStruct((LANES, LANES), f32),
            rows(PLANES * ROWS),
            rows(PLANES * ROWS),
            rows(8),
            rows(8),
            rows(16),
            rows(3),
            jax.ShapeDtypeStruct((SUB + 8, LANES), f32),
            jax.ShapeDtypeStruct((RPAD, LANES), f32),
            jax.ShapeDtypeStruct((2 * SUB, 2 * LANES), f32),
        ],
        scratch_shapes=[
            pltpu.VMEM((PLANES * ROWS, SUB, LANES), f32),
            pltpu.VMEM((PLANES * ROWS, SUB, LANES), f32),
            pltpu.VMEM((LANES, LANES), f32),
            pltpu.SemaphoreType.DMA((2,)),
            pltpu.SemaphoreType.DMA((2, 2)),
        ],
        compiler_params=pltpu.CompilerParams(vmem_limit_bytes=VMEM_BYTES),
    )(box_cost, box_owner, *operands)


def corners_kernel(own, below, above, whole, to_left, to_right):
    lane = lax.broadcasted_iota(jnp.int32, (8, LANES), 1)
    for z in range(PLANES):
        for part in PARTS:
            before = below[z * 2 + 1, part, :]
            after = above[z * 2, part, :]
            for c, column in enumerate((LANES - 2, LANES - 1, 0, 1)):
                value = jnp.where(
                    lane == LANES - 1,
                    pltpu.roll(before, LANES - 1 - column, 1),
                    jnp.where(
                        lane == ROWS,
                        pltpu.roll(after, (ROWS - column) % LANES, 1),
                        own[z * 4 + c, part, :],
                    ),
                )
                whole[z * 4 + c, part, :] = value
                if c < 2:
                    to_right[z * 2 + c, part, :] = value
                else:
                    to_left[z * 2 + c - 2, part, :] = value


def corners(own, below, above):
    rows = lambda n: jax.ShapeDtypeStruct((n, SUB, LANES), f32)
    return pl.pallas_call(
        corners_kernel,
        out_shape=[rows(16), rows(8), rows(8)],
        compiler_params=pltpu.CompilerParams(vmem_limit_bytes=VMEM_BYTES),
    )(own, below, above)


def swap_quarters(planes, lane):
    low_half = lane < 64
    even = ((lane >> 5) & 1) == 0
    a, b, c, d = planes
    a, c = (
        jnp.where(low_half, a, pltpu.roll(c, 64, 1)),
        jnp.where(low_half, pltpu.roll(a, 64, 1), c),
    )
    b, d = (
        jnp.where(low_half, b, pltpu.roll(d, 64, 1)),
        jnp.where(low_half, pltpu.roll(b, 64, 1), d),
    )
    a, b = (
        jnp.where(even, a, pltpu.roll(b, 32, 1)),
        jnp.where(even, pltpu.roll(a, 96, 1), b),
    )
    c, d = (
        jnp.where(even, c, pltpu.roll(d, 32, 1)),
        jnp.where(even, pltpu.roll(c, 96, 1), d),
    )
    return [a, b, c, d]


def substep_kernel(
    box_cost,
    flame_flag,
    field_in,
    coef_in,
    below,
    above,
    left,
    right,
    own,
    gathered,
    scales,
    table_ref,
    log_table_ref,
    sum_table_ref,
    out,
    load_out,
    field,
    coef,
    first,
    strip_field,
    strip_coef,
    strip_first,
    fluxes,
    edge_flux,
    raw_flux,
    spread,
    packed,
    start_ref,
    conc_ref,
    ext_ref,
    out_rows,
    in_sem,
    out_sem,
):
    def fetch(z):
        held, rows = pl.ds(z * ROWS, ROWS), pl.ds(z * HROWS + 2, ROWS)
        return [
            pltpu.make_async_copy(field_in.at[held], field.at[rows], in_sem.at[z, 0]),
            pltpu.make_async_copy(coef_in.at[held], coef.at[rows], in_sem.at[z, 1]),
        ]

    for z in range(PLANES):
        for copy in fetch(z):
            copy.start()
    inv_mass = scales[0]
    live = live_rows()
    table = table_ref[:, : 3 * SUB + 8].astype(bf16)
    lane = lax.broadcasted_iota(jnp.int32, (8, LANES), 1)
    received = gathered[...]
    columns = lax.broadcasted_iota(jnp.int32, received.shape, 1)
    peak = jnp.max(jnp.where(columns == 0, received, 0.0), keepdims=True)
    step = CFL_SAFE / ((4.0 + 2.0 * Z_WEIGHT) * peak)
    mine = jnp.sum(jnp.where(columns == 1, received, 0.0))
    everyone = jnp.sum(jnp.where(columns == 2, received, 0.0))
    load_out[0, 0] = mine / (everyone / 16.0)
    step = jnp.broadcast_to(step, (8, LANES))

    for z in range(PLANES):
        for layer in range(2):
            field[z * HROWS + layer] = below[z * 2 + layer]
            field[z * HROWS + ROWS + 2 + layer] = above[z * 2 + layer]
        for c in range(2):
            strip_field[z * 8 + c] = left[z * 2 + c]
            strip_field[z * 8 + 2 + c] = own[z * 4 + 2 + c]
            strip_field[z * 8 + 4 + c] = own[z * 4 + c]
            strip_field[z * 8 + 6 + c] = right[z * 2 + c]

    def coefficients(source, target, base, count):
        def body(index, carry):
            at = [base + index * CHUNK + i for i in range(CHUNK)]
            rows = [source[i] for i in at]
            for i, value in zip(at, diffusivity(rows, inv_mass, table, live)):
                target[i] = value
            return carry

        lax.fori_loop(0, count // CHUNK, body, 0, unroll=4)

    def face(source, weight, here, there, part):
        return (weight[here, part, :] + weight[there, part, :]) * (
            source[there, part, :] - source[here, part, :]
        )

    odd = (lane & 1) == 1

    def side_fluxes(source, weight):
        even_from = lane >> 1
        odd_from = ((lane + 1) >> 1) & (ROWS - 1)
        for z in range(PLANES):
            for part in PARTS:
                entering = face(source, weight, z * 8 + 1, z * 8 + 2, part)
                leaving = face(source, weight, z * 8 + 5, z * 8 + 6, part)
                fluxes[z * 2, part, :] = entering
                fluxes[z * 2 + 1, part, :] = leaving
                pick = lambda v, at: jnp.take_along_axis(v, at, axis=1, mode="promise_in_bounds")
                edge_flux[z, part, :] = jnp.where(
                    odd, pick(leaving, odd_from), pick(entering, even_from)
                )

    def strip_update():
        for r in (1, 2, 5, 6):
            for part in PARTS:
                above_flux = None
                for z in range(PLANES):
                    at = z * 8 + r
                    here = strip_field[at, part, :]
                    weight = strip_coef[at, part, :]
                    total = face(strip_field, strip_coef, at, at + 1, part)
                    total = total - face(strip_field, strip_coef, at - 1, at, part)
                    onward = (weight + pltpu.roll(weight, LANES - 1, 1)) * (
                        pltpu.roll(here, LANES - 1, 1) - here
                    )
                    total = total + (onward - pltpu.roll(onward, 1, 1))
                    if above_flux is not None:
                        total = total - Z_WEIGHT * above_flux
                    if z < PLANES - 1:
                        above_flux = face(strip_field, strip_coef, at, at + 8, part)
                        total = total + Z_WEIGHT * above_flux
                    strip_first[at, part, :] = here + step * total

    def onward_flux(source, weight, at, part):
        c, d = source[at, part, :], weight[at, part, :]
        return (d + pltpu.roll(d, LANES - 1, 1)) * (pltpu.roll(c, LANES - 1, 1) - c)

    def updated(source, weight, x0, count, part, onward, ends):
        result = [[] for _ in range(count)]
        above_flux = [None] * count
        for z in range(PLANES):
            base = z * HROWS + x0 + 1
            here = [source[base + i, part, :] for i in range(count + 2)]
            coefs = [weight[base + i, part, :] for i in range(count + 2)]
            along = [
                (coefs[i] + coefs[i + 1]) * (here[i + 1] - here[i]) for i in range(count + 1)
            ]
            for i in range(count):
                c, d = here[i + 1], coefs[i + 1]
                raw, back = onward[i][z]
                entering, leaving = ends[i][z]
                total = (along[i + 1] - along[i]) + (
                    jnp.where(lane == LANES - 1, leaving, raw)
                    - jnp.where(lane == 0, entering, back)
                )
                if z < PLANES - 1:
                    over = base + i + 1 + HROWS
                    flux = Z_WEIGHT * (
                        (d + weight[over, part, :]) * (source[over, part, :] - c)
                    )
                    total = total + flux
                if z > 0:
                    total = total - above_flux[i]
                if z < PLANES - 1:
                    above_flux[i] = flux
                result[i].append(c + step * total)
        return result

    def outer_row(source, weight, x, part):
        shift = -x % LANES
        onward, ends = [], []
        for z in range(PLANES):
            raw = onward_flux(source, weight, z * HROWS + x + 2, part)
            onward.append((raw, pltpu.roll(raw, 1, 1)))
            ends.append(
                (
                    pltpu.roll(fluxes[z * 2, part, :], shift, 1),
                    pltpu.roll(fluxes[z * 2 + 1, part, :], (shift + LANES - 1) % LANES, 1),
                )
            )
        return updated(source, weight, x, 1, part, [onward], [ends])[0]

    def start_flux(source, weight, group):
        for part in PARTS:
            for i in range(GROUP):
                for z in range(PLANES):
                    raw_flux[i * PLANES + z, part, :] = onward_flux(
                        source, weight, z * HROWS + group * GROUP + i + 2, part
                    )

    def finish_rows(source, weight, group, part):
        x = group * GROUP
        onward, ends = [], []
        for i in range(GROUP):
            raws = [raw_flux[i * PLANES + z, part, :] for z in range(PLANES)]
            onward.append([(raw, pltpu.roll(raw, 1, 1)) for raw in raws])
            shift = (2 * LANES - 2 * (x + i)) & (LANES - 1)
            edges = [pltpu.roll(edge_flux[z, part, :], shift, 1) for z in range(PLANES)]
            ends.append([(edge, edge) for edge in edges])
        return updated(source, weight, x, GROUP, part, onward, ends)

    coefficients(strip_field, strip_coef, 0, PLANES * 8)
    side_fluxes(strip_field, strip_coef)
    strip_update()
    for z in range(PLANES):
        for copy in fetch(z):
            copy.wait()
    halo = [z * HROWS + x for z in range(PLANES) for x in (0, 1, ROWS + 2, ROWS + 3)]
    for n in range(0, len(halo), CHUNK):
        at = halo[n : n + CHUNK]
        for i, value in zip(at, diffusivity([field[i] for i in at], inv_mass, table, live)):
            coef[i] = value

    for x in (-1, ROWS):
        for part in PARTS:
            for z, value in enumerate(outer_row(field, coef, x, part)):
                first[z * HROWS + x + 2, part, :] = value

    start_flux(field, coef, 0)

    def first_rows(group, carry):
        for part in PARTS:
            for i, planes in enumerate(finish_rows(field, coef, group, part)):
                for z, value in enumerate(planes):
                    first[z * HROWS + group * GROUP + i + 2, part, :] = value
        start_flux(field, coef, group + 1)
        return carry

    lax.fori_loop(0, ROWS // GROUP, first_rows, 0)
    for z in range(PLANES):
        first[z * HROWS] = field[z * HROWS]
        first[z * HROWS + HROWS - 1] = field[z * HROWS + HROWS - 1]
        for r in (0, 3, 4, 7):
            strip_first[z * 8 + r] = strip_field[z * 8 + r]
    coefficients(strip_first, strip_coef, 0, PLANES * 8)
    side_fluxes(strip_first, strip_coef)
    coefficients(first, coef, 0, PLANES * HROWS)

    def pack(group):
        for part in PARTS:
            for i in range(GROUP):
                planes = [spread[i * PLANES + z, part, :] for z in range(PLANES)]
                planes = swap_quarters(planes, lane)
                for j in range(4):
                    packed[j * ROWS + group * GROUP + i, part, :] = planes[j]

    start_flux(first, coef, 0)

    def second_rows(group, carry):
        pack(jnp.maximum(group - 1, 0))
        for part in PARTS:
            for i, planes in enumerate(finish_rows(first, coef, group, part)):
                for z, value in enumerate(planes):
                    spread[i * PLANES + z, part, :] = value
        start_flux(first, coef, group + 1)
        return carry

    for i in range(GROUP * PLANES):
        spread[i] = jnp.ones((SUB, LANES), f32)
    lax.fori_loop(0, ROWS // GROUP, second_rows, 0)
    pack(ROWS // GROUP - 1)

    log_table = log_table_ref[:, : 2 * SUB + 16].astype(bf16)
    sum_table = sum_table_ref[:, : 2 * RPAD].astype(bf16)
    ext_row = lax.broadcasted_iota(jnp.int32, (16, LANES), 0)
    is_high = (ext_row == 0) | (ext_row == 2) | (ext_row == 5)
    is_middle = (ext_row == 1) | (ext_row == 3)
    is_one = (ext_row >= 6) & (ext_row < 9)
    mass = scales[1]
    heat = scales[2]
    sub24 = lax.broadcasted_iota(jnp.int32, (SUB, LANES), 0)

    def box(p, j, carry):
        base = j * ROWS + p * BOX

        def prepare(i, inner):
            row = packed[base + i]
            beginning = row * inv_mass
            start_ref[i] = beginning
            conc_ref[i] = beginning
            inverse = 1.0 / row[SPECIES : SPECIES + 1, :]
            high = coarse(inverse)
            middle = coarse(inverse - high)
            rest = (inverse - high) - middle
            ext = jnp.where(
                is_high,
                jnp.broadcast_to(high, (16, LANES)),
                jnp.where(
                    is_middle,
                    jnp.broadcast_to(middle, (16, LANES)),
                    jnp.where(ext_row == 4, jnp.broadcast_to(rest, (16, LANES)), 0.0),
                ),
            )
            ext_ref[i] = jnp.where(is_one, 1.0, ext)
            return inner

        lax.fori_loop(0, BOX, prepare, 0, unroll=8)

        chunks = BOX // BOX_CHUNK

        def rates(chunk):
            at = [chunk * BOX_CHUNK + i for i in range(BOX_CHUNK)]
            conc = jnp.concatenate([conc_ref[i] for i in at], axis=1)
            ext = jnp.concatenate([ext_ref[i] for i in at], axis=1)
            logs = jnp.log2(conc)
            high = coarse(logs)
            stacked = jnp.concatenate([high, logs - high, ext], axis=0).astype(bf16)
            return jnp.dot(log_table, stacked, preferred_element_type=f32)

        def advance(chunk, exponent):
            at = [chunk * BOX_CHUNK + i for i in range(BOX_CHUNK)]
            progress = jnp.exp2(exponent)
            high = coarse(progress)
            stacked = jnp.concatenate([high, progress - high], axis=0).astype(bf16)
            sums = jnp.dot(sum_table, stacked, preferred_element_type=f32)
            conc = jnp.concatenate([conc_ref[i] for i in at], axis=1)
            start = jnp.concatenate([start_ref[i] for i in at], axis=1)
            conc = (start + sums[:SUB, :]) * (conc / (conc + sums[SUB:, :]))
            for n, i in enumerate(at):
                conc_ref[i] = conc[:, n * LANES : (n + 1) * LANES]

        def sweep(number, inner):
            ahead = rates(0)
            for chunk in range(chunks):
                exponent = ahead
                if chunk + 1 < chunks:
                    ahead = rates(chunk + 1)
                advance(chunk, exponent)
            return inner

        lax.fori_loop(0, box_cost[p, j], sweep, 0)
        flag = flame_flag[p, j].astype(f32)

        def finish(i, inner):
            row = packed[base + i]
            advanced = conc_ref[i] * mass
            source = jnp.sum(heat * (advanced - row), axis=0, keepdims=True)
            temperature = row[SPECIES : SPECIES + 1, :] + flag * source
            packed[base + i] = jnp.where(
                sub24 == SPECIES, jnp.broadcast_to(temperature, (SUB, LANES)), advanced
            )
            return inner

        lax.fori_loop(0, BOX, finish, 0, unroll=8)
        return carry

    def give(x, carry):
        for part in PARTS:
            planes = swap_quarters([packed[j * ROWS + x, part, :] for j in range(4)], lane)
            for z in range(PLANES):
                out_rows[z, x, part, :] = planes[z]
        return carry

    for p in range(2):
        rows = pl.ds(p * BOX, BOX)
        lax.fori_loop(0, 4, functools.partial(box, p), 0)
        lax.fori_loop(p * BOX, (p + 1) * BOX, give, 0, unroll=4)
        for k in range(FIELDS):
            pltpu.make_async_copy(
                out_rows.at[:, rows, k], out.at[k, :, rows], out_sem.at[p]
            ).start()
    for p in range(2):
        whole = out.at[:, :, pl.ds(p * BOX, BOX)]
        pltpu.make_async_copy(whole, whole, out_sem.at[p]).wait()


def substep(box_cost, flame_flag, *operands):
    vmem = pl.BlockSpec(memory_space=pltpu.VMEM)
    smem = pl.BlockSpec(memory_space=pltpu.SMEM)
    hbm = pl.BlockSpec(memory_space=pl.ANY)
    rows = lambda n: pltpu.VMEM((n, SUB, LANES), f32)
    return pl.pallas_call(
        substep_kernel,
        in_specs=[smem, smem, hbm, hbm] + [vmem] * (len(operands) - 2),
        out_specs=[hbm, smem],
        out_shape=[
            jax.ShapeDtypeStruct((FIELDS, PLANES, ROWS, LANES), f32),
            jax.ShapeDtypeStruct((1, 1), f32),
        ],
        scratch_shapes=[
            rows(PLANES * HROWS),
            rows(PLANES * HROWS),
            rows(PLANES * HROWS),
            rows(32),
            rows(32),
            rows(32),
            rows(8),
            rows(4),
            rows(GROUP * PLANES),
            rows(GROUP * PLANES),
            rows(PLANES * ROWS),
            rows(BOX),
            rows(BOX),
            pltpu.VMEM((BOX, 16, LANES), f32),
            pltpu.VMEM((PLANES, ROWS, SUB, LANES), f32),
            pltpu.SemaphoreType.DMA((PLANES, 2)),
            pltpu.SemaphoreType.DMA((2,)),
        ],
        compiler_params=pltpu.CompilerParams(vmem_limit_bytes=VMEM_BYTES),
    )(box_cost, flame_flag, *operands)


def shifted(x, axis, by):
    count = lax.axis_size(axis)
    return lax.ppermute(x, axis, [(i, (i + by) % count) for i in range(count)])


def per_device(
    state,
    masses,
    reciprocals,
    rate_scale,
    energy,
    reactants,
    products,
    heat_release,
    box_cost,
    box_owner,
    flame_flag,
):
    message, field, coef, low, high, own, *constants = local_peak(
        box_cost,
        box_owner,
        state.reshape(FIELDS, PLANES * ROWS, LANES),
        masses.reshape(1, -1),
        reciprocals,
        rate_scale.reshape(1, -1),
        energy.reshape(1, -1),
        reactants.T,
        products.T,
        heat_release.reshape(1, -1),
    )
    below = shifted(high, "gx", 1)
    above = shifted(low, "gx", -1)
    own, to_left, to_right = corners(own, below, above)
    left = shifted(to_right, "gy", 1)
    right = shifted(to_left, "gy", -1)
    gathered = lax.all_to_all(message, ("gx", "gy"), 0, 0, tiled=True)
    return tuple(
        substep(
            box_cost,
            flame_flag,
            field,
            coef,
            below,
            above,
            left,
            right,
            own,
            gathered,
            *constants,
        )
    )


def solution(mesh):
    split = P("gx", "gy")
    whole = P(None, None, "gx", "gy")
    return jax.shard_map(
        per_device,
        mesh=mesh,
        in_specs=(whole, P(), P(), P(), P(), P(), P(), P(), split, split, split),
        out_specs=(whole, split),
        check_vma=False,
    )
```

```python
import functools

import jax
import jax.numpy as jnp
from jax import lax
from jax.experimental import pallas as pl
from jax.experimental.pallas import tpu as pltpu
from jax.sharding import PartitionSpec as P

SPECIES = 21
FIELDS = 22
SUB = 24
LANES = 128
PLANES = 4
ROWS = 64
HROWS = ROWS + 4
BOX = 32
REACTIONS = 84
RPAD = 88
CHUNK = 4
BOX_CHUNK = 4
GROUP = 2
AHEAD = 3
LOG2E = 1.4426950408889634
Z_WEIGHT = 0.25
CFL_SAFE = 0.5
HALF = 0.5
VMEM_BYTES = 56 * 1024 * 1024

PARTS = [slice(0, 8), slice(8, 16), slice(16, 24)]

f32 = jnp.float32
bf16 = jnp.bfloat16


def live_rows():
    return (lax.broadcasted_iota(jnp.int32, (SUB, LANES), 0) < SPECIES).astype(f32)


def fill_spare(rows, count):
    def body(i, carry):
        rows[i, FIELDS:SUB, :] = jnp.ones((SUB - FIELDS, LANES), f32)
        return carry

    lax.fori_loop(0, count, body, 0, unroll=8)


def coarse(x):
    return x.astype(bf16).astype(f32)


def diffusivity(rows, inv_mass, table, live):
    amounts = jnp.concatenate([row * inv_mass for row in rows], axis=1)
    high = coarse(amounts)
    low = amounts - high
    blank = jnp.zeros((8, amounts.shape[1]), f32)
    stacked = jnp.concatenate([high, low, high, blank], axis=0).astype(bf16)
    sums = jnp.dot(table, stacked, preferred_element_type=f32)
    result = []
    for i, row in enumerate(rows):
        lanes = slice(i * LANES, (i + 1) * LANES)
        heat = row[SPECIES : SPECIES + 1, :]
        scale = (HALF * heat * jnp.sqrt(heat)) * sums[SUB : SUB + 8, lanes]
        scale = jnp.concatenate([scale] * 3, axis=0)
        result.append(live * (1.0 - row) * scale / sums[:SUB, lanes])
    return result


def split3(x):
    high = coarse(x)
    middle = coarse(x - high)
    return high, middle, coarse((x - high) - middle)


def fill_tables(
    masses,
    reciprocals,
    rate_scale,
    energy,
    reactants,
    products,
    heat_release,
    scales,
    table,
    log_table,
    sum_table,
    square,
):
    lane = lax.broadcasted_iota(jnp.int32, (LANES, LANES), 1)
    row = lax.broadcasted_iota(jnp.int32, (LANES, LANES), 0)

    def padded(value, filler=0.0):
        square[...] = jnp.full((LANES, LANES), filler, f32)
        square[: value.shape[0], : value.shape[1]] = value
        return square[...]

    def column(ref, filler):
        return jnp.broadcast_to(padded(ref[...], filler)[:1], (LANES, LANES)).T

    mass = column(masses, 1.0)[:SUB]
    scales[0] = 1.0 / mass
    scales[1] = mass
    scales[2] = column(heat_release, 0.0)[:SUB]

    cross = padded(reciprocals[...])
    cross = jnp.where(row == lane, 0.0, cross).T
    cross = jnp.where(lane < SPECIES, jnp.where(row < SPECIES, cross, 1.0), 0.0)[: SUB + 8]
    high = coarse(cross)
    table[...] = high + pltpu.roll(high, SUB, 1) + pltpu.roll(cross - high, 2 * SUB, 1)

    react_back = padded(reactants[...].astype(f32))
    react = react_back.T
    eh, em, _ = split3((-LOG2E) * column(energy, 0.0)[:RPAD])
    ah, am, al = split3(jnp.log2(column(rate_scale, 1.0)[:RPAD]))
    place = lane[:RPAD]
    ext = jnp.zeros((RPAD, LANES), f32)
    spare = (SPECIES, SPECIES + 1, SPECIES + 2)
    for n, value in zip(spare + tuple(SUB + n for n in spare), (eh, eh, ah, em, am, al)):
        ext = jnp.where(place == n, value, ext)
    log_table[...] = react[:RPAD] + pltpu.roll(react[:RPAD], SUB, 1) + ext

    make = padded(products[...].astype(f32))[:SUB]
    sums = HALF * jnp.concatenate([make, react_back[:SUB]], axis=0)
    moved = pltpu.roll(sums, RPAD, 1)
    place = lane[: 2 * SUB]
    sum_table[:, :LANES] = jnp.where(place < RPAD, sums, moved)
    sum_table[:, LANES:] = jnp.where(place < 2 * RPAD - LANES, moved, 0.0)


def edges_kernel(
    state,
    masses,
    reciprocals,
    rate_scale,
    energy,
    reactants,
    products,
    heat_release,
    field_out,
    low,
    high,
    own,
    scales,
    table,
    log_table,
    sum_table,
    field,
    square,
    in_sem,
    out_sem,
):
    def half_rows(half):
        return pl.ds(half * 2 * ROWS, 2 * ROWS)

    def keep(half):
        rows = half_rows(half)
        return pltpu.make_async_copy(field.at[rows], field_out.at[rows], out_sem.at[half])

    for half in range(2):
        rows = half_rows(half)
        for k in range(FIELDS):
            pltpu.make_async_copy(state.at[k, rows], field.at[rows, k], in_sem.at[half]).start()
    fill_spare(field, PLANES * ROWS)
    fill_tables(
        masses,
        reciprocals,
        rate_scale,
        energy,
        reactants,
        products,
        heat_release,
        scales,
        table,
        log_table,
        sum_table,
        square,
    )
    lane = lax.broadcasted_iota(jnp.int32, (8, LANES), 1)
    for half in range(2):
        whole = state.at[:, half_rows(half)]
        pltpu.make_async_copy(whole, whole, in_sem.at[half]).wait()
        keep(half).start()
        planes = (2 * half, 2 * half + 1)
        for z in planes:
            for layer in range(2):
                low[z * 2 + layer] = field[z * ROWS + layer]
                high[z * 2 + layer] = field[z * ROWS + ROWS - 2 + layer]

        def gather(index, held):
            mine = (lane >> 2) == index
            result = []
            for z in planes:
                for group in range(2):
                    for part in PARTS:
                        row = field[z * ROWS + group * 32 + index, part, :]
                        turned = pltpu.roll(row, 4 * index + 2, 1)
                        result.append(jnp.where(mine, turned, held[len(result)]))
            return tuple(result)

        held = lax.fori_loop(0, 32, gather, (jnp.ones((8, LANES), f32),) * 12, unroll=2)
        for i, z in enumerate(planes):
            for n, part in enumerate(PARTS):
                for c in range(4):
                    index = (4 * lane + c) & (LANES - 1)
                    pick = lambda v: jnp.take_along_axis(v, index, axis=1, mode="promise_in_bounds")
                    own[z * 4 + c, part, :] = jnp.where(
                        lane < 32, pick(held[i * 6 + n]), pick(held[i * 6 + 3 + n])
                    )
    for half in range(2):
        keep(half).wait()


def edges(*operands):
    vmem = pl.BlockSpec(memory_space=pltpu.VMEM)
    hbm = pl.BlockSpec(memory_space=pl.ANY)
    rows = lambda n: jax.ShapeDtypeStruct((n, SUB, LANES), f32)
    return pl.pallas_call(
        edges_kernel,
        in_specs=[hbm] + [vmem] * 7,
        out_specs=[hbm] + [vmem] * 7,
        out_shape=[
            rows(PLANES * ROWS),
            rows(8),
            rows(8),
            rows(16),
            rows(3),
            jax.ShapeDtypeStruct((SUB + 8, LANES), f32),
            jax.ShapeDtypeStruct((RPAD, LANES), f32),
            jax.ShapeDtypeStruct((2 * SUB, 2 * LANES), f32),
        ],
        scratch_shapes=[
            pltpu.VMEM((PLANES * ROWS, SUB, LANES), f32),
            pltpu.VMEM((LANES, LANES), f32),
            pltpu.SemaphoreType.DMA((2,)),
            pltpu.SemaphoreType.DMA((2,)),
        ],
        compiler_params=pltpu.CompilerParams(vmem_limit_bytes=VMEM_BYTES),
    )(*operands)


def lane_flux(row, weight):
    onward = LANES - 1
    return (weight + pltpu.roll(weight, onward, 1)) * (pltpu.roll(row, onward, 1) - row)


def peak_kernel(
    box_cost,
    box_owner,
    field_in,
    scales,
    table_ref,
    message,
    coef_out,
    flux_out,
    field,
    coef,
    flux,
    in_sem,
    out_sem,
):
    quarter = lambda z: pl.ds(z * ROWS, ROWS)

    def fetch(z):
        return pltpu.make_async_copy(
            field_in.at[quarter(z)], field.at[quarter(z)], in_sem.at[z]
        )

    def keep(z):
        return [
            pltpu.make_async_copy(coef.at[quarter(z)], coef_out.at[quarter(z)], out_sem.at[z, 0]),
            pltpu.make_async_copy(flux.at[quarter(z)], flux_out.at[quarter(z)], out_sem.at[z, 1]),
        ]

    for z in range(PLANES):
        fetch(z).start()
    inv_mass = scales[0]
    live = live_rows()
    table = table_ref[:, : 3 * SUB + 8].astype(bf16)
    best = jnp.zeros((SUB, LANES), f32)
    for z in range(PLANES):
        fetch(z).wait()

        def body(index, best):
            at = [z * ROWS + index * CHUNK + i for i in range(CHUNK)]
            rows = [field[i] for i in at]
            for i, row, value in zip(at, rows, diffusivity(rows, inv_mass, table, live)):
                coef[i] = value
                flux[i] = lane_flux(row, value)
                best = jnp.maximum(best, value)
            return best

        best = lax.fori_loop(0, ROWS // CHUNK, body, best, unroll=4)
        for copy in keep(z):
            copy.start()
    top = 2.0 * jnp.max(best)
    device = lax.broadcasted_iota(jnp.int32, (LANES, LANES), 0)
    column = lax.broadcasted_iota(jnp.int32, (LANES, LANES), 1)
    count = lax.axis_size("gy")
    same = device // count == lax.axis_index("gx")
    place = device % count
    charged = jnp.zeros((LANES, LANES), f32)
    total = 0.0
    for p in range(2):
        for j in range(4):
            cost = box_cost[p, j].astype(f32)
            total = total + cost
            charged = charged + jnp.where(place == box_owner[p, j], cost, 0.0)
    tally = jnp.where(column == 1, charged, jnp.where(column == 2, total, 0.0))
    message[...] = jnp.where(column == 0, top, jnp.where(same, tally, 0.0))
    for z in range(PLANES):
        for copy in keep(z):
            copy.wait()


def local_peak(box_cost, box_owner, field, scales, table):
    vmem = pl.BlockSpec(memory_space=pltpu.VMEM)
    smem = pl.BlockSpec(memory_space=pltpu.SMEM)
    hbm = pl.BlockSpec(memory_space=pl.ANY)
    rows = jax.ShapeDtypeStruct((PLANES * ROWS, SUB, LANES), f32)
    devices = lax.axis_size("gx") * lax.axis_size("gy")
    assert devices == LANES or devices == 1
    return pl.pallas_call(
        peak_kernel,
        in_specs=[smem, smem, hbm, vmem, vmem],
        out_specs=[vmem, hbm, hbm],
        out_shape=[jax.ShapeDtypeStruct((LANES, LANES), f32), rows, rows],
        scratch_shapes=[
            pltpu.VMEM((PLANES * ROWS, SUB, LANES), f32),
            pltpu.VMEM((PLANES * ROWS, SUB, LANES), f32),
            pltpu.VMEM((PLANES * ROWS, SUB, LANES), f32),
            pltpu.SemaphoreType.DMA((PLANES,)),
            pltpu.SemaphoreType.DMA((PLANES, 2)),
        ],
        compiler_params=pltpu.CompilerParams(vmem_limit_bytes=VMEM_BYTES),
    )(box_cost, box_owner, field, scales, table)


def corners_kernel(own, below, above, whole, to_left, to_right):
    lane = lax.broadcasted_iota(jnp.int32, (8, LANES), 1)
    for z in range(PLANES):
        for part in PARTS:
            before = below[z * 2 + 1, part, :]
            after = above[z * 2, part, :]
            for c, column in enumerate((LANES - 2, LANES - 1, 0, 1)):
                value = jnp.where(
                    lane == LANES - 1,
                    pltpu.roll(before, LANES - 1 - column, 1),
                    jnp.where(
                        lane == ROWS,
                        pltpu.roll(after, (ROWS - column) % LANES, 1),
                        own[z * 4 + c, part, :],
                    ),
                )
                whole[z * 4 + c, part, :] = value
                if c < 2:
                    to_right[z * 2 + c, part, :] = value
                else:
                    to_left[z * 2 + c - 2, part, :] = value


def corners(own, below, above):
    rows = lambda n: jax.ShapeDtypeStruct((n, SUB, LANES), f32)
    return pl.pallas_call(
        corners_kernel,
        out_shape=[rows(16), rows(8), rows(8)],
        compiler_params=pltpu.CompilerParams(vmem_limit_bytes=VMEM_BYTES),
    )(own, below, above)


def swap_quarters(planes, lane):
    low_half = lane < 64
    even = ((lane >> 5) & 1) == 0
    a, b, c, d = planes
    a, c = (
        jnp.where(low_half, a, pltpu.roll(c, 64, 1)),
        jnp.where(low_half, pltpu.roll(a, 64, 1), c),
    )
    b, d = (
        jnp.where(low_half, b, pltpu.roll(d, 64, 1)),
        jnp.where(low_half, pltpu.roll(b, 64, 1), d),
    )
    a, b = (
        jnp.where(even, a, pltpu.roll(b, 32, 1)),
        jnp.where(even, pltpu.roll(a, 96, 1), b),
    )
    c, d = (
        jnp.where(even, c, pltpu.roll(d, 32, 1)),
        jnp.where(even, pltpu.roll(c, 96, 1), d),
    )
    return [a, b, c, d]


def substep_kernel(
    box_cost,
    flame_flag,
    field_in,
    coef_in,
    flux_in,
    below,
    above,
    left,
    right,
    own,
    gathered,
    scales,
    table_ref,
    log_table_ref,
    sum_table_ref,
    out,
    load_out,
    field,
    coef,
    first,
    strip_field,
    strip_coef,
    strip_first,
    fluxes,
    edge_flux,
    flux,
    spread,
    packed,
    start_ref,
    conc_ref,
    ext_ref,
    out_rows,
    in_sem,
    out_sem,
):
    def fetch(z):
        held, rows = pl.ds(z * ROWS, ROWS), pl.ds(z * HROWS + 2, ROWS)
        return [
            pltpu.make_async_copy(field_in.at[held], field.at[rows], in_sem.at[z, 0]),
            pltpu.make_async_copy(coef_in.at[held], coef.at[rows], in_sem.at[z, 1]),
            pltpu.make_async_copy(flux_in.at[held], flux.at[rows], in_sem.at[z, 2]),
        ]

    for z in range(PLANES):
        for copy in fetch(z):
            copy.start()
    inv_mass = scales[0]
    live = live_rows()
    table = table_ref[:, : 3 * SUB + 8].astype(bf16)
    lane = lax.broadcasted_iota(jnp.int32, (8, LANES), 1)
    received = gathered[...]
    columns = lax.broadcasted_iota(jnp.int32, received.shape, 1)
    peak = jnp.max(jnp.where(columns == 0, received, 0.0), keepdims=True)
    step = CFL_SAFE / ((4.0 + 2.0 * Z_WEIGHT) * peak)
    mine = jnp.sum(jnp.where(columns == 1, received, 0.0))
    everyone = jnp.sum(jnp.where(columns == 2, received, 0.0))
    load_out[0, 0] = mine / (everyone / 16.0)
    step = jnp.broadcast_to(step, (8, LANES))

    for z in range(PLANES):
        for layer in range(2):
            field[z * HROWS + layer] = below[z * 2 + layer]
            field[z * HROWS + ROWS + 2 + layer] = above[z * 2 + layer]
        for c in range(2):
            strip_field[z * 8 + c] = left[z * 2 + c]
            strip_field[z * 8 + 2 + c] = own[z * 4 + 2 + c]
            strip_field[z * 8 + 4 + c] = own[z * 4 + c]
            strip_field[z * 8 + 6 + c] = right[z * 2 + c]

    def coefficients(source, target, count, with_flux):
        def body(index, carry):
            at = [index * CHUNK + i for i in range(CHUNK)]
            rows = [source[i] for i in at]
            for i, row, value in zip(at, rows, diffusivity(rows, inv_mass, table, live)):
                target[i] = value
                if with_flux:
                    flux[i] = lane_flux(row, value)
            return carry

        lax.fori_loop(0, count // CHUNK, body, 0, unroll=4)

    def face(source, weight, here, there, part):
        return (weight[here, part, :] + weight[there, part, :]) * (
            source[there, part, :] - source[here, part, :]
        )

    odd = (lane & 1) == 1

    def side_fluxes(source, weight):
        even_from = lane >> 1
        odd_from = ((lane + 1) >> 1) & (ROWS - 1)
        for z in range(PLANES):
            for part in PARTS:
                entering = face(source, weight, z * 8 + 1, z * 8 + 2, part)
                leaving = face(source, weight, z * 8 + 5, z * 8 + 6, part)
                fluxes[z * 2, part, :] = entering
                fluxes[z * 2 + 1, part, :] = leaving
                pick = lambda v, at: jnp.take_along_axis(v, at, axis=1, mode="promise_in_bounds")
                edge_flux[z, part, :] = jnp.where(
                    odd, pick(leaving, odd_from), pick(entering, even_from)
                )

    def strip_update():
        for r in (1, 2, 5, 6):
            for part in PARTS:
                above_flux = None
                for z in range(PLANES):
                    at = z * 8 + r
                    here = strip_field[at, part, :]
                    weight = strip_coef[at, part, :]
                    total = face(strip_field, strip_coef, at, at + 1, part)
                    total = total - face(strip_field, strip_coef, at - 1, at, part)
                    onward = (weight + pltpu.roll(weight, LANES - 1, 1)) * (
                        pltpu.roll(here, LANES - 1, 1) - here
                    )
                    total = total + (onward - pltpu.roll(onward, 1, 1))
                    if above_flux is not None:
                        total = total - Z_WEIGHT * above_flux
                    if z < PLANES - 1:
                        above_flux = face(strip_field, strip_coef, at, at + 8, part)
                        total = total + Z_WEIGHT * above_flux
                    strip_first[at, part, :] = here + step * total

    def updated(source, weight, x0, count, part, onward, ends):
        result = [[] for _ in range(count)]
        above_flux = [None] * count
        for z in range(PLANES):
            base = z * HROWS + x0 + 1
            here = [source[base + i, part, :] for i in range(count + 2)]
            coefs = [weight[base + i, part, :] for i in range(count + 2)]
            along = [
                (coefs[i] + coefs[i + 1]) * (here[i + 1] - here[i]) for i in range(count + 1)
            ]
            for i in range(count):
                c, d = here[i + 1], coefs[i + 1]
                raw, back = onward[i][z]
                entering, leaving = ends[i][z]
                total = (along[i + 1] - along[i]) + (
                    jnp.where(lane == LANES - 1, leaving, raw)
                    - jnp.where(lane == 0, entering, back)
                )
                if z < PLANES - 1:
                    over = base + i + 1 + HROWS
                    flux = Z_WEIGHT * (
                        (d + weight[over, part, :]) * (source[over, part, :] - c)
                    )
                    total = total + flux
                if z > 0:
                    total = total - above_flux[i]
                if z < PLANES - 1:
                    above_flux[i] = flux
                result[i].append(c + step * total)
        return result

    def outer_row(source, weight, x, part):
        shift = -x % LANES
        onward, ends = [], []
        for z in range(PLANES):
            at = z * HROWS + x + 2
            raw = lane_flux(source[at, part, :], weight[at, part, :])
            onward.append((raw, pltpu.roll(raw, 1, 1)))
            ends.append(
                (
                    pltpu.roll(fluxes[z * 2, part, :], shift, 1),
                    pltpu.roll(fluxes[z * 2 + 1, part, :], (shift + LANES - 1) % LANES, 1),
                )
            )
        return updated(source, weight, x, 1, part, [onward], [ends])[0]

    def finish_rows(source, weight, group, part):
        x = group * GROUP
        onward, ends = [], []
        for i in range(GROUP):
            raws = [flux[z * HROWS + x + i + 2, part, :] for z in range(PLANES)]
            onward.append([(raw, pltpu.roll(raw, 1, 1)) for raw in raws])
            shift = (2 * LANES - 2 * (x + i)) & (LANES - 1)
            edges = [pltpu.roll(edge_flux[z, part, :], shift, 1) for z in range(PLANES)]
            ends.append([(edge, edge) for edge in edges])
        return updated(source, weight, x, GROUP, part, onward, ends)

    coefficients(strip_field, strip_coef, PLANES * 8, False)
    side_fluxes(strip_field, strip_coef)
    strip_update()
    for z in range(PLANES):
        for copy in fetch(z):
            copy.wait()
    halo = [z * HROWS + x for z in range(PLANES) for x in (0, 1, ROWS + 2, ROWS + 3)]
    for n in range(0, len(halo), CHUNK):
        at = halo[n : n + CHUNK]
        for i, value in zip(at, diffusivity([field[i] for i in at], inv_mass, table, live)):
            coef[i] = value

    for x in (-1, ROWS):
        for part in PARTS:
            for z, value in enumerate(outer_row(field, coef, x, part)):
                first[z * HROWS + x + 2, part, :] = value

    def first_rows(group, carry):
        for part in PARTS:
            for i, planes in enumerate(finish_rows(field, coef, group, part)):
                for z, value in enumerate(planes):
                    first[z * HROWS + group * GROUP + i + 2, part, :] = value
        return carry

    lax.fori_loop(0, ROWS // GROUP, first_rows, 0)
    for z in range(PLANES):
        first[z * HROWS] = field[z * HROWS]
        first[z * HROWS + HROWS - 1] = field[z * HROWS + HROWS - 1]
        for r in (0, 3, 4, 7):
            strip_first[z * 8 + r] = strip_field[z * 8 + r]
    coefficients(strip_first, strip_coef, PLANES * 8, False)
    side_fluxes(strip_first, strip_coef)
    coefficients(first, coef, PLANES * HROWS, True)

    def pack(group):
        for part in PARTS:
            for i in range(GROUP):
                planes = [spread[i * PLANES + z, part, :] for z in range(PLANES)]
                planes = swap_quarters(planes, lane)
                for j in range(4):
                    packed[j * ROWS + group * GROUP + i, part, :] = planes[j]

    def second_rows(group, carry):
        pack(jnp.maximum(group - 1, 0))
        for part in PARTS:
            for i, planes in enumerate(finish_rows(first, coef, group, part)):
                for z, value in enumerate(planes):
                    spread[i * PLANES + z, part, :] = value
        return carry

    for i in range(GROUP * PLANES):
        spread[i] = jnp.ones((SUB, LANES), f32)
    lax.fori_loop(0, ROWS // GROUP, second_rows, 0)
    pack(ROWS // GROUP - 1)

    log_table = log_table_ref[:, : 2 * SUB].astype(bf16)
    sum_table = sum_table_ref[:, : 2 * RPAD].astype(bf16)
    sub = lax.broadcasted_iota(jnp.int32, (8, LANES), 0)
    spare = sub >= SPECIES - 16
    mass = scales[1]
    heat = scales[2]
    sub24 = lax.broadcasted_iota(jnp.int32, (SUB, LANES), 0)

    def box(p, j, carry):
        base = j * ROWS + p * BOX

        def prepare(i, inner):
            row = packed[base + i]
            beginning = row * inv_mass
            start_ref[i] = beginning
            conc_ref[i] = beginning
            inverse = 1.0 / jnp.broadcast_to(row[SPECIES : SPECIES + 1, :], (8, LANES))
            high = coarse(inverse)
            ext_ref[i, :8, :] = jnp.where(
                sub == SPECIES - 16, high, jnp.where(sub == SPECIES - 15, inverse - high, 1.0)
            )
            ext_ref[i, 8:, :] = jnp.where(sub == SPECIES - 16, high, 1.0)
            return inner

        lax.fori_loop(0, BOX, prepare, 0, unroll=8)

        chunks = BOX // BOX_CHUNK

        def rates(chunk):
            at = [chunk * BOX_CHUNK + i for i in range(BOX_CHUNK)]
            conc = jnp.concatenate([conc_ref[i] for i in at], axis=1)
            spare_rows = jnp.concatenate([spare] * BOX_CHUNK, axis=1)
            ext = jnp.concatenate([ext_ref[i] for i in at], axis=1)
            logs = jnp.log2(conc)
            high = coarse(logs)
            low = logs - high
            stacked = jnp.concatenate(
                [
                    high[:16],
                    jnp.where(spare_rows, ext[:8], high[16:]),
                    low[:16],
                    jnp.where(spare_rows, ext[8:], low[16:]),
                ],
                axis=0,
            ).astype(bf16)
            return jnp.dot(log_table, stacked, preferred_element_type=f32)

        def advance(chunk, exponent):
            at = [chunk * BOX_CHUNK + i for i in range(BOX_CHUNK)]
            progress = jnp.exp2(exponent)
            high = coarse(progress)
            stacked = jnp.concatenate([high, progress - high], axis=0).astype(bf16)
            sums = jnp.dot(sum_table, stacked, preferred_element_type=f32)
            conc = jnp.concatenate([conc_ref[i] for i in at], axis=1)
            start = jnp.concatenate([start_ref[i] for i in at], axis=1)
            conc = (start + sums[:SUB, :]) * (conc / (conc + sums[SUB:, :]))
            for n, i in enumerate(at):
                conc_ref[i] = conc[:, n * LANES : (n + 1) * LANES]

        def sweep(number, inner):
            ahead = [rates(chunk) for chunk in range(AHEAD)]
            for chunk in range(chunks):
                if chunk + AHEAD < chunks:
                    ahead.append(rates(chunk + AHEAD))
                advance(chunk, ahead.pop(0))
            return inner

        lax.fori_loop(0, box_cost[p, j], sweep, 0)
        flag = flame_flag[p, j].astype(f32)

        def finish(i, inner):
            row = packed[base + i]
            advanced = conc_ref[i] * mass
            source = jnp.sum(heat * (advanced - row), axis=0, keepdims=True)
            temperature = row[SPECIES : SPECIES + 1, :] + flag * source
            packed[base + i] = jnp.where(
                sub24 == SPECIES, jnp.broadcast_to(temperature, (SUB, LANES)), advanced
            )
            return inner

        lax.fori_loop(0, BOX, finish, 0, unroll=8)
        return carry

    def give(x, carry):
        for part in PARTS:
            planes = swap_quarters([packed[j * ROWS + x, part, :] for j in range(4)], lane)
            for z in range(PLANES):
                out_rows[z, x, part, :] = planes[z]
        return carry

    for p in range(2):
        rows = pl.ds(p * BOX, BOX)
        lax.fori_loop(0, 4, functools.partial(box, p), 0)
        lax.fori_loop(p * BOX, (p + 1) * BOX, give, 0, unroll=4)
        for k in range(FIELDS):
            pltpu.make_async_copy(
                out_rows.at[:, rows, k], out.at[k, :, rows], out_sem.at[p]
            ).start()
    for p in range(2):
        whole = out.at[:, :, pl.ds(p * BOX, BOX)]
        pltpu.make_async_copy(whole, whole, out_sem.at[p]).wait()


def substep(box_cost, flame_flag, *operands):
    vmem = pl.BlockSpec(memory_space=pltpu.VMEM)
    smem = pl.BlockSpec(memory_space=pltpu.SMEM)
    hbm = pl.BlockSpec(memory_space=pl.ANY)
    rows = lambda n: pltpu.VMEM((n, SUB, LANES), f32)
    return pl.pallas_call(
        substep_kernel,
        in_specs=[smem, smem, hbm, hbm, hbm] + [vmem] * (len(operands) - 3),
        out_specs=[hbm, smem],
        out_shape=[
            jax.ShapeDtypeStruct((FIELDS, PLANES, ROWS, LANES), f32),
            jax.ShapeDtypeStruct((1, 1), f32),
        ],
        scratch_shapes=[
            rows(PLANES * HROWS),
            rows(PLANES * HROWS),
            rows(PLANES * HROWS),
            rows(32),
            rows(32),
            rows(32),
            rows(8),
            rows(4),
            rows(PLANES * HROWS),
            rows(GROUP * PLANES),
            rows(PLANES * ROWS),
            rows(BOX),
            rows(BOX),
            pltpu.VMEM((BOX, 16, LANES), f32),
            pltpu.VMEM((PLANES, ROWS, SUB, LANES), f32),
            pltpu.SemaphoreType.DMA((PLANES, 3)),
            pltpu.SemaphoreType.DMA((2,)),
        ],
        compiler_params=pltpu.CompilerParams(vmem_limit_bytes=VMEM_BYTES),
    )(box_cost, flame_flag, *operands)


def shifted(x, axis, by):
    count = lax.axis_size(axis)
    return lax.ppermute(x, axis, [(i, (i + by) % count) for i in range(count)])


def per_device(
    state,
    masses,
    reciprocals,
    rate_scale,
    energy,
    reactants,
    products,
    heat_release,
    box_cost,
    box_owner,
    flame_flag,
):
    field, low, high, own, *constants = edges(
        state.reshape(FIELDS, PLANES * ROWS, LANES),
        masses.reshape(1, -1),
        reciprocals,
        rate_scale.reshape(1, -1),
        energy.reshape(1, -1),
        reactants.T,
        products.T,
        heat_release.reshape(1, -1),
    )
    below = shifted(high, "gx", 1)
    above = shifted(low, "gx", -1)
    message, coef, flux = local_peak(box_cost, box_owner, field, constants[0], constants[1])
    own, to_left, to_right = corners(own, below, above)
    left = shifted(to_right, "gy", 1)
    right = shifted(to_left, "gy", -1)
    gathered = lax.all_to_all(message, ("gx", "gy"), 0, 0, tiled=True)
    return tuple(
        substep(
            box_cost,
            flame_flag,
            field,
            coef,
            flux,
            below,
            above,
            left,
            right,
            own,
            gathered,
            *constants,
        )
    )


def solution(mesh):
    split = P("gx", "gy")
    whole = P(None, None, "gx", "gy")
    return jax.shard_map(
        per_device,
        mesh=mesh,
        in_specs=(whole, P(), P(), P(), P(), P(), P(), P(), split, split, split),
        out_specs=(whole, split),
        check_vma=False,
    )
```

```python
import functools

import jax
import jax.numpy as jnp
from jax import lax
from jax.experimental import pallas as pl
from jax.experimental.pallas import tpu as pltpu
from jax.sharding import PartitionSpec as P

SPECIES = 21
FIELDS = 22
SUB = 24
LANES = 128
PLANES = 4
ROWS = 64
HROWS = ROWS + 4
BOX = 32
REACTIONS = 84
RPAD = 88
CHUNK = 4
BOX_CHUNK = 4
GROUP = 2
LONG = 16
AHEAD = 3
LOG2E = 1.4426950408889634
Z_WEIGHT = 0.25
CFL_SAFE = 0.5
HALF = 0.5
VMEM_BYTES = 56 * 1024 * 1024

PARTS = [slice(0, 8), slice(8, 16), slice(16, 24)]

f32 = jnp.float32
bf16 = jnp.bfloat16


def live_rows():
    return (lax.broadcasted_iota(jnp.int32, (SUB, LANES), 0) < SPECIES).astype(f32)


def fill_spare(rows, count):
    def body(i, carry):
        rows[i, FIELDS:SUB, :] = jnp.ones((SUB - FIELDS, LANES), f32)
        return carry

    lax.fori_loop(0, count, body, 0, unroll=8)


def coarse(x):
    return x.astype(bf16).astype(f32)


def diffusivity(rows, inv_mass, table, live):
    amounts = jnp.concatenate([row * inv_mass for row in rows], axis=1)
    high = coarse(amounts)
    low = amounts - high
    blank = jnp.zeros((8, amounts.shape[1]), f32)
    stacked = jnp.concatenate([high, low, high, blank], axis=0).astype(bf16)
    sums = jnp.dot(table, stacked, preferred_element_type=f32)
    result = []
    for i, row in enumerate(rows):
        lanes = slice(i * LANES, (i + 1) * LANES)
        heat = row[SPECIES : SPECIES + 1, :]
        scale = (HALF * heat * jnp.sqrt(heat)) * sums[SUB : SUB + 8, lanes]
        scale = jnp.concatenate([scale] * 3, axis=0)
        result.append(live * (1.0 - row) * scale / sums[:SUB, lanes])
    return result


def split3(x):
    high = coarse(x)
    middle = coarse(x - high)
    return high, middle, coarse((x - high) - middle)


def fill_tables(
    masses,
    reciprocals,
    rate_scale,
    energy,
    reactants,
    products,
    scales,
    table,
    log_table,
    sum_table,
    square,
):
    lane = lax.broadcasted_iota(jnp.int32, (LANES, LANES), 1)
    row = lax.broadcasted_iota(jnp.int32, (LANES, LANES), 0)

    def padded(value, filler=0.0):
        square[...] = jnp.full((LANES, LANES), filler, f32)
        square[: value.shape[0], : value.shape[1]] = value
        return square[...]

    def column(ref, filler):
        return jnp.broadcast_to(padded(ref[...], filler)[:1], (LANES, LANES)).T

    mass = column(masses, 1.0)[:SUB]
    scales[0] = 1.0 / mass
    scales[1] = mass

    cross = padded(reciprocals[...])
    cross = jnp.where(row == lane, 0.0, cross).T
    cross = jnp.where(lane < SPECIES, jnp.where(row < SPECIES, cross, 1.0), 0.0)[: SUB + 8]
    high = coarse(cross)
    table[...] = high + pltpu.roll(high, SUB, 1) + pltpu.roll(cross - high, 2 * SUB, 1)

    react_back = padded(reactants[...].astype(f32))
    react = react_back.T
    eh, em, _ = split3((-LOG2E) * column(energy, 0.0)[:RPAD])
    ah, am, al = split3(jnp.log2(column(rate_scale, 1.0)[:RPAD]))
    place = lane[:RPAD]
    ext = jnp.zeros((RPAD, LANES), f32)
    spare = (SPECIES, SPECIES + 1, SPECIES + 2)
    for n, value in zip(spare + tuple(SUB + n for n in spare), (eh, eh, ah, em, am, al)):
        ext = jnp.where(place == n, value, ext)
    log_table[...] = react[:RPAD] + pltpu.roll(react[:RPAD], SUB, 1) + ext

    make = padded(products[...].astype(f32))[:SUB]
    sums = HALF * jnp.concatenate([make, react_back[:SUB]], axis=0)
    moved = pltpu.roll(sums, RPAD, 1)
    place = lane[: 2 * SUB]
    sum_table[:, :LANES] = jnp.where(place < RPAD, sums, moved)
    sum_table[:, LANES:] = jnp.where(place < 2 * RPAD - LANES, moved, 0.0)


def edges_kernel(
    state,
    masses,
    reciprocals,
    rate_scale,
    energy,
    reactants,
    products,
    field_out,
    low,
    high,
    own,
    scales,
    table,
    log_table,
    sum_table,
    field,
    square,
    in_sem,
    out_sem,
):
    def half_rows(half):
        return pl.ds(half * 2 * ROWS, 2 * ROWS)

    def keep(half):
        rows = half_rows(half)
        return pltpu.make_async_copy(field.at[rows], field_out.at[rows], out_sem.at[half])

    for half in range(2):
        rows = half_rows(half)
        for k in range(FIELDS):
            pltpu.make_async_copy(state.at[k, rows], field.at[rows, k], in_sem.at[half]).start()
    fill_spare(field, PLANES * ROWS)
    fill_tables(
        masses,
        reciprocals,
        rate_scale,
        energy,
        reactants,
        products,
        scales,
        table,
        log_table,
        sum_table,
        square,
    )
    lane = lax.broadcasted_iota(jnp.int32, (8, LANES), 1)
    for half in range(2):
        whole = state.at[:, half_rows(half)]
        pltpu.make_async_copy(whole, whole, in_sem.at[half]).wait()
        keep(half).start()
        planes = (2 * half, 2 * half + 1)
        for z in planes:
            for layer in range(2):
                low[z * 2 + layer] = field[z * ROWS + layer]
                high[z * 2 + layer] = field[z * ROWS + ROWS - 2 + layer]

        def gather(index, held):
            mine = (lane >> 2) == index
            result = []
            for z in planes:
                for group in range(2):
                    for part in PARTS:
                        row = field[z * ROWS + group * 32 + index, part, :]
                        turned = pltpu.roll(row, 4 * index + 2, 1)
                        result.append(jnp.where(mine, turned, held[len(result)]))
            return tuple(result)

        held = lax.fori_loop(0, 32, gather, (jnp.ones((8, LANES), f32),) * 12, unroll=2)
        for i, z in enumerate(planes):
            for n, part in enumerate(PARTS):
                for c in range(4):
                    index = (4 * lane + c) & (LANES - 1)
                    pick = lambda v: jnp.take_along_axis(v, index, axis=1, mode="promise_in_bounds")
                    own[z * 4 + c, part, :] = jnp.where(
                        lane < 32, pick(held[i * 6 + n]), pick(held[i * 6 + 3 + n])
                    )
    for half in range(2):
        keep(half).wait()


def edges(*operands):
    vmem = pl.BlockSpec(memory_space=pltpu.VMEM)
    hbm = pl.BlockSpec(memory_space=pl.ANY)
    rows = lambda n: jax.ShapeDtypeStruct((n, SUB, LANES), f32)
    return pl.pallas_call(
        edges_kernel,
        in_specs=[hbm] + [vmem] * 6,
        out_specs=[hbm] + [vmem] * 7,
        out_shape=[
            rows(PLANES * ROWS),
            rows(8),
            rows(8),
            rows(16),
            rows(2),
            jax.ShapeDtypeStruct((SUB + 8, LANES), f32),
            jax.ShapeDtypeStruct((RPAD, LANES), f32),
            jax.ShapeDtypeStruct((2 * SUB, 2 * LANES), f32),
        ],
        scratch_shapes=[
            pltpu.VMEM((PLANES * ROWS, SUB, LANES), f32),
            pltpu.VMEM((LANES, LANES), f32),
            pltpu.SemaphoreType.DMA((2,)),
            pltpu.SemaphoreType.DMA((2,)),
        ],
        compiler_params=pltpu.CompilerParams(vmem_limit_bytes=VMEM_BYTES),
    )(*operands)


def lane_flux(row, weight):
    onward = LANES - 1
    return (weight + pltpu.roll(weight, onward, 1)) * (pltpu.roll(row, onward, 1) - row)


def coefficient_step(source, target, flux, base, inv_mass, table, live):
    if flux is not None:
        before = jnp.maximum(base - LONG, 0)
        for i in range(LONG):
            flux[before + i] = lane_flux(source[before + i], target[before + i])
    result = []
    for n in range(0, LONG, CHUNK):
        at = [base + n + i for i in range(CHUNK)]
        values = diffusivity([source[i] for i in at], inv_mass, table, live)
        for i, value in zip(at, values):
            target[i] = value
        result += values
    return result


def peak_kernel(
    box_cost,
    box_owner,
    field_in,
    scales,
    table_ref,
    message,
    coef_out,
    flux_out,
    field,
    coef,
    flux,
    in_sem,
    out_sem,
):
    quarter = lambda z: pl.ds(z * ROWS, ROWS)

    def fetch(z):
        return pltpu.make_async_copy(
            field_in.at[quarter(z)], field.at[quarter(z)], in_sem.at[z]
        )

    def keep(z):
        return [
            pltpu.make_async_copy(coef.at[quarter(z)], coef_out.at[quarter(z)], out_sem.at[z, 0]),
            pltpu.make_async_copy(flux.at[quarter(z)], flux_out.at[quarter(z)], out_sem.at[z, 1]),
        ]

    for z in range(PLANES):
        fetch(z).start()
    inv_mass = scales[0]
    live = live_rows()
    table = table_ref[:, : 3 * SUB + 8].astype(bf16)
    best = jnp.zeros((SUB, LANES), f32)
    for z in range(PLANES):
        fetch(z).wait()

        def body(index, best):
            at = [z * ROWS + index * CHUNK + i for i in range(CHUNK)]
            rows = [field[i] for i in at]
            for i, row, value in zip(at, rows, diffusivity(rows, inv_mass, table, live)):
                coef[i] = value
                flux[i] = lane_flux(row, value)
                best = jnp.maximum(best, value)
            return best

        best = lax.fori_loop(0, ROWS // CHUNK, body, best, unroll=4)
        for copy in keep(z):
            copy.start()
    top = 2.0 * jnp.max(best)
    device = lax.broadcasted_iota(jnp.int32, (LANES, LANES), 0)
    column = lax.broadcasted_iota(jnp.int32, (LANES, LANES), 1)
    count = lax.axis_size("gy")
    same = device // count == lax.axis_index("gx")
    place = device % count
    charged = jnp.zeros((LANES, LANES), f32)
    total = 0.0
    for p in range(2):
        for j in range(4):
            cost = box_cost[p, j].astype(f32)
            total = total + cost
            charged = charged + jnp.where(place == box_owner[p, j], cost, 0.0)
    tally = jnp.where(column == 1, charged, jnp.where(column == 2, total, 0.0))
    message[...] = jnp.where(column == 0, top, jnp.where(same, tally, 0.0))
    for z in range(PLANES):
        for copy in keep(z):
            copy.wait()


def local_peak(box_cost, box_owner, field, scales, table):
    vmem = pl.BlockSpec(memory_space=pltpu.VMEM)
    smem = pl.BlockSpec(memory_space=pltpu.SMEM)
    hbm = pl.BlockSpec(memory_space=pl.ANY)
    rows = jax.ShapeDtypeStruct((PLANES * ROWS, SUB, LANES), f32)
    devices = lax.axis_size("gx") * lax.axis_size("gy")
    assert devices == LANES or devices == 1
    return pl.pallas_call(
        peak_kernel,
        in_specs=[smem, smem, hbm, vmem, vmem],
        out_specs=[vmem, hbm, hbm],
        out_shape=[jax.ShapeDtypeStruct((LANES, LANES), f32), rows, rows],
        scratch_shapes=[
            pltpu.VMEM((PLANES * ROWS, SUB, LANES), f32),
            pltpu.VMEM((PLANES * ROWS, SUB, LANES), f32),
            pltpu.VMEM((PLANES * ROWS, SUB, LANES), f32),
            pltpu.SemaphoreType.DMA((PLANES,)),
            pltpu.SemaphoreType.DMA((PLANES, 2)),
        ],
        compiler_params=pltpu.CompilerParams(vmem_limit_bytes=VMEM_BYTES),
    )(box_cost, box_owner, field, scales, table)


def corners_kernel(own, below, above, _, whole, to_left, to_right):
    lane = lax.broadcasted_iota(jnp.int32, (8, LANES), 1)
    for z in range(PLANES):
        for part in PARTS:
            before = below[z * 2 + 1, part, :]
            after = above[z * 2, part, :]
            for c, column in enumerate((LANES - 2, LANES - 1, 0, 1)):
                value = jnp.where(
                    lane == LANES - 1,
                    pltpu.roll(before, LANES - 1 - column, 1),
                    jnp.where(
                        lane == ROWS,
                        pltpu.roll(after, (ROWS - column) % LANES, 1),
                        own[z * 4 + c, part, :],
                    ),
                )
                whole[z * 4 + c, part, :] = value
                if c < 2:
                    to_right[z * 2 + c, part, :] = value
                else:
                    to_left[z * 2 + c - 2, part, :] = value


def corners(own, below, above, message):
    rows = lambda n: jax.ShapeDtypeStruct((n, SUB, LANES), f32)
    vmem = pl.BlockSpec(memory_space=pltpu.VMEM)
    return pl.pallas_call(
        corners_kernel,
        in_specs=[vmem, vmem, vmem, pl.BlockSpec(memory_space=pl.ANY)],
        out_shape=[rows(16), rows(8), rows(8)],
        compiler_params=pltpu.CompilerParams(vmem_limit_bytes=VMEM_BYTES),
    )(own, below, above, message)


def swap_quarters(planes, lane):
    low_half = lane < 64
    even = ((lane >> 5) & 1) == 0
    a, b, c, d = planes
    a, c = (
        jnp.where(low_half, a, pltpu.roll(c, 64, 1)),
        jnp.where(low_half, pltpu.roll(a, 64, 1), c),
    )
    b, d = (
        jnp.where(low_half, b, pltpu.roll(d, 64, 1)),
        jnp.where(low_half, pltpu.roll(b, 64, 1), d),
    )
    a, b = (
        jnp.where(even, a, pltpu.roll(b, 32, 1)),
        jnp.where(even, pltpu.roll(a, 96, 1), b),
    )
    c, d = (
        jnp.where(even, c, pltpu.roll(d, 32, 1)),
        jnp.where(even, pltpu.roll(c, 96, 1), d),
    )
    return [a, b, c, d]


def substep_kernel(
    box_cost,
    flame_flag,
    field_in,
    coef_in,
    flux_in,
    below,
    above,
    left,
    right,
    own,
    gathered,
    scales,
    table_ref,
    log_table_ref,
    sum_table_ref,
    out,
    load_out,
    field,
    coef,
    first,
    strip_field,
    strip_coef,
    strip_first,
    fluxes,
    edge_flux,
    flux,
    spread,
    packed,
    start_ref,
    conc_ref,
    ext_ref,
    out_rows,
    in_sem,
    out_sem,
):
    def fetch(z):
        held, rows = pl.ds(z * ROWS, ROWS), pl.ds(z * HROWS + 2, ROWS)
        return [
            pltpu.make_async_copy(field_in.at[held], field.at[rows], in_sem.at[z, 0]),
            pltpu.make_async_copy(coef_in.at[held], coef.at[rows], in_sem.at[z, 1]),
            pltpu.make_async_copy(flux_in.at[held], flux.at[rows], in_sem.at[z, 2]),
        ]

    for z in range(PLANES):
        for copy in fetch(z):
            copy.start()
    inv_mass = scales[0]
    live = live_rows()
    table = table_ref[:, : 3 * SUB + 8].astype(bf16)
    lane = lax.broadcasted_iota(jnp.int32, (8, LANES), 1)
    received = gathered[...]
    columns = lax.broadcasted_iota(jnp.int32, received.shape, 1)
    peak = jnp.max(jnp.where(columns == 0, received, 0.0), keepdims=True)
    step = CFL_SAFE / ((4.0 + 2.0 * Z_WEIGHT) * peak)
    mine = jnp.sum(jnp.where(columns == 1, received, 0.0))
    everyone = jnp.sum(jnp.where(columns == 2, received, 0.0))
    load_out[0, 0] = mine / (everyone / 16.0)
    step = jnp.broadcast_to(step, (8, LANES))

    for z in range(PLANES):
        for layer in range(2):
            field[z * HROWS + layer] = below[z * 2 + layer]
            field[z * HROWS + ROWS + 2 + layer] = above[z * 2 + layer]
        for c in range(2):
            strip_field[z * 8 + c] = left[z * 2 + c]
            strip_field[z * 8 + 2 + c] = own[z * 4 + 2 + c]
            strip_field[z * 8 + 4 + c] = own[z * 4 + c]
            strip_field[z * 8 + 6 + c] = right[z * 2 + c]

    def coefficients(source, target, count, kept):
        def body(index, carry):
            coefficient_step(source, target, kept, index * LONG, inv_mass, table, live)
            return carry

        lax.fori_loop(0, count // LONG, body, 0)
        if kept is not None:
            for i in range(count - LONG, count):
                kept[i] = lane_flux(source[i], target[i])

    def face(source, weight, here, there, part):
        return (weight[here, part, :] + weight[there, part, :]) * (
            source[there, part, :] - source[here, part, :]
        )

    odd = (lane & 1) == 1

    def side_fluxes(source, weight):
        even_from = lane >> 1
        odd_from = ((lane + 1) >> 1) & (ROWS - 1)
        for z in range(PLANES):
            for part in PARTS:
                entering = face(source, weight, z * 8 + 1, z * 8 + 2, part)
                leaving = face(source, weight, z * 8 + 5, z * 8 + 6, part)
                fluxes[z * 2, part, :] = entering
                fluxes[z * 2 + 1, part, :] = leaving
                pick = lambda v, at: jnp.take_along_axis(v, at, axis=1, mode="promise_in_bounds")
                edge_flux[z, part, :] = jnp.where(
                    odd, pick(leaving, odd_from), pick(entering, even_from)
                )

    def strip_update():
        for r in (1, 2, 5, 6):
            for part in PARTS:
                above_flux = None
                for z in range(PLANES):
                    at = z * 8 + r
                    here = strip_field[at, part, :]
                    weight = strip_coef[at, part, :]
                    total = face(strip_field, strip_coef, at, at + 1, part)
                    total = total - face(strip_field, strip_coef, at - 1, at, part)
                    onward = (weight + pltpu.roll(weight, LANES - 1, 1)) * (
                        pltpu.roll(here, LANES - 1, 1) - here
                    )
                    total = total + (onward - pltpu.roll(onward, 1, 1))
                    if above_flux is not None:
                        total = total - Z_WEIGHT * above_flux
                    if z < PLANES - 1:
                        above_flux = face(strip_field, strip_coef, at, at + 8, part)
                        total = total + Z_WEIGHT * above_flux
                    strip_first[at, part, :] = here + step * total

    def updated(source, weight, x0, count, part, onward, ends):
        result = [[] for _ in range(count)]
        above_flux = [None] * count
        for z in range(PLANES):
            base = z * HROWS + x0 + 1
            here = [source[base + i, part, :] for i in range(count + 2)]
            coefs = [weight[base + i, part, :] for i in range(count + 2)]
            along = [
                (coefs[i] + coefs[i + 1]) * (here[i + 1] - here[i]) for i in range(count + 1)
            ]
            for i in range(count):
                c, d = here[i + 1], coefs[i + 1]
                raw, back = onward[i][z]
                entering, leaving = ends[i][z]
                total = (along[i + 1] - along[i]) + (
                    jnp.where(lane == LANES - 1, leaving, raw)
                    - jnp.where(lane == 0, entering, back)
                )
                if z < PLANES - 1:
                    over = base + i + 1 + HROWS
                    flux = Z_WEIGHT * (
                        (d + weight[over, part, :]) * (source[over, part, :] - c)
                    )
                    total = total + flux
                if z > 0:
                    total = total - above_flux[i]
                if z < PLANES - 1:
                    above_flux[i] = flux
                result[i].append(c + step * total)
        return result

    def outer_row(source, weight, x, part):
        shift = -x % LANES
        onward, ends = [], []
        for z in range(PLANES):
            at = z * HROWS + x + 2
            raw = lane_flux(source[at, part, :], weight[at, part, :])
            onward.append((raw, pltpu.roll(raw, 1, 1)))
            ends.append(
                (
                    pltpu.roll(fluxes[z * 2, part, :], shift, 1),
                    pltpu.roll(fluxes[z * 2 + 1, part, :], (shift + LANES - 1) % LANES, 1),
                )
            )
        return updated(source, weight, x, 1, part, [onward], [ends])[0]

    def finish_rows(source, weight, group, part):
        x = group * GROUP
        onward, ends = [], []
        for i in range(GROUP):
            raws = [flux[z * HROWS + x + i + 2, part, :] for z in range(PLANES)]
            onward.append([(raw, pltpu.roll(raw, 1, 1)) for raw in raws])
            shift = (2 * LANES - 2 * (x + i)) & (LANES - 1)
            edges = [pltpu.roll(edge_flux[z, part, :], shift, 1) for z in range(PLANES)]
            ends.append([(edge, edge) for edge in edges])
        return updated(source, weight, x, GROUP, part, onward, ends)

    coefficients(strip_field, strip_coef, PLANES * 8, None)
    side_fluxes(strip_field, strip_coef)
    strip_update()
    for z in range(PLANES):
        for copy in fetch(z):
            copy.wait()
    halo = [z * HROWS + x for z in range(PLANES) for x in (0, 1, ROWS + 2, ROWS + 3)]
    for n in range(0, len(halo), CHUNK):
        at = halo[n : n + CHUNK]
        for i, value in zip(at, diffusivity([field[i] for i in at], inv_mass, table, live)):
            coef[i] = value

    for x in (-1, ROWS):
        for part in PARTS:
            for z, value in enumerate(outer_row(field, coef, x, part)):
                first[z * HROWS + x + 2, part, :] = value

    def first_rows(group, carry):
        for part in PARTS:
            for i, planes in enumerate(finish_rows(field, coef, group, part)):
                for z, value in enumerate(planes):
                    first[z * HROWS + group * GROUP + i + 2, part, :] = value
        return carry

    lax.fori_loop(0, ROWS // GROUP, first_rows, 0)
    for z in range(PLANES):
        first[z * HROWS] = field[z * HROWS]
        first[z * HROWS + HROWS - 1] = field[z * HROWS + HROWS - 1]
        for r in (0, 3, 4, 7):
            strip_first[z * 8 + r] = strip_field[z * 8 + r]
    coefficients(strip_first, strip_coef, PLANES * 8, None)
    side_fluxes(strip_first, strip_coef)
    coefficients(first, coef, PLANES * HROWS, flux)

    def pack(group):
        for part in PARTS:
            for i in range(GROUP):
                planes = [spread[i * PLANES + z, part, :] for z in range(PLANES)]
                planes = swap_quarters(planes, lane)
                for j in range(4):
                    packed[j * ROWS + group * GROUP + i, part, :] = planes[j]

    def second_rows(group, carry):
        pack(jnp.maximum(group - 1, 0))
        for part in PARTS:
            for i, planes in enumerate(finish_rows(first, coef, group, part)):
                for z, value in enumerate(planes):
                    spread[i * PLANES + z, part, :] = value
        return carry

    for i in range(GROUP * PLANES):
        spread[i] = jnp.ones((SUB, LANES), f32)
    lax.fori_loop(0, ROWS // GROUP, second_rows, 0)
    pack(ROWS // GROUP - 1)

    log_table = log_table_ref[:, : 2 * SUB].astype(bf16)
    sum_table = sum_table_ref[:, : 2 * RPAD].astype(bf16)
    sub = lax.broadcasted_iota(jnp.int32, (8, LANES), 0)
    spare = sub >= SPECIES - 16
    mass = scales[1]
    heat = scales[2]
    sub24 = lax.broadcasted_iota(jnp.int32, (SUB, LANES), 0)

    def box(p, j, carry):
        base = j * ROWS + p * BOX

        def prepare(i, inner):
            row = packed[base + i]
            beginning = row * inv_mass
            start_ref[i] = beginning
            conc_ref[i] = beginning
            inverse = 1.0 / jnp.broadcast_to(row[SPECIES : SPECIES + 1, :], (8, LANES))
            high = coarse(inverse)
            ext_ref[i, :8, :] = jnp.where(
                sub == SPECIES - 16, high, jnp.where(sub == SPECIES - 15, inverse - high, 1.0)
            )
            ext_ref[i, 8:, :] = jnp.where(sub == SPECIES - 16, high, 1.0)
            return inner

        lax.fori_loop(0, BOX, prepare, 0, unroll=8)

        chunks = BOX // BOX_CHUNK

        def rates(chunk):
            at = [chunk * BOX_CHUNK + i for i in range(BOX_CHUNK)]
            conc = jnp.concatenate([conc_ref[i] for i in at], axis=1)
            spare_rows = jnp.concatenate([spare] * BOX_CHUNK, axis=1)
            ext = jnp.concatenate([ext_ref[i] for i in at], axis=1)
            logs = jnp.log2(conc)
            high = coarse(logs)
            low = logs - high
            stacked = jnp.concatenate(
                [
                    high[:16],
                    jnp.where(spare_rows, ext[:8], high[16:]),
                    low[:16],
                    jnp.where(spare_rows, ext[8:], low[16:]),
                ],
                axis=0,
            ).astype(bf16)
            return jnp.dot(log_table, stacked, preferred_element_type=f32)

        def advance(chunk, exponent):
            at = [chunk * BOX_CHUNK + i for i in range(BOX_CHUNK)]
            progress = jnp.exp2(exponent)
            high = coarse(progress)
            stacked = jnp.concatenate([high, progress - high], axis=0).astype(bf16)
            sums = jnp.dot(sum_table, stacked, preferred_element_type=f32)
            conc = jnp.concatenate([conc_ref[i] for i in at], axis=1)
            start = jnp.concatenate([start_ref[i] for i in at], axis=1)
            conc = (start + sums[:SUB, :]) * (conc / (conc + sums[SUB:, :]))
            for n, i in enumerate(at):
                conc_ref[i] = conc[:, n * LANES : (n + 1) * LANES]

        def sweep(number, inner):
            ahead = [rates(chunk) for chunk in range(AHEAD)]
            for chunk in range(chunks):
                if chunk + AHEAD < chunks:
                    ahead.append(rates(chunk + AHEAD))
                advance(chunk, ahead.pop(0))
            return inner

        lax.fori_loop(0, box_cost[p, j], sweep, 0)
        flag = flame_flag[p, j].astype(f32)

        def finish(i, inner):
            row = packed[base + i]
            advanced = conc_ref[i] * mass
            source = jnp.sum(heat * (advanced - row), axis=0, keepdims=True)
            temperature = row[SPECIES : SPECIES + 1, :] + flag * source
            packed[base + i] = jnp.where(
                sub24 == SPECIES, jnp.broadcast_to(temperature, (SUB, LANES)), advanced
            )
            return inner

        lax.fori_loop(0, BOX, finish, 0, unroll=8)
        return carry

    def give(x, carry):
        for part in PARTS:
            planes = swap_quarters([packed[j * ROWS + x, part, :] for j in range(4)], lane)
            for z in range(PLANES):
                out_rows[z, x, part, :] = planes[z]
        return carry

    for p in range(2):
        rows = pl.ds(p * BOX, BOX)
        lax.fori_loop(0, 4, functools.partial(box, p), 0)
        lax.fori_loop(p * BOX, (p + 1) * BOX, give, 0, unroll=4)
        for k in range(FIELDS):
            pltpu.make_async_copy(
                out_rows.at[:, rows, k], out.at[k, :, rows], out_sem.at[p]
            ).start()
    for p in range(2):
        whole = out.at[:, :, pl.ds(p * BOX, BOX)]
        pltpu.make_async_copy(whole, whole, out_sem.at[p]).wait()


def substep(box_cost, flame_flag, *operands):
    vmem = pl.BlockSpec(memory_space=pltpu.VMEM)
    smem = pl.BlockSpec(memory_space=pltpu.SMEM)
    hbm = pl.BlockSpec(memory_space=pl.ANY)
    rows = lambda n: pltpu.VMEM((n, SUB, LANES), f32)
    return pl.pallas_call(
        substep_kernel,
        in_specs=[smem, smem, hbm, hbm, hbm] + [vmem] * (len(operands) - 3),
        out_specs=[hbm, smem],
        out_shape=[
            jax.ShapeDtypeStruct((FIELDS, PLANES, ROWS, LANES), f32),
            jax.ShapeDtypeStruct((1, 1), f32),
        ],
        scratch_shapes=[
            rows(PLANES * HROWS),
            rows(PLANES * HROWS),
            rows(PLANES * HROWS),
            rows(32),
            rows(32),
            rows(32),
            rows(8),
            rows(4),
            rows(PLANES * HROWS),
            rows(GROUP * PLANES),
            rows(PLANES * ROWS),
            rows(BOX),
            rows(BOX),
            pltpu.VMEM((BOX, 16, LANES), f32),
            pltpu.VMEM((PLANES, ROWS, SUB, LANES), f32),
            pltpu.SemaphoreType.DMA((PLANES, 3)),
            pltpu.SemaphoreType.DMA((2,)),
        ],
        compiler_params=pltpu.CompilerParams(vmem_limit_bytes=VMEM_BYTES),
    )(box_cost, flame_flag, *operands)


def shifted(x, axis, by):
    count = lax.axis_size(axis)
    return lax.ppermute(x, axis, [(i, (i + by) % count) for i in range(count)])


def per_device(
    state,
    masses,
    reciprocals,
    rate_scale,
    energy,
    reactants,
    products,
    heat_release,
    box_cost,
    box_owner,
    flame_flag,
):
    field, low, high, own, *constants = edges(
        state.reshape(FIELDS, PLANES * ROWS, LANES),
        masses.reshape(1, -1),
        reciprocals,
        rate_scale.reshape(1, -1),
        energy.reshape(1, -1),
        reactants.T,
        products.T,
    )
    below = shifted(high, "gx", 1)
    above = shifted(low, "gx", -1)
    message, coef, flux = local_peak(box_cost, box_owner, field, constants[0], constants[1])
    own, to_left, to_right = corners(own, below, above, message)
    left = shifted(to_right, "gy", 1)
    right = shifted(to_left, "gy", -1)
    gathered = lax.all_to_all(message, ("gx", "gy"), 0, 0, tiled=True)
    heat = jnp.pad(heat_release, (0, SUB - SPECIES))[:, None]
    heat = jnp.broadcast_to(heat, (1, SUB, LANES))
    constants[0] = jnp.concatenate([constants[0], heat], axis=0)
    return tuple(
        substep(
            box_cost,
            flame_flag,
            field,
            coef,
            flux,
            below,
            above,
            left,
            right,
            own,
            gathered,
            *constants,
        )
    )


def solution(mesh):
    split = P("gx", "gy")
    whole = P(None, None, "gx", "gy")
    return jax.shard_map(
        per_device,
        mesh=mesh,
        in_specs=(whole, P(), P(), P(), P(), P(), P(), P(), split, split, split),
        out_specs=(whole, split),
        check_vma=False,
    )
```

```python
import functools

import jax
import jax.numpy as jnp
from jax import lax
from jax.experimental import pallas as pl
from jax.experimental.pallas import tpu as pltpu
from jax.sharding import PartitionSpec as P

SPECIES = 21
FIELDS = 22
SUB = 24
LANES = 128
PLANES = 4
ROWS = 64
HROWS = ROWS + 4
BOX = 32
REACTIONS = 84
RPAD = 88
CHUNK = 4
BOX_CHUNK = 4
GROUP = 2
LONG = 16
AHEAD = 3
LOG2E = 1.4426950408889634
Z_WEIGHT = 0.25
CFL_SAFE = 0.5
HALF = 0.5
VMEM_BYTES = 56 * 1024 * 1024

PARTS = [slice(0, 8), slice(8, 16), slice(16, 24)]

f32 = jnp.float32
bf16 = jnp.bfloat16


def live_rows():
    return (lax.broadcasted_iota(jnp.int32, (SUB, LANES), 0) < SPECIES).astype(f32)


def fill_spare(rows, count):
    def body(i, carry):
        rows[i, FIELDS:SUB, :] = jnp.ones((SUB - FIELDS, LANES), f32)
        return carry

    lax.fori_loop(0, count, body, 0, unroll=8)


def coarse(x):
    return x.astype(bf16).astype(f32)


def diffusivity(rows, inv_mass, table, live):
    amounts = jnp.concatenate([row * inv_mass for row in rows], axis=1)
    high = coarse(amounts)
    low = amounts - high
    blank = jnp.zeros((8, amounts.shape[1]), f32)
    stacked = jnp.concatenate([high, low, high, blank], axis=0).astype(bf16)
    sums = jnp.dot(table, stacked, preferred_element_type=f32)
    result = []
    for i, row in enumerate(rows):
        lanes = slice(i * LANES, (i + 1) * LANES)
        heat = row[SPECIES : SPECIES + 1, :]
        scale = (HALF * heat * jnp.sqrt(heat)) * sums[SUB : SUB + 8, lanes]
        scale = jnp.concatenate([scale] * 3, axis=0)
        result.append(live * (1.0 - row) * scale / sums[:SUB, lanes])
    return result


def split3(x):
    high = coarse(x)
    middle = coarse(x - high)
    return high, middle, coarse((x - high) - middle)


def fill_tables(
    masses,
    reciprocals,
    rate_scale,
    energy,
    reactants,
    products,
    scales,
    table,
    log_table,
    sum_table,
    square,
):
    lane = lax.broadcasted_iota(jnp.int32, (LANES, LANES), 1)
    row = lax.broadcasted_iota(jnp.int32, (LANES, LANES), 0)

    def padded(value, filler=0.0):
        square[...] = jnp.full((LANES, LANES), filler, f32)
        square[: value.shape[0], : value.shape[1]] = value
        return square[...]

    def column(ref, filler):
        return jnp.broadcast_to(padded(ref[...], filler)[:1], (LANES, LANES)).T

    mass = column(masses, 1.0)[:SUB]
    scales[0] = 1.0 / mass
    scales[1] = mass

    cross = padded(reciprocals[...])
    cross = jnp.where(row == lane, 0.0, cross).T
    cross = jnp.where(lane < SPECIES, jnp.where(row < SPECIES, cross, 1.0), 0.0)[: SUB + 8]
    high = coarse(cross)
    table[...] = high + pltpu.roll(high, SUB, 1) + pltpu.roll(cross - high, 2 * SUB, 1)

    react_back = padded(reactants[...].astype(f32))
    react = react_back.T
    eh, em, _ = split3((-LOG2E) * column(energy, 0.0)[:RPAD])
    ah, am, al = split3(jnp.log2(column(rate_scale, 1.0)[:RPAD]))
    place = lane[:RPAD]
    ext = jnp.zeros((RPAD, LANES), f32)
    spare = (SPECIES, SPECIES + 1, SPECIES + 2)
    for n, value in zip(spare + tuple(SUB + n for n in spare), (eh, eh, ah, em, am, al)):
        ext = jnp.where(place == n, value, ext)
    log_table[...] = react[:RPAD] + pltpu.roll(react[:RPAD], SUB, 1) + ext

    make = padded(products[...].astype(f32))[:SUB]
    sums = HALF * jnp.concatenate([make, react_back[:SUB]], axis=0)
    moved = pltpu.roll(sums, RPAD, 1)
    place = lane[: 2 * SUB]
    sum_table[:, :LANES] = jnp.where(place < RPAD, sums, moved)
    sum_table[:, LANES:] = jnp.where(place < 2 * RPAD - LANES, moved, 0.0)


def edges_kernel(
    state,
    masses,
    reciprocals,
    rate_scale,
    energy,
    reactants,
    products,
    field_out,
    low,
    high,
    own,
    scales,
    table,
    log_table,
    sum_table,
    field,
    square,
    in_sem,
    out_sem,
):
    def half_rows(half):
        return pl.ds(half * 2 * ROWS, 2 * ROWS)

    def keep(half):
        rows = half_rows(half)
        return pltpu.make_async_copy(field.at[rows], field_out.at[rows], out_sem.at[half])

    for half in range(2):
        rows = half_rows(half)
        for k in range(FIELDS):
            pltpu.make_async_copy(state.at[k, rows], field.at[rows, k], in_sem.at[half]).start()
    fill_spare(field, PLANES * ROWS)
    fill_tables(
        masses,
        reciprocals,
        rate_scale,
        energy,
        reactants,
        products,
        scales,
        table,
        log_table,
        sum_table,
        square,
    )
    lane = lax.broadcasted_iota(jnp.int32, (8, LANES), 1)
    for half in range(2):
        whole = state.at[:, half_rows(half)]
        pltpu.make_async_copy(whole, whole, in_sem.at[half]).wait()
        keep(half).start()
        planes = (2 * half, 2 * half + 1)
        for z in planes:
            for layer in range(2):
                low[z * 2 + layer] = field[z * ROWS + layer]
                high[z * 2 + layer] = field[z * ROWS + ROWS - 2 + layer]

        def gather(index, held):
            mine = (lane >> 2) == index
            result = []
            for z in planes:
                for group in range(2):
                    for part in PARTS:
                        row = field[z * ROWS + group * 32 + index, part, :]
                        turned = pltpu.roll(row, 4 * index + 2, 1)
                        result.append(jnp.where(mine, turned, held[len(result)]))
            return tuple(result)

        held = lax.fori_loop(0, 32, gather, (jnp.ones((8, LANES), f32),) * 12, unroll=2)
        for i, z in enumerate(planes):
            for n, part in enumerate(PARTS):
                for c in range(4):
                    index = (4 * lane + c) & (LANES - 1)
                    pick = lambda v: jnp.take_along_axis(v, index, axis=1, mode="promise_in_bounds")
                    own[z * 4 + c, part, :] = jnp.where(
                        lane < 32, pick(held[i * 6 + n]), pick(held[i * 6 + 3 + n])
                    )
    for half in range(2):
        keep(half).wait()


def edges(*operands):
    vmem = pl.BlockSpec(memory_space=pltpu.VMEM)
    hbm = pl.BlockSpec(memory_space=pl.ANY)
    rows = lambda n: jax.ShapeDtypeStruct((n, SUB, LANES), f32)
    return pl.pallas_call(
        edges_kernel,
        in_specs=[hbm] + [vmem] * 6,
        out_specs=[hbm] + [vmem] * 7,
        out_shape=[
            rows(PLANES * ROWS),
            rows(8),
            rows(8),
            rows(16),
            rows(2),
            jax.ShapeDtypeStruct((SUB + 8, LANES), f32),
            jax.ShapeDtypeStruct((RPAD, LANES), f32),
            jax.ShapeDtypeStruct((2 * SUB, 2 * LANES), f32),
        ],
        scratch_shapes=[
            pltpu.VMEM((PLANES * ROWS, SUB, LANES), f32),
            pltpu.VMEM((LANES, LANES), f32),
            pltpu.SemaphoreType.DMA((2,)),
            pltpu.SemaphoreType.DMA((2,)),
        ],
        compiler_params=pltpu.CompilerParams(vmem_limit_bytes=VMEM_BYTES),
    )(*operands)


def lane_flux(row, weight):
    onward = LANES - 1
    return (weight + pltpu.roll(weight, onward, 1)) * (pltpu.roll(row, onward, 1) - row)


def coefficient_step(source, target, flux, base, inv_mass, table, live):
    if flux is not None:
        before = jnp.maximum(base - LONG, 0)
        for i in range(LONG):
            flux[before + i] = lane_flux(source[before + i], target[before + i])
    result = []
    for n in range(0, LONG, CHUNK):
        at = [base + n + i for i in range(CHUNK)]
        values = diffusivity([source[i] for i in at], inv_mass, table, live)
        for i, value in zip(at, values):
            target[i] = value
        result += values
    return result


def peak_kernel(
    box_cost,
    box_owner,
    field_in,
    scales,
    table_ref,
    message,
    coef_out,
    flux_out,
    field,
    coef,
    flux,
    in_sem,
    out_sem,
):
    quarter = lambda z: pl.ds(z * ROWS, ROWS)

    def fetch(z):
        return pltpu.make_async_copy(
            field_in.at[quarter(z)], field.at[quarter(z)], in_sem.at[z]
        )

    def keep(z):
        return [
            pltpu.make_async_copy(coef.at[quarter(z)], coef_out.at[quarter(z)], out_sem.at[z, 0]),
            pltpu.make_async_copy(flux.at[quarter(z)], flux_out.at[quarter(z)], out_sem.at[z, 1]),
        ]

    for z in range(PLANES):
        fetch(z).start()
    inv_mass = scales[0]
    live = live_rows()
    table = table_ref[:, : 3 * SUB + 8].astype(bf16)
    best = jnp.zeros((SUB, LANES), f32)
    for z in range(PLANES):
        fetch(z).wait()

        def body(index, best):
            at = [z * ROWS + index * CHUNK + i for i in range(CHUNK)]
            rows = [field[i] for i in at]
            for i, row, value in zip(at, rows, diffusivity(rows, inv_mass, table, live)):
                coef[i] = value
                flux[i] = lane_flux(row, value)
                best = jnp.maximum(best, value)
            return best

        best = lax.fori_loop(0, ROWS // CHUNK, body, best, unroll=4)
        for copy in keep(z):
            copy.start()
    top = 2.0 * jnp.max(best)
    device = lax.broadcasted_iota(jnp.int32, (LANES, LANES), 0)
    column = lax.broadcasted_iota(jnp.int32, (LANES, LANES), 1)
    count = lax.axis_size("gy")
    same = device // count == lax.axis_index("gx")
    place = device % count
    charged = jnp.zeros((LANES, LANES), f32)
    total = 0.0
    for p in range(2):
        for j in range(4):
            cost = box_cost[p, j].astype(f32)
            total = total + cost
            charged = charged + jnp.where(place == box_owner[p, j], cost, 0.0)
    tally = jnp.where(column == 1, charged, jnp.where(column == 2, total, 0.0))
    message[...] = jnp.where(column == 0, top, jnp.where(same, tally, 0.0))
    for z in range(PLANES):
        for copy in keep(z):
            copy.wait()


def local_peak(box_cost, box_owner, field, scales, table):
    vmem = pl.BlockSpec(memory_space=pltpu.VMEM)
    smem = pl.BlockSpec(memory_space=pltpu.SMEM)
    hbm = pl.BlockSpec(memory_space=pl.ANY)
    rows = jax.ShapeDtypeStruct((PLANES * ROWS, SUB, LANES), f32)
    devices = lax.axis_size("gx") * lax.axis_size("gy")
    assert devices == LANES or devices == 1
    return pl.pallas_call(
        peak_kernel,
        in_specs=[smem, smem, hbm, vmem, vmem],
        out_specs=[vmem, hbm, hbm],
        out_shape=[jax.ShapeDtypeStruct((LANES, LANES), f32), rows, rows],
        scratch_shapes=[
            pltpu.VMEM((PLANES * ROWS, SUB, LANES), f32),
            pltpu.VMEM((PLANES * ROWS, SUB, LANES), f32),
            pltpu.VMEM((PLANES * ROWS, SUB, LANES), f32),
            pltpu.SemaphoreType.DMA((PLANES,)),
            pltpu.SemaphoreType.DMA((PLANES, 2)),
        ],
        compiler_params=pltpu.CompilerParams(vmem_limit_bytes=VMEM_BYTES),
    )(box_cost, box_owner, field, scales, table)


def corners_kernel(own, below, above, _, whole, to_left, to_right):
    lane = lax.broadcasted_iota(jnp.int32, (8, LANES), 1)
    for z in range(PLANES):
        for part in PARTS:
            before = below[z * 2 + 1, part, :]
            after = above[z * 2, part, :]
            for c, column in enumerate((LANES - 2, LANES - 1, 0, 1)):
                value = jnp.where(
                    lane == LANES - 1,
                    pltpu.roll(before, LANES - 1 - column, 1),
                    jnp.where(
                        lane == ROWS,
                        pltpu.roll(after, (ROWS - column) % LANES, 1),
                        own[z * 4 + c, part, :],
                    ),
                )
                whole[z * 4 + c, part, :] = value
                if c < 2:
                    to_right[z * 2 + c, part, :] = value
                else:
                    to_left[z * 2 + c - 2, part, :] = value


def corners(own, below, above, message):
    rows = lambda n: jax.ShapeDtypeStruct((n, SUB, LANES), f32)
    vmem = pl.BlockSpec(memory_space=pltpu.VMEM)
    return pl.pallas_call(
        corners_kernel,
        in_specs=[vmem, vmem, vmem, pl.BlockSpec(memory_space=pl.ANY)],
        out_shape=[rows(16), rows(8), rows(8)],
        compiler_params=pltpu.CompilerParams(vmem_limit_bytes=VMEM_BYTES),
    )(own, below, above, message)


def swap_quarters(planes, lane):
    low_half = lane < 64
    even = ((lane >> 5) & 1) == 0
    a, b, c, d = planes
    a, c = (
        jnp.where(low_half, a, pltpu.roll(c, 64, 1)),
        jnp.where(low_half, pltpu.roll(a, 64, 1), c),
    )
    b, d = (
        jnp.where(low_half, b, pltpu.roll(d, 64, 1)),
        jnp.where(low_half, pltpu.roll(b, 64, 1), d),
    )
    a, b = (
        jnp.where(even, a, pltpu.roll(b, 32, 1)),
        jnp.where(even, pltpu.roll(a, 96, 1), b),
    )
    c, d = (
        jnp.where(even, c, pltpu.roll(d, 32, 1)),
        jnp.where(even, pltpu.roll(c, 96, 1), d),
    )
    return [a, b, c, d]


def substep_kernel(
    box_cost,
    flame_flag,
    field_in,
    coef_in,
    flux_in,
    below,
    above,
    left,
    right,
    own,
    gathered,
    scales,
    table_ref,
    log_table_ref,
    sum_table_ref,
    out,
    load_out,
    field,
    coef,
    first,
    strip_field,
    strip_coef,
    strip_first,
    fluxes,
    edge_flux,
    flux,
    spread,
    start_ref,
    conc_ref,
    ext_ref,
    out_rows,
    in_sem,
    out_sem,
):
    def fetch(p):
        copies = []
        for z in range(PLANES):
            held = pl.ds(z * ROWS + p * BOX, BOX)
            rows = pl.ds(z * HROWS + 2 + p * BOX, BOX)
            for n, (source, target) in enumerate(
                ((field_in, field), (coef_in, coef), (flux_in, flux))
            ):
                copies.append(
                    pltpu.make_async_copy(source.at[held], target.at[rows], in_sem.at[p, n])
                )
        return copies

    for p in range(2):
        for copy in fetch(p):
            copy.start()
    inv_mass = scales[0]
    live = live_rows()
    table = table_ref[:, : 3 * SUB + 8].astype(bf16)
    lane = lax.broadcasted_iota(jnp.int32, (8, LANES), 1)
    received = gathered[...]
    columns = lax.broadcasted_iota(jnp.int32, received.shape, 1)
    peak = jnp.max(jnp.where(columns == 0, received, 0.0), keepdims=True)
    step = CFL_SAFE / ((4.0 + 2.0 * Z_WEIGHT) * peak)
    mine = jnp.sum(jnp.where(columns == 1, received, 0.0))
    everyone = jnp.sum(jnp.where(columns == 2, received, 0.0))
    load_out[0, 0] = mine / (everyone / 16.0)
    step = jnp.broadcast_to(step, (8, LANES))

    for z in range(PLANES):
        for layer in range(2):
            field[z * HROWS + layer] = below[z * 2 + layer]
            field[z * HROWS + ROWS + 2 + layer] = above[z * 2 + layer]
        for c in range(2):
            strip_field[z * 8 + c] = left[z * 2 + c]
            strip_field[z * 8 + 2 + c] = own[z * 4 + 2 + c]
            strip_field[z * 8 + 4 + c] = own[z * 4 + c]
            strip_field[z * 8 + 6 + c] = right[z * 2 + c]

    def coefficients(source, target, count, kept):
        def body(index, carry):
            coefficient_step(source, target, kept, index * LONG, inv_mass, table, live)
            return carry

        lax.fori_loop(0, count // LONG, body, 0)
        if kept is not None:
            for i in range(count - LONG, count):
                kept[i] = lane_flux(source[i], target[i])

    def face(source, weight, here, there, part):
        return (weight[here, part, :] + weight[there, part, :]) * (
            source[there, part, :] - source[here, part, :]
        )

    odd = (lane & 1) == 1

    def side_fluxes(source, weight):
        even_from = lane >> 1
        odd_from = ((lane + 1) >> 1) & (ROWS - 1)
        for z in range(PLANES):
            for part in PARTS:
                entering = face(source, weight, z * 8 + 1, z * 8 + 2, part)
                leaving = face(source, weight, z * 8 + 5, z * 8 + 6, part)
                fluxes[z * 2, part, :] = entering
                fluxes[z * 2 + 1, part, :] = leaving
                pick = lambda v, at: jnp.take_along_axis(v, at, axis=1, mode="promise_in_bounds")
                edge_flux[z, part, :] = jnp.where(
                    odd, pick(leaving, odd_from), pick(entering, even_from)
                )

    def strip_update():
        for r in (1, 2, 5, 6):
            for part in PARTS:
                above_flux = None
                for z in range(PLANES):
                    at = z * 8 + r
                    here = strip_field[at, part, :]
                    weight = strip_coef[at, part, :]
                    total = face(strip_field, strip_coef, at, at + 1, part)
                    total = total - face(strip_field, strip_coef, at - 1, at, part)
                    onward = (weight + pltpu.roll(weight, LANES - 1, 1)) * (
                        pltpu.roll(here, LANES - 1, 1) - here
                    )
                    total = total + (onward - pltpu.roll(onward, 1, 1))
                    if above_flux is not None:
                        total = total - Z_WEIGHT * above_flux
                    if z < PLANES - 1:
                        above_flux = face(strip_field, strip_coef, at, at + 8, part)
                        total = total + Z_WEIGHT * above_flux
                    strip_first[at, part, :] = here + step * total

    def updated(source, weight, x0, count, part, onward, ends):
        result = [[] for _ in range(count)]
        above_flux = [None] * count
        for z in range(PLANES):
            base = z * HROWS + x0 + 1
            here = [source[base + i, part, :] for i in range(count + 2)]
            coefs = [weight[base + i, part, :] for i in range(count + 2)]
            along = [
                (coefs[i] + coefs[i + 1]) * (here[i + 1] - here[i]) for i in range(count + 1)
            ]
            for i in range(count):
                c, d = here[i + 1], coefs[i + 1]
                raw, back = onward[i][z]
                entering, leaving = ends[i][z]
                total = (along[i + 1] - along[i]) + (
                    jnp.where(lane == LANES - 1, leaving, raw)
                    - jnp.where(lane == 0, entering, back)
                )
                if z < PLANES - 1:
                    over = base + i + 1 + HROWS
                    flux = Z_WEIGHT * (
                        (d + weight[over, part, :]) * (source[over, part, :] - c)
                    )
                    total = total + flux
                if z > 0:
                    total = total - above_flux[i]
                if z < PLANES - 1:
                    above_flux[i] = flux
                result[i].append(c + step * total)
        return result

    def outer_row(source, weight, x, part):
        shift = -x % LANES
        onward, ends = [], []
        for z in range(PLANES):
            at = z * HROWS + x + 2
            raw = lane_flux(source[at, part, :], weight[at, part, :])
            onward.append((raw, pltpu.roll(raw, 1, 1)))
            ends.append(
                (
                    pltpu.roll(fluxes[z * 2, part, :], shift, 1),
                    pltpu.roll(fluxes[z * 2 + 1, part, :], (shift + LANES - 1) % LANES, 1),
                )
            )
        return updated(source, weight, x, 1, part, [onward], [ends])[0]

    def finish_rows(source, weight, group, part):
        x = group * GROUP
        onward, ends = [], []
        for i in range(GROUP):
            raws = [flux[z * HROWS + x + i + 2, part, :] for z in range(PLANES)]
            onward.append([(raw, pltpu.roll(raw, 1, 1)) for raw in raws])
            shift = (2 * LANES - 2 * (x + i)) & (LANES - 1)
            edges = [pltpu.roll(edge_flux[z, part, :], shift, 1) for z in range(PLANES)]
            ends.append([(edge, edge) for edge in edges])
        return updated(source, weight, x, GROUP, part, onward, ends)

    coefficients(strip_field, strip_coef, PLANES * 8, None)
    side_fluxes(strip_field, strip_coef)
    strip_update()
    halo = [z * HROWS + x for z in range(PLANES) for x in (0, 1, ROWS + 2, ROWS + 3)]
    for n in range(0, len(halo), CHUNK):
        at = halo[n : n + CHUNK]
        for i, value in zip(at, diffusivity([field[i] for i in at], inv_mass, table, live)):
            coef[i] = value

    def outer_rows(x):
        for part in PARTS:
            for z, value in enumerate(outer_row(field, coef, x, part)):
                first[z * HROWS + x + 2, part, :] = value

    def first_rows(group, carry):
        for part in PARTS:
            for i, planes in enumerate(finish_rows(field, coef, group, part)):
                for z, value in enumerate(planes):
                    first[z * HROWS + group * GROUP + i + 2, part, :] = value
        return carry

    for copy in fetch(0):
        copy.wait()
    outer_rows(-1)
    lax.fori_loop(0, BOX // GROUP - 1, first_rows, 0)
    for copy in fetch(1):
        copy.wait()
    lax.fori_loop(BOX // GROUP - 1, ROWS // GROUP, first_rows, 0)
    outer_rows(ROWS)
    for z in range(PLANES):
        first[z * HROWS] = field[z * HROWS]
        first[z * HROWS + HROWS - 1] = field[z * HROWS + HROWS - 1]
        for r in (0, 3, 4, 7):
            strip_first[z * 8 + r] = strip_field[z * 8 + r]
    coefficients(strip_first, strip_coef, PLANES * 8, None)
    side_fluxes(strip_first, strip_coef)
    coefficients(first, coef, PLANES * HROWS, flux)

    sub = lax.broadcasted_iota(jnp.int32, (8, LANES), 0)
    heat_row = sub == SPECIES - 16

    def pack(group):
        for n, part in enumerate(PARTS):
            for i in range(GROUP):
                planes = [spread[i * PLANES + z, part, :] for z in range(PLANES)]
                planes = swap_quarters(planes, lane)
                for j in range(4):
                    at = j * ROWS + group * GROUP + i
                    beginning = planes[j] * inv_mass[part]
                    start_ref[at, part, :] = beginning
                    conc_ref[at, part, :] = beginning
                    if n == 2:
                        heat = jnp.broadcast_to(planes[j][SPECIES - 16 : SPECIES - 15, :], sub.shape)
                        inverse = 1.0 / heat
                        high = coarse(inverse)
                        ext_ref[at, :8, :] = jnp.where(
                            heat_row,
                            high,
                            jnp.where(sub == SPECIES - 15, inverse - high, 1.0),
                        )
                        ext_ref[at, 8:, :] = jnp.where(heat_row, high, 1.0)

    def second_rows(group, carry):
        pack(jnp.maximum(group - 1, 0))
        for part in PARTS:
            for i, planes in enumerate(finish_rows(first, coef, group, part)):
                for z, value in enumerate(planes):
                    spread[i * PLANES + z, part, :] = value
        return carry

    for i in range(GROUP * PLANES):
        spread[i] = jnp.ones((SUB, LANES), f32)
    lax.fori_loop(0, ROWS // GROUP, second_rows, 0)
    pack(ROWS // GROUP - 1)

    log_table = log_table_ref[:, : 2 * SUB].astype(bf16)
    sum_table = sum_table_ref[:, : 2 * RPAD].astype(bf16)
    spare = sub >= SPECIES - 16
    mass = scales[1]
    heat_mass = scales[2] * mass

    def box(p, j):
        base = j * ROWS + p * BOX
        chunks = BOX // BOX_CHUNK

        def rates(chunk):
            at = [base + chunk * BOX_CHUNK + i for i in range(BOX_CHUNK)]
            conc = jnp.concatenate([conc_ref[i] for i in at], axis=1)
            spare_rows = jnp.concatenate([spare] * BOX_CHUNK, axis=1)
            ext = jnp.concatenate([ext_ref[i] for i in at], axis=1)
            logs = jnp.log2(conc)
            high = coarse(logs)
            low = logs - high
            stacked = jnp.concatenate(
                [
                    high[:16],
                    jnp.where(spare_rows, ext[:8], high[16:]),
                    low[:16],
                    jnp.where(spare_rows, ext[8:], low[16:]),
                ],
                axis=0,
            ).astype(bf16)
            return jnp.dot(log_table, stacked, preferred_element_type=f32)

        def advance(chunk, exponent):
            at = [base + chunk * BOX_CHUNK + i for i in range(BOX_CHUNK)]
            progress = jnp.exp2(exponent)
            high = coarse(progress)
            stacked = jnp.concatenate([high, progress - high], axis=0).astype(bf16)
            sums = jnp.dot(sum_table, stacked, preferred_element_type=f32)
            conc = jnp.concatenate([conc_ref[i] for i in at], axis=1)
            start = jnp.concatenate([start_ref[i] for i in at], axis=1)
            conc = (start + sums[:SUB, :]) * (conc / (conc + sums[SUB:, :]))
            for n, i in enumerate(at):
                conc_ref[i] = conc[:, n * LANES : (n + 1) * LANES]

        def sweep(number, inner):
            ahead = [rates(chunk) for chunk in range(AHEAD)]
            for chunk in range(chunks):
                if chunk + AHEAD < chunks:
                    ahead.append(rates(chunk + AHEAD))
                advance(chunk, ahead.pop(0))
            return inner

        lax.fori_loop(0, box_cost[p, j], sweep, 0)

    def give(p, flags, x, carry):
        planes = []
        for j in range(4):
            conc, start = conc_ref[j * ROWS + x], start_ref[j * ROWS + x]
            advanced = conc * mass
            source = jnp.sum(heat_mass * (conc - start), axis=0, keepdims=True)
            heat = start[16:, :] + jnp.broadcast_to(flags[j] * source, sub.shape)
            planes.append(
                [advanced[:8], advanced[8:16], jnp.where(heat_row, heat, advanced[16:])]
            )
        for n, part in enumerate(PARTS):
            for z, value in enumerate(swap_quarters([plane[n] for plane in planes], lane)):
                out_rows[z, x, part, :] = value
        return carry

    quarter = BOX // 2
    for p in range(2):
        for j in range(4):
            box(p, j)
        flags = [flame_flag[p, j].astype(f32) for j in range(4)]
        for n in range(2):
            begin = p * BOX + n * quarter
            rows = pl.ds(begin, quarter)
            lax.fori_loop(
                begin, begin + quarter, functools.partial(give, p, flags), 0, unroll=4
            )
            for k in range(FIELDS):
                pltpu.make_async_copy(
                    out_rows.at[:, rows, k], out.at[k, :, rows], out_sem.at[p]
                ).start()
    for p in range(2):
        whole = out.at[:, :, pl.ds(p * BOX, BOX)]
        pltpu.make_async_copy(whole, whole, out_sem.at[p]).wait()


def substep(box_cost, flame_flag, *operands):
    vmem = pl.BlockSpec(memory_space=pltpu.VMEM)
    smem = pl.BlockSpec(memory_space=pltpu.SMEM)
    hbm = pl.BlockSpec(memory_space=pl.ANY)
    rows = lambda n: pltpu.VMEM((n, SUB, LANES), f32)
    return pl.pallas_call(
        substep_kernel,
        in_specs=[smem, smem, hbm, hbm, hbm] + [vmem] * (len(operands) - 3),
        out_specs=[hbm, smem],
        out_shape=[
            jax.ShapeDtypeStruct((FIELDS, PLANES, ROWS, LANES), f32),
            jax.ShapeDtypeStruct((1, 1), f32),
        ],
        scratch_shapes=[
            rows(PLANES * HROWS),
            rows(PLANES * HROWS),
            rows(PLANES * HROWS),
            rows(32),
            rows(32),
            rows(32),
            rows(8),
            rows(4),
            rows(PLANES * HROWS),
            rows(GROUP * PLANES),
            rows(PLANES * ROWS),
            rows(PLANES * ROWS),
            pltpu.VMEM((PLANES * ROWS, 16, LANES), f32),
            pltpu.VMEM((PLANES, ROWS, SUB, LANES), f32),
            pltpu.SemaphoreType.DMA((2, 3)),
            pltpu.SemaphoreType.DMA((2,)),
        ],
        compiler_params=pltpu.CompilerParams(vmem_limit_bytes=VMEM_BYTES),
    )(box_cost, flame_flag, *operands)


def shifted(x, axis, by):
    count = lax.axis_size(axis)
    return lax.ppermute(x, axis, [(i, (i + by) % count) for i in range(count)])


def per_device(
    state,
    masses,
    reciprocals,
    rate_scale,
    energy,
    reactants,
    products,
    heat_release,
    box_cost,
    box_owner,
    flame_flag,
):
    field, low, high, own, *constants = edges(
        state.reshape(FIELDS, PLANES * ROWS, LANES),
        masses.reshape(1, -1),
        reciprocals,
        rate_scale.reshape(1, -1),
        energy.reshape(1, -1),
        reactants.T,
        products.T,
    )
    below = shifted(high, "gx", 1)
    above = shifted(low, "gx", -1)
    message, coef, flux = local_peak(box_cost, box_owner, field, constants[0], constants[1])
    own, to_left, to_right = corners(own, below, above, message)
    left = shifted(to_right, "gy", 1)
    right = shifted(to_left, "gy", -1)
    gathered = lax.all_to_all(message, ("gx", "gy"), 0, 0, tiled=True)
    heat = jnp.pad(heat_release, (0, SUB - SPECIES))[:, None]
    heat = jnp.broadcast_to(heat, (1, SUB, LANES))
    constants[0] = jnp.concatenate([constants[0], heat], axis=0)
    return tuple(
        substep(
            box_cost,
            flame_flag,
            field,
            coef,
            flux,
            below,
            above,
            left,
            right,
            own,
            gathered,
            *constants,
        )
    )


def solution(mesh):
    split = P("gx", "gy")
    whole = P(None, None, "gx", "gy")
    return jax.shard_map(
        per_device,
        mesh=mesh,
        in_specs=(whole, P(), P(), P(), P(), P(), P(), P(), split, split, split),
        out_specs=(whole, split),
        check_vma=False,
    )
```

```python
import functools

import jax
import jax.numpy as jnp
from jax import lax
from jax.experimental import pallas as pl
from jax.experimental.pallas import tpu as pltpu
from jax.sharding import PartitionSpec as P

SPECIES = 21
FIELDS = 22
SUB = 24
LANES = 128
PLANES = 4
ROWS = 64
HROWS = ROWS + 4
BOX = 32
REACTIONS = 84
RPAD = 88
CHUNK = 4
BOX_CHUNK = 4
GROUP = 2
LONG = 16
AHEAD = 3
LOG2E = 1.4426950408889634
Z_WEIGHT = 0.25
CFL_SAFE = 0.5
HALF = 0.5
VMEM_BYTES = 56 * 1024 * 1024

PARTS = [slice(0, 8), slice(8, 16), slice(16, 24)]

f32 = jnp.float32
bf16 = jnp.bfloat16


def live_rows():
    return (lax.broadcasted_iota(jnp.int32, (SUB, LANES), 0) < SPECIES).astype(f32)


def fill_spare(rows, count):
    def body(i, carry):
        rows[i, FIELDS:SUB, :] = jnp.ones((SUB - FIELDS, LANES), f32)
        return carry

    lax.fori_loop(0, count, body, 0, unroll=8)


def coarse(x):
    return x.astype(bf16).astype(f32)


def diffusivity(rows, inv_mass, table, live):
    amounts = jnp.concatenate([row * inv_mass for row in rows], axis=1)
    high = coarse(amounts)
    low = amounts - high
    blank = jnp.zeros((8, amounts.shape[1]), f32)
    stacked = jnp.concatenate([high, low, high, blank], axis=0).astype(bf16)
    sums = jnp.dot(table, stacked, preferred_element_type=f32)
    result = []
    for i, row in enumerate(rows):
        lanes = slice(i * LANES, (i + 1) * LANES)
        heat = row[SPECIES : SPECIES + 1, :]
        scale = (HALF * heat * jnp.sqrt(heat)) * sums[SUB : SUB + 8, lanes]
        scale = jnp.concatenate([scale] * 3, axis=0)
        result.append(live * (1.0 - row) * scale / sums[:SUB, lanes])
    return result


def split3(x):
    high = coarse(x)
    middle = coarse(x - high)
    return high, middle, coarse((x - high) - middle)


def fill_tables(
    masses,
    reciprocals,
    rate_scale,
    energy,
    reactants,
    products,
    scales,
    table,
    log_table,
    sum_table,
    square,
):
    lane = lax.broadcasted_iota(jnp.int32, (LANES, LANES), 1)
    row = lax.broadcasted_iota(jnp.int32, (LANES, LANES), 0)

    def padded(value, filler=0.0):
        square[...] = jnp.full((LANES, LANES), filler, f32)
        square[: value.shape[0], : value.shape[1]] = value
        return square[...]

    def column(ref, filler):
        return jnp.broadcast_to(padded(ref[...], filler)[:1], (LANES, LANES)).T

    mass = column(masses, 1.0)[:SUB]
    scales[0] = 1.0 / mass
    scales[1] = mass

    cross = padded(reciprocals[...])
    cross = jnp.where(row == lane, 0.0, cross).T
    cross = jnp.where(lane < SPECIES, jnp.where(row < SPECIES, cross, 1.0), 0.0)[: SUB + 8]
    high = coarse(cross)
    table[...] = high + pltpu.roll(high, SUB, 1) + pltpu.roll(cross - high, 2 * SUB, 1)

    react_back = padded(reactants[...].astype(f32))
    react = react_back.T
    eh, em, _ = split3((-LOG2E) * column(energy, 0.0)[:RPAD])
    ah, am, al = split3(jnp.log2(column(rate_scale, 1.0)[:RPAD]))
    place = lane[:RPAD]
    ext = jnp.zeros((RPAD, LANES), f32)
    spare = (SPECIES, SPECIES + 1, SPECIES + 2)
    for n, value in zip(spare + tuple(SUB + n for n in spare), (eh, eh, ah, em, am, al)):
        ext = jnp.where(place == n, value, ext)
    log_table[...] = react[:RPAD] + pltpu.roll(react[:RPAD], SUB, 1) + ext

    make = padded(products[...].astype(f32))[:SUB]
    sums = HALF * jnp.concatenate([make, react_back[:SUB]], axis=0)
    moved = pltpu.roll(sums, RPAD, 1)
    place = lane[: 2 * SUB]
    sum_table[:, :LANES] = jnp.where(place < RPAD, sums, moved)
    sum_table[:, LANES:] = jnp.where(place < 2 * RPAD - LANES, moved, 0.0)


def edges_kernel(
    state,
    masses,
    reciprocals,
    rate_scale,
    energy,
    reactants,
    products,
    field_out,
    low,
    high,
    own,
    to_left,
    to_right,
    scales,
    table,
    log_table,
    sum_table,
    field,
    square,
    in_sem,
    out_sem,
):
    def half_rows(half):
        return pl.ds(half * 2 * ROWS, 2 * ROWS)

    def keep(half):
        rows = half_rows(half)
        return pltpu.make_async_copy(field.at[rows], field_out.at[rows], out_sem.at[half])

    for half in range(2):
        rows = half_rows(half)
        for k in range(FIELDS):
            pltpu.make_async_copy(state.at[k, rows], field.at[rows, k], in_sem.at[half]).start()
    fill_spare(field, PLANES * ROWS)
    fill_tables(
        masses,
        reciprocals,
        rate_scale,
        energy,
        reactants,
        products,
        scales,
        table,
        log_table,
        sum_table,
        square,
    )
    lane = lax.broadcasted_iota(jnp.int32, (8, LANES), 1)
    for half in range(2):
        whole = state.at[:, half_rows(half)]
        pltpu.make_async_copy(whole, whole, in_sem.at[half]).wait()
        keep(half).start()
        planes = (2 * half, 2 * half + 1)
        for z in planes:
            for layer in range(2):
                low[z * 2 + layer] = field[z * ROWS + layer]
                high[z * 2 + layer] = field[z * ROWS + ROWS - 2 + layer]

        def gather(index, held):
            mine = (lane >> 2) == index
            result = []
            for z in planes:
                for group in range(2):
                    for part in PARTS:
                        row = field[z * ROWS + group * 32 + index, part, :]
                        turned = pltpu.roll(row, 4 * index + 2, 1)
                        result.append(jnp.where(mine, turned, held[len(result)]))
            return tuple(result)

        held = lax.fori_loop(0, 32, gather, (jnp.ones((8, LANES), f32),) * 12, unroll=2)
        for i, z in enumerate(planes):
            for n, part in enumerate(PARTS):
                for c in range(4):
                    index = (4 * lane + c) & (LANES - 1)
                    pick = lambda v: jnp.take_along_axis(v, index, axis=1, mode="promise_in_bounds")
                    value = jnp.where(
                        lane < 32, pick(held[i * 6 + n]), pick(held[i * 6 + 3 + n])
                    )
                    own[z * 4 + c, part, :] = value
                    side = to_right if c < 2 else to_left
                    side[z * 2 + c % 2, part, :] = value
    for half in range(2):
        keep(half).wait()


def edges(*operands):
    vmem = pl.BlockSpec(memory_space=pltpu.VMEM)
    hbm = pl.BlockSpec(memory_space=pl.ANY)
    rows = lambda n: jax.ShapeDtypeStruct((n, SUB, LANES), f32)
    return pl.pallas_call(
        edges_kernel,
        in_specs=[hbm] + [vmem] * 6,
        out_specs=[hbm] + [vmem] * 9,
        out_shape=[
            rows(PLANES * ROWS),
            rows(8),
            rows(8),
            rows(16),
            rows(8),
            rows(8),
            rows(2),
            jax.ShapeDtypeStruct((SUB + 8, LANES), f32),
            jax.ShapeDtypeStruct((RPAD, LANES), f32),
            jax.ShapeDtypeStruct((2 * SUB, 2 * LANES), f32),
        ],
        scratch_shapes=[
            pltpu.VMEM((PLANES * ROWS, SUB, LANES), f32),
            pltpu.VMEM((LANES, LANES), f32),
            pltpu.SemaphoreType.DMA((2,)),
            pltpu.SemaphoreType.DMA((2,)),
        ],
        compiler_params=pltpu.CompilerParams(vmem_limit_bytes=VMEM_BYTES),
    )(*operands)


def lane_flux(row, weight):
    onward = LANES - 1
    return (weight + pltpu.roll(weight, onward, 1)) * (pltpu.roll(row, onward, 1) - row)


def coefficient_step(source, target, flux, base, inv_mass, table, live):
    if flux is not None:
        before = jnp.maximum(base - LONG, 0)
        for i in range(LONG):
            flux[before + i] = lane_flux(source[before + i], target[before + i])
    result = []
    for n in range(0, LONG, CHUNK):
        at = [base + n + i for i in range(CHUNK)]
        values = diffusivity([source[i] for i in at], inv_mass, table, live)
        for i, value in zip(at, values):
            target[i] = value
        result += values
    return result


def peak_kernel(
    box_cost, box_owner, field_in, scales, table_ref, message, coef_out, field, coef, in_sem, out_sem
):
    quarter = lambda z: pl.ds(z * ROWS, ROWS)

    def fetch(z):
        return pltpu.make_async_copy(
            field_in.at[quarter(z)], field.at[quarter(z)], in_sem.at[z]
        )

    def keep(z):
        return pltpu.make_async_copy(coef.at[quarter(z)], coef_out.at[quarter(z)], out_sem.at[z])

    for z in range(PLANES):
        fetch(z).start()
    inv_mass = scales[0]
    live = live_rows()
    table = table_ref[:, : 3 * SUB + 8].astype(bf16)
    best = jnp.zeros((SUB, LANES), f32)
    for z in range(PLANES):
        fetch(z).wait()

        def body(index, best):
            at = [z * ROWS + index * CHUNK + i for i in range(CHUNK)]
            rows = [field[i] for i in at]
            for i, value in zip(at, diffusivity(rows, inv_mass, table, live)):
                coef[i] = value
                best = jnp.maximum(best, value)
            return best

        best = lax.fori_loop(0, ROWS // CHUNK, body, best, unroll=4)
        keep(z).start()
    top = 2.0 * jnp.max(best)
    device = lax.broadcasted_iota(jnp.int32, (LANES, LANES), 0)
    column = lax.broadcasted_iota(jnp.int32, (LANES, LANES), 1)
    nx, ny = lax.axis_size("gx"), lax.axis_size("gy")
    gx, gy = lax.axis_index("gx"), lax.axis_index("gy")
    same = device // ny == gx
    place = device % ny
    charged = jnp.zeros((LANES, LANES), f32)
    total = 0.0
    for p in range(2):
        for j in range(4):
            cost = box_cost[p, j].astype(f32)
            total = total + cost
            charged = charged + jnp.where(place == box_owner[p, j], cost, 0.0)
    tally = jnp.where(same, jnp.where(column == LANES - 2, charged, total), 0.0)
    corner = jnp.zeros((LANES, LANES), f32)
    for x, dx in ((0, nx - 1), (ROWS - 1, 1)):
        block = jnp.concatenate(
            [field[z * ROWS + x] for z in range(PLANES)]
            + [jnp.zeros((LANES - PLANES * SUB, LANES), f32)],
            axis=0,
        ).T
        for y, dy in ((0, ny - 1), (LANES - 1, 1)):
            there = lax.rem(gx + dx, nx) * ny + lax.rem(gy + dy, ny)
            cells = jnp.broadcast_to(block[y : y + 1], (LANES, LANES))
            corner = jnp.where(device == there, cells, corner)
    message[...] = jnp.where(
        column == LANES - 3, top, jnp.where(column > LANES - 3, tally, corner)
    )
    for z in range(PLANES):
        keep(z).wait()


def local_peak(box_cost, box_owner, field, scales, table):
    vmem = pl.BlockSpec(memory_space=pltpu.VMEM)
    smem = pl.BlockSpec(memory_space=pltpu.SMEM)
    hbm = pl.BlockSpec(memory_space=pl.ANY)
    rows = jax.ShapeDtypeStruct((PLANES * ROWS, SUB, LANES), f32)
    assert lax.axis_size("gx") * lax.axis_size("gy") == LANES
    return pl.pallas_call(
        peak_kernel,
        in_specs=[smem, smem, hbm, vmem, vmem],
        out_specs=[vmem, hbm],
        out_shape=[jax.ShapeDtypeStruct((LANES, LANES), f32), rows],
        scratch_shapes=[
            pltpu.VMEM((PLANES * ROWS, SUB, LANES), f32),
            pltpu.VMEM((PLANES * ROWS, SUB, LANES), f32),
            pltpu.SemaphoreType.DMA((PLANES,)),
            pltpu.SemaphoreType.DMA((PLANES,)),
        ],
        compiler_params=pltpu.CompilerParams(vmem_limit_bytes=VMEM_BYTES),
    )(box_cost, box_owner, field, scales, table)


def divergence_rows(source, weight, x0, count, part, onward, ends):
    lane = lax.broadcasted_iota(jnp.int32, (8, LANES), 1)
    result = [[] for _ in range(count)]
    above_flux = [None] * count
    for z in range(PLANES):
        base = z * HROWS + x0 + 1
        here = [source[base + i, part, :] for i in range(count + 2)]
        coefs = [weight[base + i, part, :] for i in range(count + 2)]
        along = [(coefs[i] + coefs[i + 1]) * (here[i + 1] - here[i]) for i in range(count + 1)]
        for i in range(count):
            c, d = here[i + 1], coefs[i + 1]
            raw, back = onward[i][z]
            entering, leaving = ends[i][z]
            total = (along[i + 1] - along[i]) + (
                jnp.where(lane == LANES - 1, leaving, raw) - jnp.where(lane == 0, entering, back)
            )
            if z < PLANES - 1:
                over = base + i + 1 + HROWS
                flux = Z_WEIGHT * ((d + weight[over, part, :]) * (source[over, part, :] - c))
                total = total + flux
            if z > 0:
                total = total - above_flux[i]
            if z < PLANES - 1:
                above_flux[i] = flux
            result[i].append((c, total))
    return result


def group_rows(source, weight, flux_at, edge_flux, group, part):
    x = group * GROUP
    onward, ends = [], []
    for i in range(GROUP):
        raws = [flux_at(i, z, part) for z in range(PLANES)]
        onward.append([(raw, pltpu.roll(raw, 1, 1)) for raw in raws])
        shift = (2 * LANES - 2 * (x + i)) & (LANES - 1)
        edges = [pltpu.roll(edge_flux[z, part, :], shift, 1) for z in range(PLANES)]
        ends.append([(edge, edge) for edge in edges])
    return divergence_rows(source, weight, x, GROUP, part, onward, ends)


def interleaved(entering, leaving):
    lane = lax.broadcasted_iota(jnp.int32, (8, LANES), 1)
    pick = lambda v, at: jnp.take_along_axis(v, at, axis=1, mode="promise_in_bounds")
    return jnp.where(
        (lane & 1) == 1,
        pick(leaving, ((lane + 1) >> 1) & (ROWS - 1)),
        pick(entering, lane >> 1),
    )


def first_kernel(
    field_in,
    coef_in,
    below,
    above,
    left,
    right,
    own,
    scales,
    table_ref,
    out,
    field,
    coef,
    total,
    edge_flux,
    raw_flux,
    in_sem,
    out_sem,
):
    def fetch(p):
        copies = []
        for z in range(PLANES):
            held = pl.ds(z * ROWS + p * BOX, BOX)
            rows = pl.ds(z * HROWS + 2 + p * BOX, BOX)
            for n, (source, target) in enumerate(((field_in, field), (coef_in, coef))):
                copies.append(
                    pltpu.make_async_copy(source.at[held], target.at[rows], in_sem.at[p, n])
                )
        return copies

    part_way = BOX // GROUP - 1

    def deliver(p):
        begin, end = ((0, part_way * GROUP), (part_way * GROUP, ROWS))[p]
        rows = [pl.ds(z * ROWS + begin, end - begin) for z in range(PLANES)]
        return [pltpu.make_async_copy(total.at[r], out.at[r], out_sem.at[p]) for r in rows]

    for p in range(2):
        for copy in fetch(p):
            copy.start()
    inv_mass = scales[0]
    live = live_rows()
    table = table_ref[:, : 3 * SUB + 8].astype(bf16)
    for z in range(PLANES):
        at = [z * HROWS + 1, z * HROWS + ROWS + 2]
        halo = [below[z * 2 + 1], above[z * 2]]
        sides = [left[z * 2 + 1], own[z * 4 + 2], own[z * 4 + 1], right[z * 2]]
        coefs = diffusivity(halo + sides, inv_mass, table, live)
        for i, row, value in zip(at, halo, coefs):
            field[i] = row
            coef[i] = value
        entering = (coefs[2] + coefs[3]) * (sides[1] - sides[0])
        leaving = (coefs[4] + coefs[5]) * (sides[3] - sides[2])
        for part in PARTS:
            edge_flux[z, part, :] = interleaved(entering[part], leaving[part])

    def start_flux(group):
        for part in PARTS:
            for i in range(GROUP):
                for z in range(PLANES):
                    at = z * HROWS + group * GROUP + i + 2
                    raw_flux[i * PLANES + z, part, :] = lane_flux(
                        field[at, part, :], coef[at, part, :]
                    )

    def rows(group, carry):
        kept = lambda i, z, part: raw_flux[i * PLANES + z, part, :]
        for part in PARTS:
            for i, planes in enumerate(group_rows(field, coef, kept, edge_flux, group, part)):
                for z, (_, value) in enumerate(planes):
                    total[z * ROWS + group * GROUP + i, part, :] = value
        start_flux(jnp.minimum(group + 1, ROWS // GROUP - 1))
        return carry

    for copy in fetch(0):
        copy.wait()
    start_flux(0)
    lax.fori_loop(0, part_way, rows, 0)
    for copy in deliver(0):
        copy.start()
    for copy in fetch(1):
        copy.wait()
    lax.fori_loop(part_way, ROWS // GROUP, rows, 0)
    for copy in deliver(1):
        copy.start()
    for p in range(2):
        for copy in deliver(p):
            copy.wait()


def first_divergence(*operands):
    vmem = pl.BlockSpec(memory_space=pltpu.VMEM)
    hbm = pl.BlockSpec(memory_space=pl.ANY)
    rows = lambda n: pltpu.VMEM((n, SUB, LANES), f32)
    return pl.pallas_call(
        first_kernel,
        in_specs=[hbm, hbm] + [vmem] * 7,
        out_specs=hbm,
        out_shape=jax.ShapeDtypeStruct((PLANES * ROWS, SUB, LANES), f32),
        scratch_shapes=[
            rows(PLANES * HROWS),
            rows(PLANES * HROWS),
            rows(PLANES * ROWS),
            rows(PLANES),
            rows(GROUP * PLANES),
            pltpu.SemaphoreType.DMA((2, 2)),
            pltpu.SemaphoreType.DMA((2,)),
        ],
        compiler_params=pltpu.CompilerParams(vmem_limit_bytes=VMEM_BYTES),
    )(*operands)


def swap_quarters(planes, lane):
    low_half = lane < 64
    even = ((lane >> 5) & 1) == 0
    a, b, c, d = planes
    a, c = (
        jnp.where(low_half, a, pltpu.roll(c, 64, 1)),
        jnp.where(low_half, pltpu.roll(a, 64, 1), c),
    )
    b, d = (
        jnp.where(low_half, b, pltpu.roll(d, 64, 1)),
        jnp.where(low_half, pltpu.roll(b, 64, 1), d),
    )
    a, b = (
        jnp.where(even, a, pltpu.roll(b, 32, 1)),
        jnp.where(even, pltpu.roll(a, 96, 1), b),
    )
    c, d = (
        jnp.where(even, c, pltpu.roll(d, 32, 1)),
        jnp.where(even, pltpu.roll(c, 96, 1), d),
    )
    return [a, b, c, d]


def substep_kernel(
    box_cost,
    flame_flag,
    field_in,
    total_in,
    below,
    above,
    left,
    right,
    own,
    gathered,
    scales,
    table_ref,
    log_table_ref,
    sum_table_ref,
    out,
    load_out,
    field,
    coef,
    first,
    strip_field,
    strip_coef,
    strip_first,
    fluxes,
    edge_flux,
    flux,
    spread,
    start_ref,
    conc_ref,
    ext_ref,
    out_rows,
    in_sem,
    out_sem,
):
    def fetch(p):
        copies = []
        for z in range(PLANES):
            held = pl.ds(z * ROWS + p * BOX, BOX)
            rows = pl.ds(z * HROWS + 2 + p * BOX, BOX)
            for n, (source, target) in enumerate(
                ((field_in, field), (total_in, first))
            ):
                copies.append(
                    pltpu.make_async_copy(source.at[held], target.at[rows], in_sem.at[p, n])
                )
        return copies

    for p in range(2):
        for copy in fetch(p):
            copy.start()
    inv_mass = scales[0]
    live = live_rows()
    table = table_ref[:, : 3 * SUB + 8].astype(bf16)
    lane = lax.broadcasted_iota(jnp.int32, (8, LANES), 1)
    received = gathered[...]
    columns = lax.broadcasted_iota(jnp.int32, received.shape, 1)
    peak = jnp.max(jnp.where(columns == LANES - 3, received, 0.0), keepdims=True)
    step = CFL_SAFE / ((4.0 + 2.0 * Z_WEIGHT) * peak)
    mine = jnp.sum(jnp.where(columns == LANES - 2, received, 0.0))
    everyone = jnp.sum(jnp.where(columns == LANES - 1, received, 0.0))
    load_out[0, 0] = mine / (everyone / 16.0)
    step = jnp.broadcast_to(step, (8, LANES))

    nx, ny = lax.axis_size("gx"), lax.axis_size("gy")

    def outside(dy):
        cells = []
        for dx in (1, nx - 1):
            source = lax.rem(lax.axis_index("gx") + dx, nx) * ny
            source = source + lax.rem(lax.axis_index("gy") + dy, ny)
            cells.append(jnp.broadcast_to(gathered[pl.ds(source, 1), :], received.shape))
        rows = lax.broadcasted_iota(jnp.int32, received.shape, 0)
        return jnp.where(rows == ROWS, cells[0], cells[1]).T

    corners = [outside(ny - 1), outside(1)]
    tips = (lane == ROWS) | (lane == LANES - 1)

    for z in range(PLANES):
        for layer in range(2):
            field[z * HROWS + layer] = below[z * 2 + layer]
            field[z * HROWS + ROWS + 2 + layer] = above[z * 2 + layer]
        for c in range(2):
            strip_field[z * 8 + c] = left[z * 2 + c]
            strip_field[z * 8 + 2 + c] = own[z * 4 + 2 + c]
            strip_field[z * 8 + 4 + c] = own[z * 4 + c]
            strip_field[z * 8 + 6 + c] = right[z * 2 + c]
        for n, part in enumerate(PARTS):
            rows = slice(z * SUB + n * 8, z * SUB + n * 8 + 8)
            for r, cells in ((1, corners[0]), (6, corners[1])):
                strip_field[z * 8 + r, part, :] = jnp.where(
                    tips, cells[rows], strip_field[z * 8 + r, part, :]
                )
            before = below[z * 2 + 1, part, :]
            after = above[z * 2, part, :]
            for r, column in ((2, 0), (5, LANES - 1)):
                strip_field[z * 8 + r, part, :] = jnp.where(
                    lane == LANES - 1,
                    pltpu.roll(before, LANES - 1 - column, 1),
                    jnp.where(
                        lane == ROWS,
                        pltpu.roll(after, (ROWS - column) % LANES, 1),
                        strip_field[z * 8 + r, part, :],
                    ),
                )

    def coefficients(source, target, count, kept):
        def body(index, carry):
            coefficient_step(source, target, kept, index * LONG, inv_mass, table, live)
            return carry

        lax.fori_loop(0, count // LONG, body, 0)
        if kept is not None:
            for i in range(count - LONG, count):
                kept[i] = lane_flux(source[i], target[i])

    def face(source, weight, here, there, part):
        return (weight[here, part, :] + weight[there, part, :]) * (
            source[there, part, :] - source[here, part, :]
        )

    def side_fluxes(source, weight):
        for z in range(PLANES):
            for part in PARTS:
                entering = face(source, weight, z * 8 + 1, z * 8 + 2, part)
                leaving = face(source, weight, z * 8 + 5, z * 8 + 6, part)
                fluxes[z * 2, part, :] = entering
                fluxes[z * 2 + 1, part, :] = leaving
                edge_flux[z, part, :] = interleaved(entering, leaving)

    def strip_update():
        for r in (1, 2, 5, 6):
            for part in PARTS:
                above_flux = None
                for z in range(PLANES):
                    at = z * 8 + r
                    here = strip_field[at, part, :]
                    weight = strip_coef[at, part, :]
                    total = face(strip_field, strip_coef, at, at + 1, part)
                    total = total - face(strip_field, strip_coef, at - 1, at, part)
                    onward = (weight + pltpu.roll(weight, LANES - 1, 1)) * (
                        pltpu.roll(here, LANES - 1, 1) - here
                    )
                    total = total + (onward - pltpu.roll(onward, 1, 1))
                    if above_flux is not None:
                        total = total - Z_WEIGHT * above_flux
                    if z < PLANES - 1:
                        above_flux = face(strip_field, strip_coef, at, at + 8, part)
                        total = total + Z_WEIGHT * above_flux
                    strip_first[at, part, :] = here + step * total

    def outer_row(source, weight, x, part):
        shift = -x % LANES
        onward, ends = [], []
        for z in range(PLANES):
            at = z * HROWS + x + 2
            raw = lane_flux(source[at, part, :], weight[at, part, :])
            onward.append((raw, pltpu.roll(raw, 1, 1)))
            ends.append(
                (
                    pltpu.roll(fluxes[z * 2, part, :], shift, 1),
                    pltpu.roll(fluxes[z * 2 + 1, part, :], (shift + LANES - 1) % LANES, 1),
                )
            )
        return divergence_rows(source, weight, x, 1, part, [onward], [ends])[0]

    coefficients(strip_field, strip_coef, PLANES * 8, None)
    side_fluxes(strip_field, strip_coef)
    strip_update()
    for p in range(2):
        for copy in fetch(p):
            copy.wait()
    for z in range(PLANES):
        at = [z * HROWS + x for x in (0, 1, 2, ROWS + 1, ROWS + 2, ROWS + 3)]
        for i, value in zip(at, diffusivity([field[i] for i in at], inv_mass, table, live)):
            coef[i] = value
    for x in (-1, ROWS):
        for part in PARTS:
            for z, (value, total) in enumerate(outer_row(field, coef, x, part)):
                first[z * HROWS + x + 2, part, :] = value + step * total
    wide_step = jnp.concatenate([step] * 3, axis=0)

    def first_rows(x, carry):
        for z in range(PLANES):
            at = z * HROWS + 2 + x
            first[at] = field[at] + wide_step * first[at]
        return carry

    lax.fori_loop(0, ROWS, first_rows, 0, unroll=4)
    for z in range(PLANES):
        first[z * HROWS] = field[z * HROWS]
        first[z * HROWS + HROWS - 1] = field[z * HROWS + HROWS - 1]
        for r in (0, 3, 4, 7):
            strip_first[z * 8 + r] = strip_field[z * 8 + r]
    coefficients(strip_first, strip_coef, PLANES * 8, None)
    side_fluxes(strip_first, strip_coef)
    coefficients(first, coef, PLANES * HROWS, flux)

    sub = lax.broadcasted_iota(jnp.int32, (8, LANES), 0)
    heat_row = sub == SPECIES - 16

    def pack(group):
        for n, part in enumerate(PARTS):
            for i in range(GROUP):
                planes = [spread[i * PLANES + z, part, :] for z in range(PLANES)]
                planes = swap_quarters(planes, lane)
                for j in range(4):
                    at = j * ROWS + group * GROUP + i
                    beginning = planes[j] * inv_mass[part]
                    start_ref[at, part, :] = beginning
                    conc_ref[at, part, :] = beginning
                    if n == 2:
                        heat = jnp.broadcast_to(planes[j][SPECIES - 16 : SPECIES - 15, :], sub.shape)
                        inverse = 1.0 / heat
                        high = coarse(inverse)
                        ext_ref[at, :8, :] = jnp.where(
                            heat_row,
                            high,
                            jnp.where(sub == SPECIES - 15, inverse - high, 1.0),
                        )
                        ext_ref[at, 8:, :] = jnp.where(heat_row, high, 1.0)

    def second_rows(group, carry):
        pack(jnp.maximum(group - 1, 0))
        for part in PARTS:
            kept = lambda i, z, part: flux[z * HROWS + group * GROUP + i + 2, part, :]
            for i, planes in enumerate(group_rows(first, coef, kept, edge_flux, group, part)):
                for z, (value, total) in enumerate(planes):
                    spread[i * PLANES + z, part, :] = value + step * total
        return carry

    for i in range(GROUP * PLANES):
        spread[i] = jnp.ones((SUB, LANES), f32)
    lax.fori_loop(0, ROWS // GROUP, second_rows, 0)
    pack(ROWS // GROUP - 1)

    log_table = log_table_ref[:, : 2 * SUB].astype(bf16)
    sum_table = sum_table_ref[:, : 2 * RPAD].astype(bf16)
    spare = sub >= SPECIES - 16
    mass = scales[1]
    heat_mass = scales[2] * mass

    def box(p, j):
        base = j * ROWS + p * BOX
        chunks = BOX // BOX_CHUNK

        def rates(chunk):
            at = [base + chunk * BOX_CHUNK + i for i in range(BOX_CHUNK)]
            conc = jnp.concatenate([conc_ref[i] for i in at], axis=1)
            spare_rows = jnp.concatenate([spare] * BOX_CHUNK, axis=1)
            ext = jnp.concatenate([ext_ref[i] for i in at], axis=1)
            logs = jnp.log2(conc)
            high = coarse(logs)
            low = logs - high
            stacked = jnp.concatenate(
                [
                    high[:16],
                    jnp.where(spare_rows, ext[:8], high[16:]),
                    low[:16],
                    jnp.where(spare_rows, ext[8:], low[16:]),
                ],
                axis=0,
            ).astype(bf16)
            return jnp.dot(log_table, stacked, preferred_element_type=f32)

        def advance(chunk, exponent):
            at = [base + chunk * BOX_CHUNK + i for i in range(BOX_CHUNK)]
            progress = jnp.exp2(exponent)
            high = coarse(progress)
            stacked = jnp.concatenate([high, progress - high], axis=0).astype(bf16)
            sums = jnp.dot(sum_table, stacked, preferred_element_type=f32)
            conc = jnp.concatenate([conc_ref[i] for i in at], axis=1)
            start = jnp.concatenate([start_ref[i] for i in at], axis=1)
            conc = (start + sums[:SUB, :]) * (conc / (conc + sums[SUB:, :]))
            for n, i in enumerate(at):
                conc_ref[i] = conc[:, n * LANES : (n + 1) * LANES]

        def sweep(number, inner):
            ahead = [rates(chunk) for chunk in range(AHEAD)]
            for chunk in range(chunks):
                if chunk + AHEAD < chunks:
                    ahead.append(rates(chunk + AHEAD))
                advance(chunk, ahead.pop(0))
            return inner

        lax.fori_loop(0, box_cost[p, j], sweep, 0)

    def give(p, flags, x, carry):
        planes = []
        for j in range(4):
            conc, start = conc_ref[j * ROWS + x], start_ref[j * ROWS + x]
            advanced = conc * mass
            source = jnp.sum(heat_mass * (conc - start), axis=0, keepdims=True)
            heat = start[16:, :] + jnp.broadcast_to(flags[j] * source, sub.shape)
            planes.append(
                [advanced[:8], advanced[8:16], jnp.where(heat_row, heat, advanced[16:])]
            )
        for n, part in enumerate(PARTS):
            for z, value in enumerate(swap_quarters([plane[n] for plane in planes], lane)):
                out_rows[z, x, part, :] = value
        return carry

    quarter = BOX // 2
    for p in range(2):
        for j in range(4):
            box(p, j)
        flags = [flame_flag[p, j].astype(f32) for j in range(4)]
        for n in range(2):
            begin = p * BOX + n * quarter
            rows = pl.ds(begin, quarter)
            lax.fori_loop(
                begin, begin + quarter, functools.partial(give, p, flags), 0, unroll=4
            )
            for k in range(FIELDS):
                pltpu.make_async_copy(
                    out_rows.at[:, rows, k], out.at[k, :, rows], out_sem.at[p]
                ).start()
    for p in range(2):
        whole = out.at[:, :, pl.ds(p * BOX, BOX)]
        pltpu.make_async_copy(whole, whole, out_sem.at[p]).wait()


def substep(box_cost, flame_flag, *operands):
    vmem = pl.BlockSpec(memory_space=pltpu.VMEM)
    smem = pl.BlockSpec(memory_space=pltpu.SMEM)
    hbm = pl.BlockSpec(memory_space=pl.ANY)
    rows = lambda n: pltpu.VMEM((n, SUB, LANES), f32)
    return pl.pallas_call(
        substep_kernel,
        in_specs=[smem, smem, hbm, hbm] + [vmem] * (len(operands) - 2),
        out_specs=[hbm, smem],
        out_shape=[
            jax.ShapeDtypeStruct((FIELDS, PLANES, ROWS, LANES), f32),
            jax.ShapeDtypeStruct((1, 1), f32),
        ],
        scratch_shapes=[
            rows(PLANES * HROWS),
            rows(PLANES * HROWS),
            rows(PLANES * HROWS),
            rows(32),
            rows(32),
            rows(32),
            rows(8),
            rows(4),
            rows(PLANES * HROWS),
            rows(GROUP * PLANES),
            rows(PLANES * ROWS),
            rows(PLANES * ROWS),
            pltpu.VMEM((PLANES * ROWS, 16, LANES), f32),
            pltpu.VMEM((PLANES, ROWS, SUB, LANES), f32),
            pltpu.SemaphoreType.DMA((2, 2)),
            pltpu.SemaphoreType.DMA((2,)),
        ],
        compiler_params=pltpu.CompilerParams(vmem_limit_bytes=VMEM_BYTES),
    )(box_cost, flame_flag, *operands)


def shifted(x, axis, by):
    count = lax.axis_size(axis)
    return lax.ppermute(x, axis, [(i, (i + by) % count) for i in range(count)])


def per_device(
    state,
    masses,
    reciprocals,
    rate_scale,
    energy,
    reactants,
    products,
    heat_release,
    box_cost,
    box_owner,
    flame_flag,
):
    field, low, high, own, to_left, to_right, *constants = edges(
        state.reshape(FIELDS, PLANES * ROWS, LANES),
        masses.reshape(1, -1),
        reciprocals,
        rate_scale.reshape(1, -1),
        energy.reshape(1, -1),
        reactants.T,
        products.T,
    )
    below = shifted(high, "gx", 1)
    above = shifted(low, "gx", -1)
    left = shifted(to_right, "gy", 1)
    right = shifted(to_left, "gy", -1)
    message, coef = local_peak(box_cost, box_owner, field, constants[0], constants[1])
    total = first_divergence(
        field, coef, below, above, left, right, own, constants[0], constants[1]
    )
    gathered = lax.all_to_all(message, ("gx", "gy"), 0, 0, tiled=True)
    heat = jnp.pad(heat_release, (0, SUB - SPECIES))[:, None]
    heat = jnp.broadcast_to(heat, (1, SUB, LANES))
    constants[0] = jnp.concatenate([constants[0], heat], axis=0)
    return tuple(
        substep(
            box_cost,
            flame_flag,
            field,
            total,
            below,
            above,
            left,
            right,
            own,
            gathered,
            *constants,
        )
    )


def solution(mesh):
    split = P("gx", "gy")
    whole = P(None, None, "gx", "gy")
    return jax.shard_map(
        per_device,
        mesh=mesh,
        in_specs=(whole, P(), P(), P(), P(), P(), P(), P(), split, split, split),
        out_specs=(whole, split),
        check_vma=False,
    )
```

```python
import functools

import jax
import jax.numpy as jnp
from jax import lax
from jax.experimental import pallas as pl
from jax.experimental.pallas import tpu as pltpu
from jax.sharding import PartitionSpec as P

SPECIES = 21
FIELDS = 22
SUB = 24
LANES = 128
PLANES = 4
ROWS = 64
HROWS = ROWS + 4
BOX = 32
REACTIONS = 84
RPAD = 88
CHUNK = 4
BOX_CHUNK = 4
GROUP = 4
SMALLEST = 1e-30
LONG = 16
AHEAD = 4
LOG2E = 1.4426950408889634
Z_WEIGHT = 0.25
CFL_SAFE = 0.5
HALF = 0.5
VMEM_BYTES = 56 * 1024 * 1024

PARTS = [slice(0, 8), slice(8, 16), slice(16, 24)]

f32 = jnp.float32
bf16 = jnp.bfloat16


def live_rows():
    return (lax.broadcasted_iota(jnp.int32, (SUB, LANES), 0) < SPECIES).astype(f32)


def fill_spare(rows, count):
    def body(i, carry):
        rows[i, FIELDS:SUB, :] = jnp.ones((SUB - FIELDS, LANES), f32)
        return carry

    lax.fori_loop(0, count, body, 0, unroll=8)


def coarse(x):
    return x.astype(bf16).astype(f32)


def diffusivity(rows, inv_mass, table, live):
    amounts = jnp.concatenate([row * inv_mass for row in rows], axis=1)
    high = coarse(amounts)
    low = amounts - high
    blank = jnp.zeros((8, amounts.shape[1]), f32)
    stacked = jnp.concatenate([high, low, high, blank], axis=0).astype(bf16)
    sums = jnp.dot(table, stacked, preferred_element_type=f32)
    result = []
    for i, row in enumerate(rows):
        lanes = slice(i * LANES, (i + 1) * LANES)
        heat = row[SPECIES : SPECIES + 1, :]
        scale = (HALF * heat * jnp.sqrt(heat)) * sums[SUB : SUB + 8, lanes]
        scale = jnp.concatenate([scale] * 3, axis=0)
        result.append(live * (1.0 - row) * scale / sums[:SUB, lanes])
    return result


def split3(x):
    high = coarse(x)
    middle = coarse(x - high)
    return high, middle, coarse((x - high) - middle)


def fill_tables(
    masses,
    reciprocals,
    rate_scale,
    energy,
    reactants,
    products,
    scales,
    table,
    log_table,
    sum_table,
    square,
):
    lane = lax.broadcasted_iota(jnp.int32, (LANES, LANES), 1)
    row = lax.broadcasted_iota(jnp.int32, (LANES, LANES), 0)

    def padded(value, filler=0.0):
        square[...] = jnp.full((LANES, LANES), filler, f32)
        square[: value.shape[0], : value.shape[1]] = value
        return square[...]

    def column(ref, filler):
        return jnp.broadcast_to(padded(ref[...], filler)[:1], (LANES, LANES)).T

    mass = column(masses, 1.0)[:SUB]
    scales[0] = 1.0 / mass
    scales[1] = mass

    cross = padded(reciprocals[...])
    cross = jnp.where(row == lane, 0.0, cross).T
    cross = jnp.where(lane < SPECIES, jnp.where(row < SPECIES, cross, 1.0), 0.0)[: SUB + 8]
    high = coarse(cross)
    table[...] = high + pltpu.roll(high, SUB, 1) + pltpu.roll(cross - high, 2 * SUB, 1)

    react_back = padded(reactants[...].astype(f32))
    react = react_back.T
    eh, em, _ = split3((-LOG2E) * column(energy, 0.0)[:RPAD])
    ah, am, al = split3(jnp.log2(column(rate_scale, 1.0)[:RPAD]))
    place = lane[:RPAD]
    ext = jnp.zeros((RPAD, LANES), f32)
    spare = (SPECIES, SPECIES + 1, SPECIES + 2)
    for n, value in zip(spare + tuple(SUB + n for n in spare), (eh, eh, ah, em, am, al)):
        ext = jnp.where(place == n, value, ext)
    log_table[...] = react[:RPAD] + pltpu.roll(react[:RPAD], SUB, 1) + ext

    make = padded(products[...].astype(f32))[:SUB]
    sums = HALF * jnp.concatenate([make, react_back[:SUB]], axis=0)
    moved = pltpu.roll(sums, RPAD, 1)
    place = lane[: 2 * SUB]
    sum_table[:, :LANES] = jnp.where(place < RPAD, sums, moved)
    sum_table[:, LANES:] = jnp.where(place < 2 * RPAD - LANES, moved, 0.0)


def edges_kernel(
    state,
    masses,
    reciprocals,
    rate_scale,
    energy,
    reactants,
    products,
    field_out,
    low,
    high,
    own,
    to_left,
    to_right,
    scales,
    table,
    log_table,
    sum_table,
    field,
    square,
    in_sem,
    out_sem,
):
    def half_rows(half):
        return pl.ds(half * 2 * ROWS, 2 * ROWS)

    def keep(half):
        rows = half_rows(half)
        return pltpu.make_async_copy(field.at[rows], field_out.at[rows], out_sem.at[half])

    for half in range(2):
        rows = half_rows(half)
        for k in range(FIELDS):
            pltpu.make_async_copy(state.at[k, rows], field.at[rows, k], in_sem.at[half]).start()
    fill_spare(field, PLANES * ROWS)
    fill_tables(
        masses,
        reciprocals,
        rate_scale,
        energy,
        reactants,
        products,
        scales,
        table,
        log_table,
        sum_table,
        square,
    )
    lane = lax.broadcasted_iota(jnp.int32, (8, LANES), 1)
    for half in range(2):
        whole = state.at[:, half_rows(half)]
        pltpu.make_async_copy(whole, whole, in_sem.at[half]).wait()
        keep(half).start()
        planes = (2 * half, 2 * half + 1)
        for z in planes:
            for layer in range(2):
                low[z * 2 + layer] = field[z * ROWS + layer]
                high[z * 2 + layer] = field[z * ROWS + ROWS - 2 + layer]

        def gather(index, held):
            mine = (lane >> 2) == index
            result = []
            for z in planes:
                for group in range(2):
                    for part in PARTS:
                        row = field[z * ROWS + group * 32 + index, part, :]
                        turned = pltpu.roll(row, 4 * index + 2, 1)
                        result.append(jnp.where(mine, turned, held[len(result)]))
            return tuple(result)

        held = lax.fori_loop(0, 32, gather, (jnp.ones((8, LANES), f32),) * 12, unroll=2)
        for i, z in enumerate(planes):
            for n, part in enumerate(PARTS):
                for c in range(4):
                    index = (4 * lane + c) & (LANES - 1)
                    pick = lambda v: jnp.take_along_axis(v, index, axis=1, mode="promise_in_bounds")
                    value = jnp.where(
                        lane < 32, pick(held[i * 6 + n]), pick(held[i * 6 + 3 + n])
                    )
                    own[z * 4 + c, part, :] = value
                    side = to_right if c < 2 else to_left
                    side[z * 2 + c % 2, part, :] = value
    for half in range(2):
        keep(half).wait()


def edges(*operands):
    vmem = pl.BlockSpec(memory_space=pltpu.VMEM)
    hbm = pl.BlockSpec(memory_space=pl.ANY)
    rows = lambda n: jax.ShapeDtypeStruct((n, SUB, LANES), f32)
    return pl.pallas_call(
        edges_kernel,
        in_specs=[hbm] + [vmem] * 6,
        out_specs=[hbm] + [vmem] * 9,
        out_shape=[
            rows(PLANES * ROWS),
            rows(8),
            rows(8),
            rows(16),
            rows(8),
            rows(8),
            rows(2),
            jax.ShapeDtypeStruct((SUB + 8, LANES), f32),
            jax.ShapeDtypeStruct((RPAD, LANES), f32),
            jax.ShapeDtypeStruct((2 * SUB, 2 * LANES), f32),
        ],
        scratch_shapes=[
            pltpu.VMEM((PLANES * ROWS, SUB, LANES), f32),
            pltpu.VMEM((LANES, LANES), f32),
            pltpu.SemaphoreType.DMA((2,)),
            pltpu.SemaphoreType.DMA((2,)),
        ],
        compiler_params=pltpu.CompilerParams(vmem_limit_bytes=VMEM_BYTES),
    )(*operands)


def lane_flux(row, weight):
    onward = LANES - 1
    return (weight + pltpu.roll(weight, onward, 1)) * (pltpu.roll(row, onward, 1) - row)


def coefficient_step(source, target, flux, base, inv_mass, table, live):
    if flux is not None:
        before = jnp.maximum(base - LONG, 0)
        for i in range(LONG):
            flux[before + i] = lane_flux(source[before + i], target[before + i])
    result = []
    for n in range(0, LONG, CHUNK):
        at = [base + n + i for i in range(CHUNK)]
        values = diffusivity([source[i] for i in at], inv_mass, table, live)
        for i, value in zip(at, values):
            target[i] = value
        result += values
    return result


def peak_kernel(
    box_cost, box_owner, field_in, scales, table_ref, message, coef_out, field, coef, in_sem, out_sem
):
    quarter = lambda z: pl.ds(z * ROWS, ROWS)

    def fetch(z):
        return pltpu.make_async_copy(
            field_in.at[quarter(z)], field.at[quarter(z)], in_sem.at[z]
        )

    def keep(z):
        return pltpu.make_async_copy(coef.at[quarter(z)], coef_out.at[quarter(z)], out_sem.at[z])

    for z in range(PLANES):
        fetch(z).start()
    inv_mass = scales[0]
    live = live_rows()
    table = table_ref[:, : 3 * SUB + 8].astype(bf16)
    best = jnp.zeros((SUB, LANES), f32)
    for z in range(PLANES):
        fetch(z).wait()

        def body(index, best):
            at = [z * ROWS + index * CHUNK + i for i in range(CHUNK)]
            rows = [field[i] for i in at]
            for i, value in zip(at, diffusivity(rows, inv_mass, table, live)):
                coef[i] = value
                best = jnp.maximum(best, value)
            return best

        best = lax.fori_loop(0, ROWS // CHUNK, body, best, unroll=4)
        keep(z).start()
    top = 2.0 * jnp.max(best)
    device = lax.broadcasted_iota(jnp.int32, (LANES, LANES), 0)
    column = lax.broadcasted_iota(jnp.int32, (LANES, LANES), 1)
    nx, ny = lax.axis_size("gx"), lax.axis_size("gy")
    gx, gy = lax.axis_index("gx"), lax.axis_index("gy")
    same = device // ny == gx
    place = device % ny
    charged = jnp.zeros((LANES, LANES), f32)
    total = 0.0
    for p in range(2):
        for j in range(4):
            cost = box_cost[p, j].astype(f32)
            total = total + cost
            charged = charged + jnp.where(place == box_owner[p, j], cost, 0.0)
    tally = jnp.where(same, jnp.where(column == LANES - 2, charged, total), 0.0)
    corner = jnp.zeros((LANES, LANES), f32)
    for x, dx in ((0, nx - 1), (ROWS - 1, 1)):
        block = jnp.concatenate(
            [field[z * ROWS + x] for z in range(PLANES)]
            + [jnp.zeros((LANES - PLANES * SUB, LANES), f32)],
            axis=0,
        ).T
        for y, dy in ((0, ny - 1), (LANES - 1, 1)):
            there = lax.rem(gx + dx, nx) * ny + lax.rem(gy + dy, ny)
            cells = jnp.broadcast_to(block[y : y + 1], (LANES, LANES))
            corner = jnp.where(device == there, cells, corner)
    message[...] = jnp.where(
        column == LANES - 3, top, jnp.where(column > LANES - 3, tally, corner)
    )
    for z in range(PLANES):
        keep(z).wait()


def local_peak(box_cost, box_owner, field, scales, table):
    vmem = pl.BlockSpec(memory_space=pltpu.VMEM)
    smem = pl.BlockSpec(memory_space=pltpu.SMEM)
    hbm = pl.BlockSpec(memory_space=pl.ANY)
    rows = jax.ShapeDtypeStruct((PLANES * ROWS, SUB, LANES), f32)
    assert lax.axis_size("gx") * lax.axis_size("gy") == LANES
    return pl.pallas_call(
        peak_kernel,
        in_specs=[smem, smem, hbm, vmem, vmem],
        out_specs=[vmem, hbm],
        out_shape=[jax.ShapeDtypeStruct((LANES, LANES), f32), rows],
        scratch_shapes=[
            pltpu.VMEM((PLANES * ROWS, SUB, LANES), f32),
            pltpu.VMEM((PLANES * ROWS, SUB, LANES), f32),
            pltpu.SemaphoreType.DMA((PLANES,)),
            pltpu.SemaphoreType.DMA((PLANES,)),
        ],
        compiler_params=pltpu.CompilerParams(vmem_limit_bytes=VMEM_BYTES),
    )(box_cost, box_owner, field, scales, table)


def divergence_rows(source, weight, x0, count, part, onward, ends):
    lane = lax.broadcasted_iota(jnp.int32, (8, LANES), 1)
    result = [[] for _ in range(count)]
    above_flux = [None] * count
    for z in range(PLANES):
        base = z * HROWS + x0 + 1
        here = [source[base + i, part, :] for i in range(count + 2)]
        coefs = [weight[base + i, part, :] for i in range(count + 2)]
        along = [(coefs[i] + coefs[i + 1]) * (here[i + 1] - here[i]) for i in range(count + 1)]
        for i in range(count):
            c, d = here[i + 1], coefs[i + 1]
            raw, back = onward[i][z]
            entering, leaving = ends[i][z]
            total = (along[i + 1] - along[i]) + (
                jnp.where(lane == LANES - 1, leaving, raw) - jnp.where(lane == 0, entering, back)
            )
            if z < PLANES - 1:
                over = base + i + 1 + HROWS
                flux = Z_WEIGHT * ((d + weight[over, part, :]) * (source[over, part, :] - c))
                total = total + flux
            if z > 0:
                total = total - above_flux[i]
            if z < PLANES - 1:
                above_flux[i] = flux
            result[i].append((c, total))
    return result


def group_rows(source, weight, flux_at, edge_flux, group, part):
    x = group * GROUP
    onward, ends = [], []
    for i in range(GROUP):
        raws = [flux_at(i, z, part) for z in range(PLANES)]
        onward.append([(raw, pltpu.roll(raw, 1, 1)) for raw in raws])
        shift = (2 * LANES - 2 * (x + i)) & (LANES - 1)
        edges = [pltpu.roll(edge_flux[z, part, :], shift, 1) for z in range(PLANES)]
        ends.append([(edge, edge) for edge in edges])
    return divergence_rows(source, weight, x, GROUP, part, onward, ends)


def interleaved(entering, leaving):
    lane = lax.broadcasted_iota(jnp.int32, (8, LANES), 1)
    pick = lambda v, at: jnp.take_along_axis(v, at, axis=1, mode="promise_in_bounds")
    return jnp.where(
        (lane & 1) == 1,
        pick(leaving, ((lane + 1) >> 1) & (ROWS - 1)),
        pick(entering, lane >> 1),
    )


def first_kernel(
    field_in,
    coef_in,
    below,
    above,
    left,
    right,
    own,
    scales,
    table_ref,
    out,
    field,
    coef,
    total,
    edge_flux,
    raw_flux,
    in_sem,
    out_sem,
):
    def fetch(p):
        copies = []
        for z in range(PLANES):
            held = pl.ds(z * ROWS + p * BOX, BOX)
            rows = pl.ds(z * HROWS + 2 + p * BOX, BOX)
            for n, (source, target) in enumerate(((field_in, field), (coef_in, coef))):
                copies.append(
                    pltpu.make_async_copy(source.at[held], target.at[rows], in_sem.at[p, n])
                )
        return copies

    part_way = BOX // GROUP - 1
    stages = (0, part_way, (part_way + ROWS // GROUP) // 2 + 1, ROWS // GROUP)

    def deliver(n):
        begin, end = stages[n] * GROUP, stages[n + 1] * GROUP
        rows = [pl.ds(z * ROWS + begin, end - begin) for z in range(PLANES)]
        return [pltpu.make_async_copy(total.at[r], out.at[r], out_sem.at[n]) for r in rows]

    for p in range(2):
        for copy in fetch(p):
            copy.start()
    inv_mass = scales[0]
    live = live_rows()
    table = table_ref[:, : 3 * SUB + 8].astype(bf16)
    for z in range(PLANES):
        at = [z * HROWS + 1, z * HROWS + ROWS + 2]
        halo = [below[z * 2 + 1], above[z * 2]]
        sides = [left[z * 2 + 1], own[z * 4 + 2], own[z * 4 + 1], right[z * 2]]
        coefs = diffusivity(halo + sides, inv_mass, table, live)
        for i, row, value in zip(at, halo, coefs):
            field[i] = row
            coef[i] = value
        entering = (coefs[2] + coefs[3]) * (sides[1] - sides[0])
        leaving = (coefs[4] + coefs[5]) * (sides[3] - sides[2])
        for part in PARTS:
            edge_flux[z, part, :] = interleaved(entering[part], leaving[part])

    def start_flux(group):
        for part in PARTS:
            for i in range(GROUP):
                for z in range(PLANES):
                    at = z * HROWS + group * GROUP + i + 2
                    raw_flux[i * PLANES + z, part, :] = lane_flux(
                        field[at, part, :], coef[at, part, :]
                    )

    def rows(group, carry):
        kept = lambda i, z, part: raw_flux[i * PLANES + z, part, :]
        for part in PARTS:
            for i, planes in enumerate(group_rows(field, coef, kept, edge_flux, group, part)):
                for z, (_, value) in enumerate(planes):
                    total[z * ROWS + group * GROUP + i, part, :] = value
        start_flux(jnp.minimum(group + 1, ROWS // GROUP - 1))
        return carry

    for copy in fetch(0):
        copy.wait()
    start_flux(0)
    for n in range(3):
        if n == 1:
            for copy in fetch(1):
                copy.wait()
        lax.fori_loop(stages[n], stages[n + 1], rows, 0)
        for copy in deliver(n):
            copy.start()
    for n in range(3):
        for copy in deliver(n):
            copy.wait()


def first_divergence(*operands):
    vmem = pl.BlockSpec(memory_space=pltpu.VMEM)
    hbm = pl.BlockSpec(memory_space=pl.ANY)
    rows = lambda n: pltpu.VMEM((n, SUB, LANES), f32)
    return pl.pallas_call(
        first_kernel,
        in_specs=[hbm, hbm] + [vmem] * 7,
        out_specs=hbm,
        out_shape=jax.ShapeDtypeStruct((PLANES * ROWS, SUB, LANES), f32),
        scratch_shapes=[
            rows(PLANES * HROWS),
            rows(PLANES * HROWS),
            rows(PLANES * ROWS),
            rows(PLANES),
            rows(GROUP * PLANES),
            pltpu.SemaphoreType.DMA((2, 2)),
            pltpu.SemaphoreType.DMA((3,)),
        ],
        compiler_params=pltpu.CompilerParams(vmem_limit_bytes=VMEM_BYTES),
    )(*operands)


def swap_quarters(planes, lane):
    low_half = lane < 64
    even = ((lane >> 5) & 1) == 0
    a, b, c, d = planes
    a, c = (
        jnp.where(low_half, a, pltpu.roll(c, 64, 1)),
        jnp.where(low_half, pltpu.roll(a, 64, 1), c),
    )
    b, d = (
        jnp.where(low_half, b, pltpu.roll(d, 64, 1)),
        jnp.where(low_half, pltpu.roll(b, 64, 1), d),
    )
    a, b = (
        jnp.where(even, a, pltpu.roll(b, 32, 1)),
        jnp.where(even, pltpu.roll(a, 96, 1), b),
    )
    c, d = (
        jnp.where(even, c, pltpu.roll(d, 32, 1)),
        jnp.where(even, pltpu.roll(c, 96, 1), d),
    )
    return [a, b, c, d]


def substep_kernel(
    box_cost,
    flame_flag,
    field_in,
    total_in,
    below,
    above,
    left,
    right,
    own,
    gathered,
    scales,
    table_ref,
    log_table_ref,
    sum_table_ref,
    out,
    load_out,
    field,
    coef,
    first,
    strip_field,
    strip_coef,
    strip_first,
    fluxes,
    edge_flux,
    flux,
    spread,
    start_ref,
    conc_ref,
    ext_ref,
    out_rows,
    in_sem,
    out_sem,
):
    def fetch(p):
        copies = []
        for z in range(PLANES):
            held = pl.ds(z * ROWS + p * BOX, BOX)
            rows = pl.ds(z * HROWS + 2 + p * BOX, BOX)
            for n, (source, target) in enumerate(
                ((field_in, field), (total_in, first))
            ):
                copies.append(
                    pltpu.make_async_copy(source.at[held], target.at[rows], in_sem.at[p, n])
                )
        return copies

    for p in range(2):
        for copy in fetch(p):
            copy.start()
    inv_mass = scales[0]
    live = live_rows()
    table = table_ref[:, : 3 * SUB + 8].astype(bf16)
    lane = lax.broadcasted_iota(jnp.int32, (8, LANES), 1)
    received = gathered[...]
    columns = lax.broadcasted_iota(jnp.int32, received.shape, 1)
    peak = jnp.max(jnp.where(columns == LANES - 3, received, 0.0), keepdims=True)
    step = CFL_SAFE / ((4.0 + 2.0 * Z_WEIGHT) * peak)
    mine = jnp.sum(jnp.where(columns == LANES - 2, received, 0.0))
    everyone = jnp.sum(jnp.where(columns == LANES - 1, received, 0.0))
    load_out[0, 0] = mine / (everyone / 16.0)
    step = jnp.broadcast_to(step, (8, LANES))

    nx, ny = lax.axis_size("gx"), lax.axis_size("gy")

    def outside(dy):
        cells = []
        for dx in (1, nx - 1):
            source = lax.rem(lax.axis_index("gx") + dx, nx) * ny
            source = source + lax.rem(lax.axis_index("gy") + dy, ny)
            cells.append(jnp.broadcast_to(gathered[pl.ds(source, 1), :], received.shape))
        rows = lax.broadcasted_iota(jnp.int32, received.shape, 0)
        return jnp.where(rows == ROWS, cells[0], cells[1]).T

    corners = [outside(ny - 1), outside(1)]
    tips = (lane == ROWS) | (lane == LANES - 1)

    for z in range(PLANES):
        for layer in range(2):
            field[z * HROWS + layer] = below[z * 2 + layer]
            field[z * HROWS + ROWS + 2 + layer] = above[z * 2 + layer]
        for c in range(2):
            strip_field[z * 8 + c] = left[z * 2 + c]
            strip_field[z * 8 + 2 + c] = own[z * 4 + 2 + c]
            strip_field[z * 8 + 4 + c] = own[z * 4 + c]
            strip_field[z * 8 + 6 + c] = right[z * 2 + c]
        for n, part in enumerate(PARTS):
            rows = slice(z * SUB + n * 8, z * SUB + n * 8 + 8)
            for r, cells in ((1, corners[0]), (6, corners[1])):
                strip_field[z * 8 + r, part, :] = jnp.where(
                    tips, cells[rows], strip_field[z * 8 + r, part, :]
                )
            before = below[z * 2 + 1, part, :]
            after = above[z * 2, part, :]
            for r, column in ((2, 0), (5, LANES - 1)):
                strip_field[z * 8 + r, part, :] = jnp.where(
                    lane == LANES - 1,
                    pltpu.roll(before, LANES - 1 - column, 1),
                    jnp.where(
                        lane == ROWS,
                        pltpu.roll(after, (ROWS - column) % LANES, 1),
                        strip_field[z * 8 + r, part, :],
                    ),
                )

    def coefficients(source, target, count, kept):
        def body(index, carry):
            coefficient_step(source, target, kept, index * LONG, inv_mass, table, live)
            return carry

        lax.fori_loop(0, count // LONG, body, 0)
        if kept is not None:
            for i in range(count - LONG, count):
                kept[i] = lane_flux(source[i], target[i])

    def face(source, weight, here, there, part):
        return (weight[here, part, :] + weight[there, part, :]) * (
            source[there, part, :] - source[here, part, :]
        )

    def side_fluxes(source, weight):
        for z in range(PLANES):
            for part in PARTS:
                entering = face(source, weight, z * 8 + 1, z * 8 + 2, part)
                leaving = face(source, weight, z * 8 + 5, z * 8 + 6, part)
                fluxes[z * 2, part, :] = entering
                fluxes[z * 2 + 1, part, :] = leaving
                edge_flux[z, part, :] = interleaved(entering, leaving)

    def strip_update():
        for r in (1, 2, 5, 6):
            for part in PARTS:
                above_flux = None
                for z in range(PLANES):
                    at = z * 8 + r
                    here = strip_field[at, part, :]
                    weight = strip_coef[at, part, :]
                    total = face(strip_field, strip_coef, at, at + 1, part)
                    total = total - face(strip_field, strip_coef, at - 1, at, part)
                    onward = (weight + pltpu.roll(weight, LANES - 1, 1)) * (
                        pltpu.roll(here, LANES - 1, 1) - here
                    )
                    total = total + (onward - pltpu.roll(onward, 1, 1))
                    if above_flux is not None:
                        total = total - Z_WEIGHT * above_flux
                    if z < PLANES - 1:
                        above_flux = face(strip_field, strip_coef, at, at + 8, part)
                        total = total + Z_WEIGHT * above_flux
                    strip_first[at, part, :] = here + step * total

    def outer_row(source, weight, x, part):
        shift = -x % LANES
        onward, ends = [], []
        for z in range(PLANES):
            at = z * HROWS + x + 2
            raw = lane_flux(source[at, part, :], weight[at, part, :])
            onward.append((raw, pltpu.roll(raw, 1, 1)))
            ends.append(
                (
                    pltpu.roll(fluxes[z * 2, part, :], shift, 1),
                    pltpu.roll(fluxes[z * 2 + 1, part, :], (shift + LANES - 1) % LANES, 1),
                )
            )
        return divergence_rows(source, weight, x, 1, part, [onward], [ends])[0]

    coefficients(strip_field, strip_coef, PLANES * 8, None)
    side_fluxes(strip_field, strip_coef)
    strip_update()
    for p in range(2):
        for copy in fetch(p):
            copy.wait()
    for z in range(PLANES):
        at = [z * HROWS + x for x in (0, 1, 2, ROWS + 1, ROWS + 2, ROWS + 3)]
        for i, value in zip(at, diffusivity([field[i] for i in at], inv_mass, table, live)):
            coef[i] = value
    for x in (-1, ROWS):
        for part in PARTS:
            for z, (value, total) in enumerate(outer_row(field, coef, x, part)):
                first[z * HROWS + x + 2, part, :] = value + step * total
    wide_step = jnp.concatenate([step] * 3, axis=0)

    def first_rows(x, carry):
        for z in range(PLANES):
            at = z * HROWS + 2 + x
            first[at] = field[at] + wide_step * first[at]
        return carry

    lax.fori_loop(0, ROWS, first_rows, 0, unroll=4)
    for z in range(PLANES):
        first[z * HROWS] = field[z * HROWS]
        first[z * HROWS + HROWS - 1] = field[z * HROWS + HROWS - 1]
        for r in (0, 3, 4, 7):
            strip_first[z * 8 + r] = strip_field[z * 8 + r]
    coefficients(strip_first, strip_coef, PLANES * 8, None)
    side_fluxes(strip_first, strip_coef)
    coefficients(first, coef, PLANES * HROWS, flux)

    sub = lax.broadcasted_iota(jnp.int32, (8, LANES), 0)
    heat_row = sub == SPECIES - 16

    def pack(group):
        for n, part in enumerate(PARTS):
            for i in range(GROUP):
                planes = [spread[i * PLANES + z, part, :] for z in range(PLANES)]
                planes = swap_quarters(planes, lane)
                for j in range(4):
                    at = j * ROWS + group * GROUP + i
                    beginning = planes[j] * inv_mass[part]
                    start_ref[at, part, :] = beginning
                    conc_ref[at, part, :] = beginning
                    if n == 2:
                        heat = jnp.broadcast_to(planes[j][SPECIES - 16 : SPECIES - 15, :], sub.shape)
                        inverse = 1.0 / jnp.maximum(heat, SMALLEST)
                        high = coarse(inverse)
                        ext_ref[at, :8, :] = jnp.where(
                            heat_row,
                            high,
                            jnp.where(sub == SPECIES - 15, inverse - high, 1.0),
                        )
                        ext_ref[at, 8:, :] = jnp.where(heat_row, high, 1.0)

    def second_rows(group, carry):
        pack(jnp.maximum(group - 1, 0))
        for part in PARTS:
            kept = lambda i, z, part: flux[z * HROWS + group * GROUP + i + 2, part, :]
            for i, planes in enumerate(group_rows(first, coef, kept, edge_flux, group, part)):
                for z, (value, total) in enumerate(planes):
                    spread[i * PLANES + z, part, :] = value + step * total
        return carry

    for i in range(GROUP * PLANES):
        spread[i] = jnp.ones((SUB, LANES), f32)
    lax.fori_loop(0, ROWS // GROUP, second_rows, 0)
    pack(ROWS // GROUP - 1)

    log_table = log_table_ref[:, : 2 * SUB].astype(bf16)
    sum_table = sum_table_ref[:, : 2 * RPAD].astype(bf16)
    spare = sub >= SPECIES - 16
    mass = scales[1]
    heat_mass = scales[2] * mass

    def box(p, j):
        base = j * ROWS + p * BOX
        chunks = BOX // BOX_CHUNK

        def rates(chunk):
            at = [base + chunk * BOX_CHUNK + i for i in range(BOX_CHUNK)]
            conc = jnp.concatenate([conc_ref[i] for i in at], axis=1)
            spare_rows = jnp.concatenate([spare] * BOX_CHUNK, axis=1)
            ext = jnp.concatenate([ext_ref[i] for i in at], axis=1)
            logs = jnp.log2(conc)
            high = coarse(logs)
            low = logs - high
            stacked = jnp.concatenate(
                [
                    high[:16],
                    jnp.where(spare_rows, ext[:8], high[16:]),
                    low[:16],
                    jnp.where(spare_rows, ext[8:], low[16:]),
                ],
                axis=0,
            ).astype(bf16)
            return jnp.dot(log_table, stacked, preferred_element_type=f32)

        def advance(chunk, exponent):
            at = [base + chunk * BOX_CHUNK + i for i in range(BOX_CHUNK)]
            progress = jnp.exp2(exponent)
            high = coarse(progress)
            stacked = jnp.concatenate([high, progress - high], axis=0).astype(bf16)
            sums = jnp.dot(sum_table, stacked, preferred_element_type=f32)
            conc = jnp.concatenate([conc_ref[i] for i in at], axis=1)
            start = jnp.concatenate([start_ref[i] for i in at], axis=1)
            conc = (start + sums[:SUB, :]) * (conc / (conc + sums[SUB:, :]))
            for n, i in enumerate(at):
                conc_ref[i] = conc[:, n * LANES : (n + 1) * LANES]

        def sweep(number, inner):
            ahead = [rates(chunk) for chunk in range(AHEAD)]
            for chunk in range(chunks):
                if chunk + AHEAD < chunks:
                    ahead.append(rates(chunk + AHEAD))
                advance(chunk, ahead.pop(0))
            return inner

        lax.fori_loop(0, box_cost[p, j], sweep, 0)

    def give(p, flags, x, carry):
        planes = []
        for j in range(4):
            conc, start = conc_ref[j * ROWS + x], start_ref[j * ROWS + x]
            advanced = conc * mass
            source = jnp.sum(heat_mass * (conc - start), axis=0, keepdims=True)
            heat = start[16:, :] + jnp.broadcast_to(flags[j] * source, sub.shape)
            planes.append(
                [advanced[:8], advanced[8:16], jnp.where(heat_row, heat, advanced[16:])]
            )
        for n, part in enumerate(PARTS):
            for z, value in enumerate(swap_quarters([plane[n] for plane in planes], lane)):
                out_rows[z, x, part, :] = value
        return carry

    quarter = BOX // 2
    for p in range(2):
        for j in range(4):
            box(p, j)
        flags = [flame_flag[p, j].astype(f32) for j in range(4)]
        for n in range(2):
            begin = p * BOX + n * quarter
            rows = pl.ds(begin, quarter)
            lax.fori_loop(
                begin, begin + quarter, functools.partial(give, p, flags), 0, unroll=4
            )
            for k in range(FIELDS):
                pltpu.make_async_copy(
                    out_rows.at[:, rows, k], out.at[k, :, rows], out_sem.at[p]
                ).start()
    for p in range(2):
        whole = out.at[:, :, pl.ds(p * BOX, BOX)]
        pltpu.make_async_copy(whole, whole, out_sem.at[p]).wait()


def substep(box_cost, flame_flag, *operands):
    vmem = pl.BlockSpec(memory_space=pltpu.VMEM)
    smem = pl.BlockSpec(memory_space=pltpu.SMEM)
    hbm = pl.BlockSpec(memory_space=pl.ANY)
    rows = lambda n: pltpu.VMEM((n, SUB, LANES), f32)
    return pl.pallas_call(
        substep_kernel,
        in_specs=[smem, smem, hbm, hbm] + [vmem] * (len(operands) - 2),
        out_specs=[hbm, smem],
        out_shape=[
            jax.ShapeDtypeStruct((FIELDS, PLANES, ROWS, LANES), f32),
            jax.ShapeDtypeStruct((1, 1), f32),
        ],
        scratch_shapes=[
            rows(PLANES * HROWS),
            rows(PLANES * HROWS),
            rows(PLANES * HROWS),
            rows(32),
            rows(32),
            rows(32),
            rows(8),
            rows(4),
            rows(PLANES * HROWS),
            rows(GROUP * PLANES),
            rows(PLANES * ROWS),
            rows(PLANES * ROWS),
            pltpu.VMEM((PLANES * ROWS, 16, LANES), f32),
            pltpu.VMEM((PLANES, ROWS, SUB, LANES), f32),
            pltpu.SemaphoreType.DMA((2, 2)),
            pltpu.SemaphoreType.DMA((2,)),
        ],
        compiler_params=pltpu.CompilerParams(vmem_limit_bytes=VMEM_BYTES),
    )(box_cost, flame_flag, *operands)


def shifted(x, axis, by):
    count = lax.axis_size(axis)
    return lax.ppermute(x, axis, [(i, (i + by) % count) for i in range(count)])


def per_device(
    state,
    masses,
    reciprocals,
    rate_scale,
    energy,
    reactants,
    products,
    heat_release,
    box_cost,
    box_owner,
    flame_flag,
):
    field, low, high, own, to_left, to_right, *constants = edges(
        state.reshape(FIELDS, PLANES * ROWS, LANES),
        masses.reshape(1, -1),
        reciprocals,
        rate_scale.reshape(1, -1),
        energy.reshape(1, -1),
        reactants.T,
        products.T,
    )
    below = shifted(high, "gx", 1)
    above = shifted(low, "gx", -1)
    left = shifted(to_right, "gy", 1)
    right = shifted(to_left, "gy", -1)
    message, coef = local_peak(box_cost, box_owner, field, constants[0], constants[1])
    total = first_divergence(
        field, coef, below, above, left, right, own, constants[0], constants[1]
    )
    gathered = lax.all_to_all(message, ("gx", "gy"), 0, 0, tiled=True)
    heat = jnp.pad(heat_release, (0, SUB - SPECIES))[:, None]
    heat = jnp.broadcast_to(heat, (1, SUB, LANES))
    constants[0] = jnp.concatenate([constants[0], heat], axis=0)
    return tuple(
        substep(
            box_cost,
            flame_flag,
            field,
            total,
            below,
            above,
            left,
            right,
            own,
            gathered,
            *constants,
        )
    )


def solution(mesh):
    split = P("gx", "gy")
    whole = P(None, None, "gx", "gy")
    return jax.shard_map(
        per_device,
        mesh=mesh,
        in_specs=(whole, P(), P(), P(), P(), P(), P(), P(), split, split, split),
        out_specs=(whole, split),
        check_vma=False,
    )
```

```python
import functools

import jax
import jax.numpy as jnp
from jax import lax
from jax.experimental import pallas as pl
from jax.experimental.pallas import tpu as pltpu
from jax.sharding import PartitionSpec as P

SPECIES = 21
FIELDS = 22
SUB = 24
LANES = 128
PLANES = 4
ROWS = 64
HROWS = ROWS + 4
BOX = 32
REACTIONS = 84
RPAD = 88
CHUNK = 4
BOX_CHUNK = 4
GROUP = 2
WIDE = 4
SMALLEST = 1e-30
LONG = 16
AHEAD = 4
LOG2E = 1.4426950408889634
Z_WEIGHT = 0.25
CFL_SAFE = 0.5
HALF = 0.5
VMEM_BYTES = 56 * 1024 * 1024

PARTS = [slice(0, 8), slice(8, 16), slice(16, 24)]

f32 = jnp.float32
bf16 = jnp.bfloat16


def live_rows():
    return (lax.broadcasted_iota(jnp.int32, (SUB, LANES), 0) < SPECIES).astype(f32)


def fill_spare(rows, count):
    def body(i, carry):
        rows[i, FIELDS:SUB, :] = jnp.ones((SUB - FIELDS, LANES), f32)
        return carry

    lax.fori_loop(0, count, body, 0, unroll=8)


def coarse(x):
    return x.astype(bf16).astype(f32)


def diffusivity(rows, inv_mass, table, live):
    amounts = jnp.concatenate([row * inv_mass for row in rows], axis=1)
    high = coarse(amounts)
    low = amounts - high
    blank = jnp.zeros((8, amounts.shape[1]), f32)
    stacked = jnp.concatenate([high, low, high, blank], axis=0).astype(bf16)
    sums = jnp.dot(table, stacked, preferred_element_type=f32)
    result = []
    for i, row in enumerate(rows):
        lanes = slice(i * LANES, (i + 1) * LANES)
        heat = row[SPECIES : SPECIES + 1, :]
        scale = (HALF * heat * jnp.sqrt(heat)) * sums[SUB : SUB + 8, lanes]
        scale = jnp.concatenate([scale] * 3, axis=0)
        result.append(live * (1.0 - row) * scale / sums[:SUB, lanes])
    return result


def split3(x):
    high = coarse(x)
    middle = coarse(x - high)
    return high, middle, coarse((x - high) - middle)


def fill_tables(
    masses,
    reciprocals,
    rate_scale,
    energy,
    reactants,
    products,
    scales,
    table,
    log_table,
    sum_table,
    square,
):
    lane = lax.broadcasted_iota(jnp.int32, (LANES, LANES), 1)
    row = lax.broadcasted_iota(jnp.int32, (LANES, LANES), 0)

    def padded(value, filler=0.0):
        square[...] = jnp.full((LANES, LANES), filler, f32)
        square[: value.shape[0], : value.shape[1]] = value
        return square[...]

    def column(ref, filler):
        return jnp.broadcast_to(padded(ref[...], filler)[:1], (LANES, LANES)).T

    mass = column(masses, 1.0)[:SUB]
    scales[0] = 1.0 / mass
    scales[1] = mass

    cross = padded(reciprocals[...])
    cross = jnp.where(row == lane, 0.0, cross).T
    cross = jnp.where(lane < SPECIES, jnp.where(row < SPECIES, cross, 1.0), 0.0)[: SUB + 8]
    high = coarse(cross)
    table[...] = high + pltpu.roll(high, SUB, 1) + pltpu.roll(cross - high, 2 * SUB, 1)

    react_back = padded(reactants[...].astype(f32))
    react = react_back.T
    eh, em, _ = split3((-LOG2E) * column(energy, 0.0)[:RPAD])
    ah, am, al = split3(jnp.log2(column(rate_scale, 1.0)[:RPAD]))
    place = lane[:RPAD]
    ext = jnp.zeros((RPAD, LANES), f32)
    spare = (SPECIES, SPECIES + 1, SPECIES + 2)
    for n, value in zip(spare + tuple(SUB + n for n in spare), (eh, eh, ah, em, am, al)):
        ext = jnp.where(place == n, value, ext)
    log_table[...] = react[:RPAD] + pltpu.roll(react[:RPAD], SUB, 1) + ext

    make = padded(products[...].astype(f32))[:SUB]
    sums = HALF * jnp.concatenate([make, react_back[:SUB]], axis=0)
    moved = pltpu.roll(sums, RPAD, 1)
    place = lane[: 2 * SUB]
    sum_table[:, :LANES] = jnp.where(place < RPAD, sums, moved)
    sum_table[:, LANES:] = jnp.where(place < 2 * RPAD - LANES, moved, 0.0)


def edges_kernel(
    state,
    masses,
    reciprocals,
    rate_scale,
    energy,
    reactants,
    products,
    field_out,
    low,
    high,
    own,
    to_left,
    to_right,
    scales,
    table,
    log_table,
    sum_table,
    field,
    square,
    in_sem,
    out_sem,
):
    def half_rows(half):
        return pl.ds(half * 2 * ROWS, 2 * ROWS)

    def keep(half):
        rows = half_rows(half)
        return pltpu.make_async_copy(field.at[rows], field_out.at[rows], out_sem.at[half])

    for half in range(2):
        rows = half_rows(half)
        for k in range(FIELDS):
            pltpu.make_async_copy(state.at[k, rows], field.at[rows, k], in_sem.at[half]).start()
    fill_spare(field, PLANES * ROWS)
    fill_tables(
        masses,
        reciprocals,
        rate_scale,
        energy,
        reactants,
        products,
        scales,
        table,
        log_table,
        sum_table,
        square,
    )
    lane = lax.broadcasted_iota(jnp.int32, (8, LANES), 1)
    for half in range(2):
        whole = state.at[:, half_rows(half)]
        pltpu.make_async_copy(whole, whole, in_sem.at[half]).wait()
        keep(half).start()
        planes = (2 * half, 2 * half + 1)
        for z in planes:
            for layer in range(2):
                low[z * 2 + layer] = field[z * ROWS + layer]
                high[z * 2 + layer] = field[z * ROWS + ROWS - 2 + layer]

        def gather(index, held):
            mine = (lane >> 2) == index
            result = []
            for z in planes:
                for group in range(2):
                    for part in PARTS:
                        row = field[z * ROWS + group * 32 + index, part, :]
                        turned = pltpu.roll(row, 4 * index + 2, 1)
                        result.append(jnp.where(mine, turned, held[len(result)]))
            return tuple(result)

        held = lax.fori_loop(0, 32, gather, (jnp.ones((8, LANES), f32),) * 12, unroll=2)
        for i, z in enumerate(planes):
            for n, part in enumerate(PARTS):
                for c in range(4):
                    index = (4 * lane + c) & (LANES - 1)
                    pick = lambda v: jnp.take_along_axis(v, index, axis=1, mode="promise_in_bounds")
                    value = jnp.where(
                        lane < 32, pick(held[i * 6 + n]), pick(held[i * 6 + 3 + n])
                    )
                    own[z * 4 + c, part, :] = value
                    side = to_right if c < 2 else to_left
                    side[z * 2 + c % 2, part, :] = value
    for half in range(2):
        keep(half).wait()


def edges(*operands):
    vmem = pl.BlockSpec(memory_space=pltpu.VMEM)
    hbm = pl.BlockSpec(memory_space=pl.ANY)
    rows = lambda n: jax.ShapeDtypeStruct((n, SUB, LANES), f32)
    return pl.pallas_call(
        edges_kernel,
        in_specs=[hbm] + [vmem] * 6,
        out_specs=[hbm] + [vmem] * 9,
        out_shape=[
            rows(PLANES * ROWS),
            rows(8),
            rows(8),
            rows(16),
            rows(8),
            rows(8),
            rows(2),
            jax.ShapeDtypeStruct((SUB + 8, LANES), f32),
            jax.ShapeDtypeStruct((RPAD, LANES), f32),
            jax.ShapeDtypeStruct((2 * SUB, 2 * LANES), f32),
        ],
        scratch_shapes=[
            pltpu.VMEM((PLANES * ROWS, SUB, LANES), f32),
            pltpu.VMEM((LANES, LANES), f32),
            pltpu.SemaphoreType.DMA((2,)),
            pltpu.SemaphoreType.DMA((2,)),
        ],
        compiler_params=pltpu.CompilerParams(vmem_limit_bytes=VMEM_BYTES),
    )(*operands)


def lane_flux(row, weight):
    onward = LANES - 1
    return (weight + pltpu.roll(weight, onward, 1)) * (pltpu.roll(row, onward, 1) - row)


def coefficient_step(source, target, flux, base, inv_mass, table, live):
    if flux is not None:
        before = jnp.maximum(base - LONG, 0)
        for i in range(LONG):
            flux[before + i] = lane_flux(source[before + i], target[before + i])
    result = []
    for n in range(0, LONG, CHUNK):
        at = [base + n + i for i in range(CHUNK)]
        values = diffusivity([source[i] for i in at], inv_mass, table, live)
        for i, value in zip(at, values):
            target[i] = value
        result += values
    return result


def peak_kernel(
    box_cost, box_owner, field_in, scales, table_ref, message, coef_out, field, coef, in_sem, out_sem
):
    quarter = lambda z: pl.ds(z * ROWS, ROWS)

    def fetch(z):
        return pltpu.make_async_copy(
            field_in.at[quarter(z)], field.at[quarter(z)], in_sem.at[z]
        )

    def keep(z):
        return pltpu.make_async_copy(coef.at[quarter(z)], coef_out.at[quarter(z)], out_sem.at[z])

    for z in range(PLANES):
        fetch(z).start()
    inv_mass = scales[0]
    live = live_rows()
    table = table_ref[:, : 3 * SUB + 8].astype(bf16)
    best = jnp.zeros((SUB, LANES), f32)
    for z in range(PLANES):
        fetch(z).wait()

        def body(index, best):
            at = [z * ROWS + index * CHUNK + i for i in range(CHUNK)]
            rows = [field[i] for i in at]
            for i, value in zip(at, diffusivity(rows, inv_mass, table, live)):
                coef[i] = value
                best = jnp.maximum(best, value)
            return best

        best = lax.fori_loop(0, ROWS // CHUNK, body, best, unroll=4)
        keep(z).start()
    top = 2.0 * jnp.max(best)
    device = lax.broadcasted_iota(jnp.int32, (LANES, LANES), 0)
    column = lax.broadcasted_iota(jnp.int32, (LANES, LANES), 1)
    nx, ny = lax.axis_size("gx"), lax.axis_size("gy")
    gx, gy = lax.axis_index("gx"), lax.axis_index("gy")
    same = device // ny == gx
    place = device % ny
    charged = jnp.zeros((LANES, LANES), f32)
    total = 0.0
    for p in range(2):
        for j in range(4):
            cost = box_cost[p, j].astype(f32)
            total = total + cost
            charged = charged + jnp.where(place == box_owner[p, j], cost, 0.0)
    tally = jnp.where(same, jnp.where(column == LANES - 2, charged, total), 0.0)
    corner = jnp.zeros((LANES, LANES), f32)
    for x, dx in ((0, nx - 1), (ROWS - 1, 1)):
        block = jnp.concatenate(
            [field[z * ROWS + x] for z in range(PLANES)]
            + [jnp.zeros((LANES - PLANES * SUB, LANES), f32)],
            axis=0,
        ).T
        for y, dy in ((0, ny - 1), (LANES - 1, 1)):
            there = lax.rem(gx + dx, nx) * ny + lax.rem(gy + dy, ny)
            cells = jnp.broadcast_to(block[y : y + 1], (LANES, LANES))
            corner = jnp.where(device == there, cells, corner)
    message[...] = jnp.where(
        column == LANES - 3, top, jnp.where(column > LANES - 3, tally, corner)
    )
    for z in range(PLANES):
        keep(z).wait()


def local_peak(box_cost, box_owner, field, scales, table):
    vmem = pl.BlockSpec(memory_space=pltpu.VMEM)
    smem = pl.BlockSpec(memory_space=pltpu.SMEM)
    hbm = pl.BlockSpec(memory_space=pl.ANY)
    rows = jax.ShapeDtypeStruct((PLANES * ROWS, SUB, LANES), f32)
    assert lax.axis_size("gx") * lax.axis_size("gy") == LANES
    return pl.pallas_call(
        peak_kernel,
        in_specs=[smem, smem, hbm, vmem, vmem],
        out_specs=[vmem, hbm],
        out_shape=[jax.ShapeDtypeStruct((LANES, LANES), f32), rows],
        scratch_shapes=[
            pltpu.VMEM((PLANES * ROWS, SUB, LANES), f32),
            pltpu.VMEM((PLANES * ROWS, SUB, LANES), f32),
            pltpu.SemaphoreType.DMA((PLANES,)),
            pltpu.SemaphoreType.DMA((PLANES,)),
        ],
        compiler_params=pltpu.CompilerParams(vmem_limit_bytes=VMEM_BYTES),
    )(box_cost, box_owner, field, scales, table)


def divergence_rows(source, weight, x0, count, part, onward, ends):
    lane = lax.broadcasted_iota(jnp.int32, (8, LANES), 1)
    result = [[] for _ in range(count)]
    above_flux = [None] * count
    for z in range(PLANES):
        base = z * HROWS + x0 + 1
        here = [source[base + i, part, :] for i in range(count + 2)]
        coefs = [weight[base + i, part, :] for i in range(count + 2)]
        along = [(coefs[i] + coefs[i + 1]) * (here[i + 1] - here[i]) for i in range(count + 1)]
        for i in range(count):
            c, d = here[i + 1], coefs[i + 1]
            raw, back = onward[i][z]
            entering, leaving = ends[i][z]
            total = (along[i + 1] - along[i]) + (
                jnp.where(lane == LANES - 1, leaving, raw) - jnp.where(lane == 0, entering, back)
            )
            if z < PLANES - 1:
                over = base + i + 1 + HROWS
                flux = Z_WEIGHT * ((d + weight[over, part, :]) * (source[over, part, :] - c))
                total = total + flux
            if z > 0:
                total = total - above_flux[i]
            if z < PLANES - 1:
                above_flux[i] = flux
            result[i].append((c, total))
    return result


def group_rows(source, weight, flux_at, edge_flux, group, part, count):
    x = group * count
    onward, ends = [], []
    for i in range(count):
        raws = [flux_at(i, z, part) for z in range(PLANES)]
        onward.append([(raw, pltpu.roll(raw, 1, 1)) for raw in raws])
        shift = (2 * LANES - 2 * (x + i)) & (LANES - 1)
        edges = [pltpu.roll(edge_flux[z, part, :], shift, 1) for z in range(PLANES)]
        ends.append([(edge, edge) for edge in edges])
    return divergence_rows(source, weight, x, count, part, onward, ends)


def interleaved(entering, leaving):
    lane = lax.broadcasted_iota(jnp.int32, (8, LANES), 1)
    pick = lambda v, at: jnp.take_along_axis(v, at, axis=1, mode="promise_in_bounds")
    return jnp.where(
        (lane & 1) == 1,
        pick(leaving, ((lane + 1) >> 1) & (ROWS - 1)),
        pick(entering, lane >> 1),
    )


def first_kernel(
    field_in,
    coef_in,
    below,
    above,
    left,
    right,
    own,
    scales,
    table_ref,
    out,
    field,
    coef,
    total,
    edge_flux,
    raw_flux,
    in_sem,
    out_sem,
):
    def fetch(p):
        copies = []
        for z in range(PLANES):
            held = pl.ds(z * ROWS + p * BOX, BOX)
            rows = pl.ds(z * HROWS + 2 + p * BOX, BOX)
            for n, (source, target) in enumerate(((field_in, field), (coef_in, coef))):
                copies.append(
                    pltpu.make_async_copy(source.at[held], target.at[rows], in_sem.at[p, n])
                )
        return copies

    part_way = BOX // WIDE - 1
    stages = (0, part_way, (part_way + ROWS // WIDE) // 2 + 1, ROWS // WIDE)

    def deliver(n):
        begin, end = stages[n] * WIDE, stages[n + 1] * WIDE
        rows = [pl.ds(z * ROWS + begin, end - begin) for z in range(PLANES)]
        return [pltpu.make_async_copy(total.at[r], out.at[r], out_sem.at[n]) for r in rows]

    for p in range(2):
        for copy in fetch(p):
            copy.start()
    inv_mass = scales[0]
    live = live_rows()
    table = table_ref[:, : 3 * SUB + 8].astype(bf16)
    for z in range(PLANES):
        at = [z * HROWS + 1, z * HROWS + ROWS + 2]
        halo = [below[z * 2 + 1], above[z * 2]]
        sides = [left[z * 2 + 1], own[z * 4 + 2], own[z * 4 + 1], right[z * 2]]
        coefs = diffusivity(halo + sides, inv_mass, table, live)
        for i, row, value in zip(at, halo, coefs):
            field[i] = row
            coef[i] = value
        entering = (coefs[2] + coefs[3]) * (sides[1] - sides[0])
        leaving = (coefs[4] + coefs[5]) * (sides[3] - sides[2])
        for part in PARTS:
            edge_flux[z, part, :] = interleaved(entering[part], leaving[part])

    def start_flux(group):
        for part in PARTS:
            for i in range(WIDE):
                for z in range(PLANES):
                    at = z * HROWS + group * WIDE + i + 2
                    raw_flux[i * PLANES + z, part, :] = lane_flux(
                        field[at, part, :], coef[at, part, :]
                    )

    def rows(group, carry):
        kept = lambda i, z, part: raw_flux[i * PLANES + z, part, :]
        for part in PARTS:
            for i, planes in enumerate(group_rows(field, coef, kept, edge_flux, group, part, WIDE)):
                for z, (_, value) in enumerate(planes):
                    total[z * ROWS + group * WIDE + i, part, :] = value
        start_flux(jnp.minimum(group + 1, ROWS // WIDE - 1))
        return carry

    for copy in fetch(0):
        copy.wait()
    start_flux(0)
    for n in range(3):
        if n == 1:
            for copy in fetch(1):
                copy.wait()
        lax.fori_loop(stages[n], stages[n + 1], rows, 0)
        for copy in deliver(n):
            copy.start()
    for n in range(3):
        for copy in deliver(n):
            copy.wait()


def first_divergence(*operands):
    vmem = pl.BlockSpec(memory_space=pltpu.VMEM)
    hbm = pl.BlockSpec(memory_space=pl.ANY)
    rows = lambda n: pltpu.VMEM((n, SUB, LANES), f32)
    return pl.pallas_call(
        first_kernel,
        in_specs=[hbm, hbm] + [vmem] * 7,
        out_specs=hbm,
        out_shape=jax.ShapeDtypeStruct((PLANES * ROWS, SUB, LANES), f32),
        scratch_shapes=[
            rows(PLANES * HROWS),
            rows(PLANES * HROWS),
            rows(PLANES * ROWS),
            rows(PLANES),
            rows(WIDE * PLANES),
            pltpu.SemaphoreType.DMA((2, 2)),
            pltpu.SemaphoreType.DMA((3,)),
        ],
        compiler_params=pltpu.CompilerParams(vmem_limit_bytes=VMEM_BYTES),
    )(*operands)


def swap_quarters(planes, lane):
    low_half = lane < 64
    even = ((lane >> 5) & 1) == 0
    a, b, c, d = planes
    a, c = (
        jnp.where(low_half, a, pltpu.roll(c, 64, 1)),
        jnp.where(low_half, pltpu.roll(a, 64, 1), c),
    )
    b, d = (
        jnp.where(low_half, b, pltpu.roll(d, 64, 1)),
        jnp.where(low_half, pltpu.roll(b, 64, 1), d),
    )
    a, b = (
        jnp.where(even, a, pltpu.roll(b, 32, 1)),
        jnp.where(even, pltpu.roll(a, 96, 1), b),
    )
    c, d = (
        jnp.where(even, c, pltpu.roll(d, 32, 1)),
        jnp.where(even, pltpu.roll(c, 96, 1), d),
    )
    return [a, b, c, d]


def substep_kernel(
    box_cost,
    flame_flag,
    field_in,
    total_in,
    below,
    above,
    left,
    right,
    own,
    gathered,
    scales,
    table_ref,
    log_table_ref,
    sum_table_ref,
    out,
    load_out,
    field,
    coef,
    first,
    strip_field,
    strip_coef,
    strip_first,
    fluxes,
    edge_flux,
    flux,
    spread,
    start_ref,
    conc_ref,
    ext_ref,
    out_rows,
    in_sem,
    out_sem,
):
    def fetch(p):
        copies = []
        for z in range(PLANES):
            held = pl.ds(z * ROWS + p * BOX, BOX)
            rows = pl.ds(z * HROWS + 2 + p * BOX, BOX)
            for n, (source, target) in enumerate(
                ((field_in, field), (total_in, first))
            ):
                copies.append(
                    pltpu.make_async_copy(source.at[held], target.at[rows], in_sem.at[p, n])
                )
        return copies

    for p in range(2):
        for copy in fetch(p):
            copy.start()
    inv_mass = scales[0]
    live = live_rows()
    table = table_ref[:, : 3 * SUB + 8].astype(bf16)
    lane = lax.broadcasted_iota(jnp.int32, (8, LANES), 1)
    received = gathered[...]
    columns = lax.broadcasted_iota(jnp.int32, received.shape, 1)
    peak = jnp.max(jnp.where(columns == LANES - 3, received, 0.0), keepdims=True)
    step = CFL_SAFE / ((4.0 + 2.0 * Z_WEIGHT) * peak)
    mine = jnp.sum(jnp.where(columns == LANES - 2, received, 0.0))
    everyone = jnp.sum(jnp.where(columns == LANES - 1, received, 0.0))
    load_out[0, 0] = mine / (everyone / 16.0)
    step = jnp.broadcast_to(step, (8, LANES))

    nx, ny = lax.axis_size("gx"), lax.axis_size("gy")

    def outside(dy):
        cells = []
        for dx in (1, nx - 1):
            source = lax.rem(lax.axis_index("gx") + dx, nx) * ny
            source = source + lax.rem(lax.axis_index("gy") + dy, ny)
            cells.append(jnp.broadcast_to(gathered[pl.ds(source, 1), :], received.shape))
        rows = lax.broadcasted_iota(jnp.int32, received.shape, 0)
        return jnp.where(rows == ROWS, cells[0], cells[1]).T

    corners = [outside(ny - 1), outside(1)]
    tips = (lane == ROWS) | (lane == LANES - 1)

    for z in range(PLANES):
        for layer in range(2):
            field[z * HROWS + layer] = below[z * 2 + layer]
            field[z * HROWS + ROWS + 2 + layer] = above[z * 2 + layer]
        for c in range(2):
            strip_field[z * 8 + c] = left[z * 2 + c]
            strip_field[z * 8 + 2 + c] = own[z * 4 + 2 + c]
            strip_field[z * 8 + 4 + c] = own[z * 4 + c]
            strip_field[z * 8 + 6 + c] = right[z * 2 + c]
        for n, part in enumerate(PARTS):
            rows = slice(z * SUB + n * 8, z * SUB + n * 8 + 8)
            for r, cells in ((1, corners[0]), (6, corners[1])):
                strip_field[z * 8 + r, part, :] = jnp.where(
                    tips, cells[rows], strip_field[z * 8 + r, part, :]
                )
            before = below[z * 2 + 1, part, :]
            after = above[z * 2, part, :]
            for r, column in ((2, 0), (5, LANES - 1)):
                strip_field[z * 8 + r, part, :] = jnp.where(
                    lane == LANES - 1,
                    pltpu.roll(before, LANES - 1 - column, 1),
                    jnp.where(
                        lane == ROWS,
                        pltpu.roll(after, (ROWS - column) % LANES, 1),
                        strip_field[z * 8 + r, part, :],
                    ),
                )

    def coefficients(source, target, count, kept):
        def body(index, carry):
            coefficient_step(source, target, kept, index * LONG, inv_mass, table, live)
            return carry

        lax.fori_loop(0, count // LONG, body, 0)
        if kept is not None:
            for i in range(count - LONG, count):
                kept[i] = lane_flux(source[i], target[i])

    def face(source, weight, here, there, part):
        return (weight[here, part, :] + weight[there, part, :]) * (
            source[there, part, :] - source[here, part, :]
        )

    def side_fluxes(source, weight):
        for z in range(PLANES):
            for part in PARTS:
                entering = face(source, weight, z * 8 + 1, z * 8 + 2, part)
                leaving = face(source, weight, z * 8 + 5, z * 8 + 6, part)
                fluxes[z * 2, part, :] = entering
                fluxes[z * 2 + 1, part, :] = leaving
                edge_flux[z, part, :] = interleaved(entering, leaving)

    def strip_update():
        for r in (1, 2, 5, 6):
            for part in PARTS:
                above_flux = None
                for z in range(PLANES):
                    at = z * 8 + r
                    here = strip_field[at, part, :]
                    weight = strip_coef[at, part, :]
                    total = face(strip_field, strip_coef, at, at + 1, part)
                    total = total - face(strip_field, strip_coef, at - 1, at, part)
                    onward = (weight + pltpu.roll(weight, LANES - 1, 1)) * (
                        pltpu.roll(here, LANES - 1, 1) - here
                    )
                    total = total + (onward - pltpu.roll(onward, 1, 1))
                    if above_flux is not None:
                        total = total - Z_WEIGHT * above_flux
                    if z < PLANES - 1:
                        above_flux = face(strip_field, strip_coef, at, at + 8, part)
                        total = total + Z_WEIGHT * above_flux
                    strip_first[at, part, :] = here + step * total

    def outer_row(source, weight, x, part):
        shift = -x % LANES
        onward, ends = [], []
        for z in range(PLANES):
            at = z * HROWS + x + 2
            raw = lane_flux(source[at, part, :], weight[at, part, :])
            onward.append((raw, pltpu.roll(raw, 1, 1)))
            ends.append(
                (
                    pltpu.roll(fluxes[z * 2, part, :], shift, 1),
                    pltpu.roll(fluxes[z * 2 + 1, part, :], (shift + LANES - 1) % LANES, 1),
                )
            )
        return divergence_rows(source, weight, x, 1, part, [onward], [ends])[0]

    coefficients(strip_field, strip_coef, PLANES * 8, None)
    side_fluxes(strip_field, strip_coef)
    strip_update()
    for p in range(2):
        for copy in fetch(p):
            copy.wait()
    for z in range(PLANES):
        at = [z * HROWS + x for x in (0, 1, 2, ROWS + 1, ROWS + 2, ROWS + 3)]
        for i, value in zip(at, diffusivity([field[i] for i in at], inv_mass, table, live)):
            coef[i] = value
    for x in (-1, ROWS):
        for part in PARTS:
            for z, (value, total) in enumerate(outer_row(field, coef, x, part)):
                first[z * HROWS + x + 2, part, :] = value + step * total
    wide_step = jnp.concatenate([step] * 3, axis=0)

    def first_rows(x, carry):
        for z in range(PLANES):
            at = z * HROWS + 2 + x
            first[at] = field[at] + wide_step * first[at]
        return carry

    lax.fori_loop(0, ROWS, first_rows, 0, unroll=4)
    for z in range(PLANES):
        first[z * HROWS] = field[z * HROWS]
        first[z * HROWS + HROWS - 1] = field[z * HROWS + HROWS - 1]
        for r in (0, 3, 4, 7):
            strip_first[z * 8 + r] = strip_field[z * 8 + r]
    coefficients(strip_first, strip_coef, PLANES * 8, None)
    side_fluxes(strip_first, strip_coef)
    coefficients(first, coef, PLANES * HROWS, flux)

    sub = lax.broadcasted_iota(jnp.int32, (8, LANES), 0)
    heat_row = sub == SPECIES - 16

    def pack(group):
        for n, part in enumerate(PARTS):
            for i in range(GROUP):
                planes = [spread[i * PLANES + z, part, :] for z in range(PLANES)]
                planes = swap_quarters(planes, lane)
                for j in range(4):
                    at = j * ROWS + group * GROUP + i
                    beginning = planes[j] * inv_mass[part]
                    start_ref[at, part, :] = beginning
                    conc_ref[at, part, :] = beginning
                    if n == 2:
                        heat = jnp.broadcast_to(planes[j][SPECIES - 16 : SPECIES - 15, :], sub.shape)
                        inverse = 1.0 / jnp.maximum(heat, SMALLEST)
                        high = coarse(inverse)
                        ext_ref[at, :8, :] = jnp.where(
                            heat_row,
                            high,
                            jnp.where(sub == SPECIES - 15, inverse - high, 1.0),
                        )
                        ext_ref[at, 8:, :] = jnp.where(heat_row, high, 1.0)

    def second_rows(group, carry):
        pack(jnp.maximum(group - 1, 0))
        for part in PARTS:
            kept = lambda i, z, part: flux[z * HROWS + group * GROUP + i + 2, part, :]
            rows = group_rows(first, coef, kept, edge_flux, group, part, GROUP)
            for i, planes in enumerate(rows):
                for z, (value, total) in enumerate(planes):
                    spread[i * PLANES + z, part, :] = value + step * total
        return carry

    for i in range(GROUP * PLANES):
        spread[i] = jnp.ones((SUB, LANES), f32)
    lax.fori_loop(0, ROWS // GROUP, second_rows, 0)
    pack(ROWS // GROUP - 1)

    log_table = log_table_ref[:, : 2 * SUB].astype(bf16)
    sum_table = sum_table_ref[:, : 2 * RPAD].astype(bf16)
    spare = sub >= SPECIES - 16
    mass = scales[1]
    heat_mass = scales[2] * mass

    def box(p, j):
        base = j * ROWS + p * BOX
        chunks = BOX // BOX_CHUNK

        def rates(chunk):
            at = [base + chunk * BOX_CHUNK + i for i in range(BOX_CHUNK)]
            conc = jnp.concatenate([conc_ref[i] for i in at], axis=1)
            spare_rows = jnp.concatenate([spare] * BOX_CHUNK, axis=1)
            ext = jnp.concatenate([ext_ref[i] for i in at], axis=1)
            logs = jnp.log2(conc)
            high = coarse(logs)
            low = logs - high
            stacked = jnp.concatenate(
                [
                    high[:16],
                    jnp.where(spare_rows, ext[:8], high[16:]),
                    low[:16],
                    jnp.where(spare_rows, ext[8:], low[16:]),
                ],
                axis=0,
            ).astype(bf16)
            return jnp.dot(log_table, stacked, preferred_element_type=f32)

        def advance(chunk, exponent):
            at = [base + chunk * BOX_CHUNK + i for i in range(BOX_CHUNK)]
            progress = jnp.exp2(exponent)
            high = coarse(progress)
            stacked = jnp.concatenate([high, progress - high], axis=0).astype(bf16)
            sums = jnp.dot(sum_table, stacked, preferred_element_type=f32)
            conc = jnp.concatenate([conc_ref[i] for i in at], axis=1)
            start = jnp.concatenate([start_ref[i] for i in at], axis=1)
            conc = (start + sums[:SUB, :]) * (conc / (conc + sums[SUB:, :]))
            for n, i in enumerate(at):
                conc_ref[i] = conc[:, n * LANES : (n + 1) * LANES]

        def sweep(number, inner):
            ahead = [rates(chunk) for chunk in range(AHEAD)]
            for chunk in range(chunks):
                if chunk + AHEAD < chunks:
                    ahead.append(rates(chunk + AHEAD))
                advance(chunk, ahead.pop(0))
            return inner

        lax.fori_loop(0, box_cost[p, j], sweep, 0)

    def give(p, flags, x, carry):
        planes = []
        for j in range(4):
            conc, start = conc_ref[j * ROWS + x], start_ref[j * ROWS + x]
            advanced = conc * mass
            source = jnp.sum(heat_mass * (conc - start), axis=0, keepdims=True)
            heat = start[16:, :] + jnp.broadcast_to(flags[j] * source, sub.shape)
            planes.append(
                [advanced[:8], advanced[8:16], jnp.where(heat_row, heat, advanced[16:])]
            )
        for n, part in enumerate(PARTS):
            for z, value in enumerate(swap_quarters([plane[n] for plane in planes], lane)):
                out_rows[z, x, part, :] = value
        return carry

    quarter = BOX // 2
    for p in range(2):
        for j in range(4):
            box(p, j)
        flags = [flame_flag[p, j].astype(f32) for j in range(4)]
        for n in range(2):
            begin = p * BOX + n * quarter
            rows = pl.ds(begin, quarter)
            lax.fori_loop(
                begin, begin + quarter, functools.partial(give, p, flags), 0, unroll=4
            )
            for k in range(FIELDS):
                pltpu.make_async_copy(
                    out_rows.at[:, rows, k], out.at[k, :, rows], out_sem.at[p]
                ).start()
    for p in range(2):
        whole = out.at[:, :, pl.ds(p * BOX, BOX)]
        pltpu.make_async_copy(whole, whole, out_sem.at[p]).wait()


def substep(box_cost, flame_flag, *operands):
    vmem = pl.BlockSpec(memory_space=pltpu.VMEM)
    smem = pl.BlockSpec(memory_space=pltpu.SMEM)
    hbm = pl.BlockSpec(memory_space=pl.ANY)
    rows = lambda n: pltpu.VMEM((n, SUB, LANES), f32)
    return pl.pallas_call(
        substep_kernel,
        in_specs=[smem, smem, hbm, hbm] + [vmem] * (len(operands) - 2),
        out_specs=[hbm, smem],
        out_shape=[
            jax.ShapeDtypeStruct((FIELDS, PLANES, ROWS, LANES), f32),
            jax.ShapeDtypeStruct((1, 1), f32),
        ],
        scratch_shapes=[
            rows(PLANES * HROWS),
            rows(PLANES * HROWS),
            rows(PLANES * HROWS),
            rows(32),
            rows(32),
            rows(32),
            rows(8),
            rows(4),
            rows(PLANES * HROWS),
            rows(GROUP * PLANES),
            rows(PLANES * ROWS),
            rows(PLANES * ROWS),
            pltpu.VMEM((PLANES * ROWS, 16, LANES), f32),
            pltpu.VMEM((PLANES, ROWS, SUB, LANES), f32),
            pltpu.SemaphoreType.DMA((2, 2)),
            pltpu.SemaphoreType.DMA((2,)),
        ],
        compiler_params=pltpu.CompilerParams(vmem_limit_bytes=VMEM_BYTES),
    )(box_cost, flame_flag, *operands)


def shifted(x, axis, by):
    count = lax.axis_size(axis)
    return lax.ppermute(x, axis, [(i, (i + by) % count) for i in range(count)])


def per_device(
    state,
    masses,
    reciprocals,
    rate_scale,
    energy,
    reactants,
    products,
    heat_release,
    box_cost,
    box_owner,
    flame_flag,
):
    field, low, high, own, to_left, to_right, *constants = edges(
        state.reshape(FIELDS, PLANES * ROWS, LANES),
        masses.reshape(1, -1),
        reciprocals,
        rate_scale.reshape(1, -1),
        energy.reshape(1, -1),
        reactants.T,
        products.T,
    )
    below = shifted(high, "gx", 1)
    above = shifted(low, "gx", -1)
    left = shifted(to_right, "gy", 1)
    right = shifted(to_left, "gy", -1)
    message, coef = local_peak(box_cost, box_owner, field, constants[0], constants[1])
    total = first_divergence(
        field, coef, below, above, left, right, own, constants[0], constants[1]
    )
    gathered = lax.all_to_all(message, ("gx", "gy"), 0, 0, tiled=True)
    heat = jnp.pad(heat_release, (0, SUB - SPECIES))[:, None]
    heat = jnp.broadcast_to(heat, (1, SUB, LANES))
    constants[0] = jnp.concatenate([constants[0], heat], axis=0)
    return tuple(
        substep(
            box_cost,
            flame_flag,
            field,
            total,
            below,
            above,
            left,
            right,
            own,
            gathered,
            *constants,
        )
    )


def solution(mesh):
    split = P("gx", "gy")
    whole = P(None, None, "gx", "gy")
    return jax.shard_map(
        per_device,
        mesh=mesh,
        in_specs=(whole, P(), P(), P(), P(), P(), P(), P(), split, split, split),
        out_specs=(whole, split),
        check_vma=False,
    )
```

```python
import functools

import jax
import jax.numpy as jnp
from jax import lax
from jax.experimental import pallas as pl
from jax.experimental.pallas import tpu as pltpu
from jax.sharding import PartitionSpec as P

SPECIES = 21
FIELDS = 22
SUB = 24
LANES = 128
PLANES = 4
ROWS = 64
HROWS = ROWS + 4
BOX = 32
REACTIONS = 84
RPAD = 88
CHUNK = 4
BOX_CHUNK = 4
GROUP = 2
WIDE = 4
SMALLEST = 1e-30
LONG = 16
AHEAD = 4
LOG2E = 1.4426950408889634
Z_WEIGHT = 0.25
CFL_SAFE = 0.5
HALF = 0.5
VMEM_BYTES = 56 * 1024 * 1024

PARTS = [slice(0, 8), slice(8, 16), slice(16, 24)]

f32 = jnp.float32
bf16 = jnp.bfloat16


def live_rows():
    return (lax.broadcasted_iota(jnp.int32, (SUB, LANES), 0) < SPECIES).astype(f32)


def fill_spare(rows, count):
    def body(i, carry):
        rows[i, FIELDS:SUB, :] = jnp.ones((SUB - FIELDS, LANES), f32)
        return carry

    lax.fori_loop(0, count, body, 0, unroll=8)


def coarse(x):
    return x.astype(bf16).astype(f32)


def diffusivity(rows, inv_mass, table, live):
    amounts = jnp.concatenate([row * inv_mass for row in rows], axis=1)
    high = coarse(amounts)
    low = amounts - high
    blank = jnp.zeros((8, amounts.shape[1]), f32)
    stacked = jnp.concatenate([high, low, high, blank], axis=0).astype(bf16)
    sums = jnp.dot(table, stacked, preferred_element_type=f32)
    result = []
    for i, row in enumerate(rows):
        lanes = slice(i * LANES, (i + 1) * LANES)
        heat = row[SPECIES : SPECIES + 1, :]
        scale = (HALF * heat * jnp.sqrt(heat)) * sums[SUB : SUB + 8, lanes]
        scale = jnp.concatenate([scale] * 3, axis=0)
        result.append(live * (1.0 - row) * scale / sums[:SUB, lanes])
    return result


def split3(x):
    high = coarse(x)
    middle = coarse(x - high)
    return high, middle, coarse((x - high) - middle)


def fill_tables(
    masses,
    reciprocals,
    rate_scale,
    energy,
    reactants,
    products,
    scales,
    table,
    log_table,
    sum_table,
    square,
):
    lane = lax.broadcasted_iota(jnp.int32, (LANES, LANES), 1)
    row = lax.broadcasted_iota(jnp.int32, (LANES, LANES), 0)

    def padded(value, filler=0.0):
        square[...] = jnp.full((LANES, LANES), filler, f32)
        square[: value.shape[0], : value.shape[1]] = value
        return square[...]

    def column(ref, filler):
        return jnp.broadcast_to(padded(ref[...], filler)[:1], (LANES, LANES)).T

    mass = column(masses, 1.0)[:SUB]
    scales[0] = 1.0 / mass
    scales[1] = mass

    cross = padded(reciprocals[...])
    cross = jnp.where(row == lane, 0.0, cross).T
    cross = jnp.where(lane < SPECIES, jnp.where(row < SPECIES, cross, 1.0), 0.0)[: SUB + 8]
    high = coarse(cross)
    table[...] = high + pltpu.roll(high, SUB, 1) + pltpu.roll(cross - high, 2 * SUB, 1)

    react_back = padded(reactants[...].astype(f32))
    react = react_back.T
    eh, em, _ = split3((-LOG2E) * column(energy, 0.0)[:RPAD])
    ah, am, al = split3(jnp.log2(column(rate_scale, 1.0)[:RPAD]))
    place = lane[:RPAD]
    ext = jnp.zeros((RPAD, LANES), f32)
    spare = (SPECIES, SPECIES + 1, SPECIES + 2)
    for n, value in zip(spare + tuple(SUB + n for n in spare), (eh, eh, ah, em, am, al)):
        ext = jnp.where(place == n, value, ext)
    log_table[...] = react[:RPAD] + pltpu.roll(react[:RPAD], SUB, 1) + ext

    make = padded(products[...].astype(f32))[:SUB]
    sums = HALF * jnp.concatenate([make, react_back[:SUB]], axis=0)
    moved = pltpu.roll(sums, RPAD, 1)
    place = lane[: 2 * SUB]
    sum_table[:, :LANES] = jnp.where(place < RPAD, sums, moved)
    sum_table[:, LANES:] = jnp.where(place < 2 * RPAD - LANES, moved, 0.0)


def edges_kernel(
    state,
    masses,
    reciprocals,
    rate_scale,
    energy,
    reactants,
    products,
    field_out,
    low,
    high,
    own,
    to_left,
    to_right,
    scales,
    table,
    log_table,
    sum_table,
    field,
    square,
    in_sem,
    out_sem,
):
    def half_rows(half):
        return pl.ds(half * 2 * ROWS, 2 * ROWS)

    def keep(half):
        rows = half_rows(half)
        return pltpu.make_async_copy(field.at[rows], field_out.at[rows], out_sem.at[half])

    for half in range(2):
        rows = half_rows(half)
        for k in range(FIELDS):
            pltpu.make_async_copy(state.at[k, rows], field.at[rows, k], in_sem.at[half]).start()
    fill_spare(field, PLANES * ROWS)
    fill_tables(
        masses,
        reciprocals,
        rate_scale,
        energy,
        reactants,
        products,
        scales,
        table,
        log_table,
        sum_table,
        square,
    )
    lane = lax.broadcasted_iota(jnp.int32, (8, LANES), 1)
    for half in range(2):
        whole = state.at[:, half_rows(half)]
        pltpu.make_async_copy(whole, whole, in_sem.at[half]).wait()
        keep(half).start()
        planes = (2 * half, 2 * half + 1)
        for z in planes:
            for layer in range(2):
                low[z * 2 + layer] = field[z * ROWS + layer]
                high[z * 2 + layer] = field[z * ROWS + ROWS - 2 + layer]

        def gather(index, held):
            mine = (lane >> 2) == index
            result = []
            for z in planes:
                for group in range(2):
                    for part in PARTS:
                        row = field[z * ROWS + group * 32 + index, part, :]
                        turned = pltpu.roll(row, 4 * index + 2, 1)
                        result.append(jnp.where(mine, turned, held[len(result)]))
            return tuple(result)

        held = lax.fori_loop(0, 32, gather, (jnp.ones((8, LANES), f32),) * 12, unroll=2)
        for i, z in enumerate(planes):
            for n, part in enumerate(PARTS):
                for c in range(4):
                    index = (4 * lane + c) & (LANES - 1)
                    pick = lambda v: jnp.take_along_axis(v, index, axis=1, mode="promise_in_bounds")
                    value = jnp.where(
                        lane < 32, pick(held[i * 6 + n]), pick(held[i * 6 + 3 + n])
                    )
                    own[z * 4 + c, part, :] = value
                    side = to_right if c < 2 else to_left
                    side[z * 2 + c % 2, part, :] = value
    for half in range(2):
        keep(half).wait()


def edges(*operands):
    vmem = pl.BlockSpec(memory_space=pltpu.VMEM)
    hbm = pl.BlockSpec(memory_space=pl.ANY)
    rows = lambda n: jax.ShapeDtypeStruct((n, SUB, LANES), f32)
    return pl.pallas_call(
        edges_kernel,
        in_specs=[hbm] + [vmem] * 6,
        out_specs=[hbm] + [vmem] * 9,
        out_shape=[
            rows(PLANES * ROWS),
            rows(8),
            rows(8),
            rows(16),
            rows(8),
            rows(8),
            rows(2),
            jax.ShapeDtypeStruct((SUB + 8, LANES), f32),
            jax.ShapeDtypeStruct((RPAD, LANES), f32),
            jax.ShapeDtypeStruct((2 * SUB, 2 * LANES), f32),
        ],
        scratch_shapes=[
            pltpu.VMEM((PLANES * ROWS, SUB, LANES), f32),
            pltpu.VMEM((LANES, LANES), f32),
            pltpu.SemaphoreType.DMA((2,)),
            pltpu.SemaphoreType.DMA((2,)),
        ],
        compiler_params=pltpu.CompilerParams(vmem_limit_bytes=VMEM_BYTES),
    )(*operands)


def lane_flux(row, weight):
    onward = LANES - 1
    return (weight + pltpu.roll(weight, onward, 1)) * (pltpu.roll(row, onward, 1) - row)


def coefficient_step(source, target, flux, base, inv_mass, table, live):
    if flux is not None:
        before = jnp.maximum(base - LONG, 0)
        for i in range(LONG):
            flux[before + i] = lane_flux(source[before + i], target[before + i])
    result = []
    for n in range(0, LONG, CHUNK):
        at = [base + n + i for i in range(CHUNK)]
        values = diffusivity([source[i] for i in at], inv_mass, table, live)
        for i, value in zip(at, values):
            target[i] = value
        result += values
    return result


def peak_kernel(
    box_cost, box_owner, field_in, scales, table_ref, message, coef_out, field, coef, in_sem, out_sem
):
    quarter = lambda z: pl.ds(z * ROWS, ROWS)

    def fetch(z):
        return pltpu.make_async_copy(
            field_in.at[quarter(z)], field.at[quarter(z)], in_sem.at[z]
        )

    def keep(z):
        return pltpu.make_async_copy(coef.at[quarter(z)], coef_out.at[quarter(z)], out_sem.at[z])

    for z in range(PLANES):
        fetch(z).start()
    inv_mass = scales[0]
    live = live_rows()
    table = table_ref[:, : 3 * SUB + 8].astype(bf16)
    best = jnp.zeros((SUB, LANES), f32)
    for z in range(PLANES):
        fetch(z).wait()

        def body(index, best):
            at = [z * ROWS + index * CHUNK + i for i in range(CHUNK)]
            rows = [field[i] for i in at]
            for i, value in zip(at, diffusivity(rows, inv_mass, table, live)):
                coef[i] = value
                best = jnp.maximum(best, value)
            return best

        best = lax.fori_loop(0, ROWS // CHUNK, body, best, unroll=4)
        keep(z).start()
    top = 2.0 * jnp.max(best)
    device = lax.broadcasted_iota(jnp.int32, (LANES, LANES), 0)
    column = lax.broadcasted_iota(jnp.int32, (LANES, LANES), 1)
    nx, ny = lax.axis_size("gx"), lax.axis_size("gy")
    gx, gy = lax.axis_index("gx"), lax.axis_index("gy")
    same = device // ny == gx
    place = device % ny
    charged = jnp.zeros((LANES, LANES), f32)
    total = 0.0
    for p in range(2):
        for j in range(4):
            cost = box_cost[p, j].astype(f32)
            total = total + cost
            charged = charged + jnp.where(place == box_owner[p, j], cost, 0.0)
    tally = jnp.where(same, jnp.where(column == LANES - 2, charged, total), 0.0)
    corner = jnp.zeros((LANES, LANES), f32)
    for x, dx in ((0, nx - 1), (ROWS - 1, 1)):
        block = jnp.concatenate(
            [field[z * ROWS + x] for z in range(PLANES)]
            + [jnp.zeros((LANES - PLANES * SUB, LANES), f32)],
            axis=0,
        ).T
        for y, dy in ((0, ny - 1), (LANES - 1, 1)):
            there = lax.rem(gx + dx, nx) * ny + lax.rem(gy + dy, ny)
            cells = jnp.broadcast_to(block[y : y + 1], (LANES, LANES))
            corner = jnp.where(device == there, cells, corner)
    message[...] = jnp.where(
        column == LANES - 3, top, jnp.where(column > LANES - 3, tally, corner)
    )
    for z in range(PLANES):
        keep(z).wait()


def local_peak(box_cost, box_owner, field, scales, table):
    vmem = pl.BlockSpec(memory_space=pltpu.VMEM)
    smem = pl.BlockSpec(memory_space=pltpu.SMEM)
    hbm = pl.BlockSpec(memory_space=pl.ANY)
    rows = jax.ShapeDtypeStruct((PLANES * ROWS, SUB, LANES), f32)
    assert lax.axis_size("gx") * lax.axis_size("gy") == LANES
    return pl.pallas_call(
        peak_kernel,
        in_specs=[smem, smem, hbm, vmem, vmem],
        out_specs=[vmem, hbm],
        out_shape=[jax.ShapeDtypeStruct((LANES, LANES), f32), rows],
        scratch_shapes=[
            pltpu.VMEM((PLANES * ROWS, SUB, LANES), f32),
            pltpu.VMEM((PLANES * ROWS, SUB, LANES), f32),
            pltpu.SemaphoreType.DMA((PLANES,)),
            pltpu.SemaphoreType.DMA((PLANES,)),
        ],
        compiler_params=pltpu.CompilerParams(vmem_limit_bytes=VMEM_BYTES),
    )(box_cost, box_owner, field, scales, table)


def divergence_rows(source, weight, x0, count, part, onward, ends):
    lane = lax.broadcasted_iota(jnp.int32, (8, LANES), 1)
    result = [[] for _ in range(count)]
    above_flux = [None] * count
    for z in range(PLANES):
        base = z * HROWS + x0 + 1
        here = [source[base + i, part, :] for i in range(count + 2)]
        coefs = [weight[base + i, part, :] for i in range(count + 2)]
        along = [(coefs[i] + coefs[i + 1]) * (here[i + 1] - here[i]) for i in range(count + 1)]
        for i in range(count):
            c, d = here[i + 1], coefs[i + 1]
            raw, back = onward[i][z]
            entering, leaving = ends[i][z]
            total = (along[i + 1] - along[i]) + (
                jnp.where(lane == LANES - 1, leaving, raw) - jnp.where(lane == 0, entering, back)
            )
            if z < PLANES - 1:
                over = base + i + 1 + HROWS
                flux = Z_WEIGHT * ((d + weight[over, part, :]) * (source[over, part, :] - c))
                total = total + flux
            if z > 0:
                total = total - above_flux[i]
            if z < PLANES - 1:
                above_flux[i] = flux
            result[i].append((c, total))
    return result


def group_rows(source, weight, flux_at, edge_flux, group, part, count):
    x = group * count
    onward, ends = [], []
    for i in range(count):
        raws = [flux_at(i, z, part) for z in range(PLANES)]
        onward.append([(raw, pltpu.roll(raw, 1, 1)) for raw in raws])
        shift = (2 * LANES - 2 * (x + i)) & (LANES - 1)
        edges = [pltpu.roll(edge_flux[z, part, :], shift, 1) for z in range(PLANES)]
        ends.append([(edge, edge) for edge in edges])
    return divergence_rows(source, weight, x, count, part, onward, ends)


def interleaved(entering, leaving):
    lane = lax.broadcasted_iota(jnp.int32, (8, LANES), 1)
    pick = lambda v, at: jnp.take_along_axis(v, at, axis=1, mode="promise_in_bounds")
    return jnp.where(
        (lane & 1) == 1,
        pick(leaving, ((lane + 1) >> 1) & (ROWS - 1)),
        pick(entering, lane >> 1),
    )


def first_kernel(
    field_in,
    coef_in,
    below,
    above,
    left,
    right,
    own,
    scales,
    table_ref,
    out,
    field,
    coef,
    total,
    edge_flux,
    raw_flux,
    in_sem,
    out_sem,
):
    def fetch(p):
        copies = []
        for z in range(PLANES):
            held = pl.ds(z * ROWS + p * BOX, BOX)
            rows = pl.ds(z * HROWS + 2 + p * BOX, BOX)
            for n, (source, target) in enumerate(((field_in, field), (coef_in, coef))):
                copies.append(
                    pltpu.make_async_copy(source.at[held], target.at[rows], in_sem.at[p, n])
                )
        return copies

    part_way = BOX // WIDE - 1
    stages = (0, part_way, (part_way + ROWS // WIDE) // 2 + 1, ROWS // WIDE)

    def deliver(n):
        begin, end = stages[n] * WIDE, stages[n + 1] * WIDE
        rows = [pl.ds(z * ROWS + begin, end - begin) for z in range(PLANES)]
        return [pltpu.make_async_copy(total.at[r], out.at[r], out_sem.at[n]) for r in rows]

    for p in range(2):
        for copy in fetch(p):
            copy.start()
    inv_mass = scales[0]
    live = live_rows()
    table = table_ref[:, : 3 * SUB + 8].astype(bf16)
    for z in range(PLANES):
        at = [z * HROWS + 1, z * HROWS + ROWS + 2]
        halo = [below[z * 2 + 1], above[z * 2]]
        sides = [left[z * 2 + 1], own[z * 4 + 2], own[z * 4 + 1], right[z * 2]]
        coefs = diffusivity(halo + sides, inv_mass, table, live)
        for i, row, value in zip(at, halo, coefs):
            field[i] = row
            coef[i] = value
        entering = (coefs[2] + coefs[3]) * (sides[1] - sides[0])
        leaving = (coefs[4] + coefs[5]) * (sides[3] - sides[2])
        for part in PARTS:
            edge_flux[z, part, :] = interleaved(entering[part], leaving[part])

    def start_flux(group):
        for part in PARTS:
            for i in range(WIDE):
                for z in range(PLANES):
                    at = z * HROWS + group * WIDE + i + 2
                    raw_flux[i * PLANES + z, part, :] = lane_flux(
                        field[at, part, :], coef[at, part, :]
                    )

    def rows(group, carry):
        kept = lambda i, z, part: raw_flux[i * PLANES + z, part, :]
        for part in PARTS:
            for i, planes in enumerate(group_rows(field, coef, kept, edge_flux, group, part, WIDE)):
                for z, (_, value) in enumerate(planes):
                    total[z * ROWS + group * WIDE + i, part, :] = value
        start_flux(jnp.minimum(group + 1, ROWS // WIDE - 1))
        return carry

    for copy in fetch(0):
        copy.wait()
    start_flux(0)
    for n in range(3):
        if n == 1:
            for copy in fetch(1):
                copy.wait()
        lax.fori_loop(stages[n], stages[n + 1], rows, 0)
        for copy in deliver(n):
            copy.start()
    for n in range(3):
        for copy in deliver(n):
            copy.wait()


def first_divergence(*operands):
    vmem = pl.BlockSpec(memory_space=pltpu.VMEM)
    hbm = pl.BlockSpec(memory_space=pl.ANY)
    rows = lambda n: pltpu.VMEM((n, SUB, LANES), f32)
    return pl.pallas_call(
        first_kernel,
        in_specs=[hbm, hbm] + [vmem] * 7,
        out_specs=hbm,
        out_shape=jax.ShapeDtypeStruct((PLANES * ROWS, SUB, LANES), f32),
        scratch_shapes=[
            rows(PLANES * HROWS),
            rows(PLANES * HROWS),
            rows(PLANES * ROWS),
            rows(PLANES),
            rows(WIDE * PLANES),
            pltpu.SemaphoreType.DMA((2, 2)),
            pltpu.SemaphoreType.DMA((3,)),
        ],
        compiler_params=pltpu.CompilerParams(vmem_limit_bytes=VMEM_BYTES),
    )(*operands)


def swap_quarters(planes, lane):
    low_half = lane < 64
    even = ((lane >> 5) & 1) == 0
    a, b, c, d = planes
    a, c = (
        jnp.where(low_half, a, pltpu.roll(c, 64, 1)),
        jnp.where(low_half, pltpu.roll(a, 64, 1), c),
    )
    b, d = (
        jnp.where(low_half, b, pltpu.roll(d, 64, 1)),
        jnp.where(low_half, pltpu.roll(b, 64, 1), d),
    )
    a, b = (
        jnp.where(even, a, pltpu.roll(b, 32, 1)),
        jnp.where(even, pltpu.roll(a, 96, 1), b),
    )
    c, d = (
        jnp.where(even, c, pltpu.roll(d, 32, 1)),
        jnp.where(even, pltpu.roll(c, 96, 1), d),
    )
    return [a, b, c, d]


def substep_kernel(
    box_cost,
    flame_flag,
    field_in,
    total_in,
    below,
    above,
    left,
    right,
    own,
    gathered,
    scales,
    table_ref,
    log_table_ref,
    sum_table_ref,
    out,
    load_out,
    field,
    coef,
    first,
    strip_field,
    strip_coef,
    strip_first,
    fluxes,
    edge_flux,
    flux,
    spread,
    start_ref,
    conc_ref,
    ext_ref,
    out_rows,
    in_sem,
    out_sem,
):
    def fetch(p):
        copies = []
        for z in range(PLANES):
            held = pl.ds(z * ROWS + p * BOX, BOX)
            rows = pl.ds(z * HROWS + 2 + p * BOX, BOX)
            for n, (source, target) in enumerate(
                ((field_in, field), (total_in, first))
            ):
                copies.append(
                    pltpu.make_async_copy(source.at[held], target.at[rows], in_sem.at[p, n])
                )
        return copies

    for p in range(2):
        for copy in fetch(p):
            copy.start()
    inv_mass = scales[0]
    live = live_rows()
    table = table_ref[:, : 3 * SUB + 8].astype(bf16)
    lane = lax.broadcasted_iota(jnp.int32, (8, LANES), 1)
    received = gathered[...]
    columns = lax.broadcasted_iota(jnp.int32, received.shape, 1)
    peak = jnp.max(jnp.where(columns == LANES - 3, received, 0.0), keepdims=True)
    step = CFL_SAFE / ((4.0 + 2.0 * Z_WEIGHT) * peak)
    mine = jnp.sum(jnp.where(columns == LANES - 2, received, 0.0))
    everyone = jnp.sum(jnp.where(columns == LANES - 1, received, 0.0))
    load_out[0, 0] = mine / (everyone / 16.0)
    step = jnp.broadcast_to(step, (8, LANES))

    nx, ny = lax.axis_size("gx"), lax.axis_size("gy")

    def outside(dy):
        cells = []
        for dx in (1, nx - 1):
            source = lax.rem(lax.axis_index("gx") + dx, nx) * ny
            source = source + lax.rem(lax.axis_index("gy") + dy, ny)
            cells.append(jnp.broadcast_to(gathered[pl.ds(source, 1), :], received.shape))
        rows = lax.broadcasted_iota(jnp.int32, received.shape, 0)
        return jnp.where(rows == ROWS, cells[0], cells[1]).T

    corners = [outside(ny - 1), outside(1)]
    tips = (lane == ROWS) | (lane == LANES - 1)

    for z in range(PLANES):
        for layer in range(2):
            field[z * HROWS + layer] = below[z * 2 + layer]
            field[z * HROWS + ROWS + 2 + layer] = above[z * 2 + layer]
        for c in range(2):
            strip_field[z * 8 + c] = left[z * 2 + c]
            strip_field[z * 8 + 2 + c] = own[z * 4 + 2 + c]
            strip_field[z * 8 + 4 + c] = own[z * 4 + c]
            strip_field[z * 8 + 6 + c] = right[z * 2 + c]
        for n, part in enumerate(PARTS):
            rows = slice(z * SUB + n * 8, z * SUB + n * 8 + 8)
            for r, cells in ((1, corners[0]), (6, corners[1])):
                strip_field[z * 8 + r, part, :] = jnp.where(
                    tips, cells[rows], strip_field[z * 8 + r, part, :]
                )
            before = below[z * 2 + 1, part, :]
            after = above[z * 2, part, :]
            for r, column in ((2, 0), (5, LANES - 1)):
                strip_field[z * 8 + r, part, :] = jnp.where(
                    lane == LANES - 1,
                    pltpu.roll(before, LANES - 1 - column, 1),
                    jnp.where(
                        lane == ROWS,
                        pltpu.roll(after, (ROWS - column) % LANES, 1),
                        strip_field[z * 8 + r, part, :],
                    ),
                )

    def coefficients(source, target, count, kept):
        def body(index, carry):
            coefficient_step(source, target, kept, index * LONG, inv_mass, table, live)
            return carry

        lax.fori_loop(0, count // LONG, body, 0)
        if kept is not None:
            for i in range(count - LONG, count):
                kept[i] = lane_flux(source[i], target[i])

    def face(source, weight, here, there, part):
        return (weight[here, part, :] + weight[there, part, :]) * (
            source[there, part, :] - source[here, part, :]
        )

    def side_fluxes(source, weight):
        for z in range(PLANES):
            for part in PARTS:
                entering = face(source, weight, z * 8 + 1, z * 8 + 2, part)
                leaving = face(source, weight, z * 8 + 5, z * 8 + 6, part)
                fluxes[z * 2, part, :] = entering
                fluxes[z * 2 + 1, part, :] = leaving
                edge_flux[z, part, :] = interleaved(entering, leaving)

    def strip_update():
        for r in (1, 2, 5, 6):
            for part in PARTS:
                above_flux = None
                for z in range(PLANES):
                    at = z * 8 + r
                    here = strip_field[at, part, :]
                    weight = strip_coef[at, part, :]
                    total = face(strip_field, strip_coef, at, at + 1, part)
                    total = total - face(strip_field, strip_coef, at - 1, at, part)
                    onward = (weight + pltpu.roll(weight, LANES - 1, 1)) * (
                        pltpu.roll(here, LANES - 1, 1) - here
                    )
                    total = total + (onward - pltpu.roll(onward, 1, 1))
                    if above_flux is not None:
                        total = total - Z_WEIGHT * above_flux
                    if z < PLANES - 1:
                        above_flux = face(strip_field, strip_coef, at, at + 8, part)
                        total = total + Z_WEIGHT * above_flux
                    strip_first[at, part, :] = here + step * total

    def outer_row(source, weight, x, part):
        shift = -x % LANES
        onward, ends = [], []
        for z in range(PLANES):
            at = z * HROWS + x + 2
            raw = lane_flux(source[at, part, :], weight[at, part, :])
            onward.append((raw, pltpu.roll(raw, 1, 1)))
            ends.append(
                (
                    pltpu.roll(fluxes[z * 2, part, :], shift, 1),
                    pltpu.roll(fluxes[z * 2 + 1, part, :], (shift + LANES - 1) % LANES, 1),
                )
            )
        return divergence_rows(source, weight, x, 1, part, [onward], [ends])[0]

    coefficients(strip_field, strip_coef, PLANES * 8, None)
    side_fluxes(strip_field, strip_coef)
    strip_update()
    wide_step = jnp.concatenate([step] * 3, axis=0)

    def first_rows(x, carry):
        for z in range(PLANES):
            at = z * HROWS + 2 + x
            first[at] = field[at] + wide_step * first[at]
        return carry

    for p in range(2):
        for copy in fetch(p):
            copy.wait()
        lax.fori_loop(p * BOX, (p + 1) * BOX, first_rows, 0, unroll=4)
    for z in range(PLANES):
        at = [z * HROWS + x for x in (0, 1, 2, ROWS + 1, ROWS + 2, ROWS + 3)]
        for i, value in zip(at, diffusivity([field[i] for i in at], inv_mass, table, live)):
            coef[i] = value
    for x in (-1, ROWS):
        for part in PARTS:
            for z, (value, total) in enumerate(outer_row(field, coef, x, part)):
                first[z * HROWS + x + 2, part, :] = value + step * total
    for z in range(PLANES):
        first[z * HROWS] = field[z * HROWS]
        first[z * HROWS + HROWS - 1] = field[z * HROWS + HROWS - 1]
        at = [z * 8 + r for r in (1, 2, 5, 6)]
        rows = [strip_first[i] for i in at]
        for i, value in zip(at, diffusivity(rows, inv_mass, table, live)):
            strip_coef[i] = value
    side_fluxes(strip_first, strip_coef)
    coefficients(first, coef, PLANES * HROWS, flux)

    sub = lax.broadcasted_iota(jnp.int32, (8, LANES), 0)
    heat_row = sub == SPECIES - 16

    def pack(group):
        for n, part in enumerate(PARTS):
            for i in range(GROUP):
                planes = [spread[i * PLANES + z, part, :] for z in range(PLANES)]
                planes = swap_quarters(planes, lane)
                for j in range(4):
                    at = j * ROWS + group * GROUP + i
                    beginning = planes[j] * inv_mass[part]
                    start_ref[at, part, :] = beginning
                    conc_ref[at, part, :] = beginning
                    if n == 2:
                        heat = jnp.broadcast_to(planes[j][SPECIES - 16 : SPECIES - 15, :], sub.shape)
                        inverse = 1.0 / jnp.maximum(heat, SMALLEST)
                        high = coarse(inverse)
                        ext_ref[at, :8, :] = jnp.where(
                            heat_row,
                            high,
                            jnp.where(sub == SPECIES - 15, inverse - high, 1.0),
                        )
                        ext_ref[at, 8:, :] = jnp.where(heat_row, high, 1.0)

    def second_rows(group, carry):
        pack(jnp.maximum(group - 1, 0))
        for part in PARTS:
            kept = lambda i, z, part: flux[z * HROWS + group * GROUP + i + 2, part, :]
            rows = group_rows(first, coef, kept, edge_flux, group, part, GROUP)
            for i, planes in enumerate(rows):
                for z, (value, total) in enumerate(planes):
                    spread[i * PLANES + z, part, :] = value + step * total
        return carry

    for i in range(GROUP * PLANES):
        spread[i] = jnp.ones((SUB, LANES), f32)
    lax.fori_loop(0, ROWS // GROUP, second_rows, 0)
    pack(ROWS // GROUP - 1)

    log_table = log_table_ref[:, : 2 * SUB].astype(bf16)
    sum_table = sum_table_ref[:, : 2 * RPAD].astype(bf16)
    spare = sub >= SPECIES - 16
    mass = scales[1]
    heat_mass = scales[2] * mass

    def box(p, j):
        base = j * ROWS + p * BOX
        chunks = BOX // BOX_CHUNK

        def rates(chunk):
            at = [base + chunk * BOX_CHUNK + i for i in range(BOX_CHUNK)]
            conc = jnp.concatenate([conc_ref[i] for i in at], axis=1)
            spare_rows = jnp.concatenate([spare] * BOX_CHUNK, axis=1)
            ext = jnp.concatenate([ext_ref[i] for i in at], axis=1)
            logs = jnp.log2(conc)
            high = coarse(logs)
            low = logs - high
            stacked = jnp.concatenate(
                [
                    high[:16],
                    jnp.where(spare_rows, ext[:8], high[16:]),
                    low[:16],
                    jnp.where(spare_rows, ext[8:], low[16:]),
                ],
                axis=0,
            ).astype(bf16)
            return jnp.dot(log_table, stacked, preferred_element_type=f32)

        def advance(chunk, exponent):
            at = [base + chunk * BOX_CHUNK + i for i in range(BOX_CHUNK)]
            progress = jnp.exp2(exponent)
            high = coarse(progress)
            stacked = jnp.concatenate([high, progress - high], axis=0).astype(bf16)
            sums = jnp.dot(sum_table, stacked, preferred_element_type=f32)
            conc = jnp.concatenate([conc_ref[i] for i in at], axis=1)
            start = jnp.concatenate([start_ref[i] for i in at], axis=1)
            conc = (start + sums[:SUB, :]) * (conc / (conc + sums[SUB:, :]))
            for n, i in enumerate(at):
                conc_ref[i] = conc[:, n * LANES : (n + 1) * LANES]

        def sweep(number, inner):
            ahead = [rates(chunk) for chunk in range(AHEAD)]
            for chunk in range(chunks):
                if chunk + AHEAD < chunks:
                    ahead.append(rates(chunk + AHEAD))
                advance(chunk, ahead.pop(0))
            return inner

        lax.fori_loop(0, box_cost[p, j], sweep, 0)

    def give(p, flags, x, carry):
        planes = []
        for j in range(4):
            conc, start = conc_ref[j * ROWS + x], start_ref[j * ROWS + x]
            advanced = conc * mass
            source = jnp.sum(heat_mass * (conc - start), axis=0, keepdims=True)
            heat = start[16:, :] + jnp.broadcast_to(flags[j] * source, sub.shape)
            planes.append(
                [advanced[:8], advanced[8:16], jnp.where(heat_row, heat, advanced[16:])]
            )
        for n, part in enumerate(PARTS):
            for z, value in enumerate(swap_quarters([plane[n] for plane in planes], lane)):
                out_rows[z, x, part, :] = value
        return carry

    quarter = BOX // 2
    for p in range(2):
        for j in range(4):
            box(p, j)
        flags = [flame_flag[p, j].astype(f32) for j in range(4)]
        for n in range(2):
            begin = p * BOX + n * quarter
            rows = pl.ds(begin, quarter)
            lax.fori_loop(
                begin, begin + quarter, functools.partial(give, p, flags), 0, unroll=4
            )
            for k in range(FIELDS):
                pltpu.make_async_copy(
                    out_rows.at[:, rows, k], out.at[k, :, rows], out_sem.at[p]
                ).start()
    for p in range(2):
        whole = out.at[:, :, pl.ds(p * BOX, BOX)]
        pltpu.make_async_copy(whole, whole, out_sem.at[p]).wait()


def substep(box_cost, flame_flag, *operands):
    vmem = pl.BlockSpec(memory_space=pltpu.VMEM)
    smem = pl.BlockSpec(memory_space=pltpu.SMEM)
    hbm = pl.BlockSpec(memory_space=pl.ANY)
    rows = lambda n: pltpu.VMEM((n, SUB, LANES), f32)
    return pl.pallas_call(
        substep_kernel,
        in_specs=[smem, smem, hbm, hbm] + [vmem] * (len(operands) - 2),
        out_specs=[hbm, smem],
        out_shape=[
            jax.ShapeDtypeStruct((FIELDS, PLANES, ROWS, LANES), f32),
            jax.ShapeDtypeStruct((1, 1), f32),
        ],
        scratch_shapes=[
            rows(PLANES * HROWS),
            rows(PLANES * HROWS),
            rows(PLANES * HROWS),
            rows(32),
            rows(32),
            rows(32),
            rows(8),
            rows(4),
            rows(PLANES * HROWS),
            rows(GROUP * PLANES),
            rows(PLANES * ROWS),
            rows(PLANES * ROWS),
            pltpu.VMEM((PLANES * ROWS, 16, LANES), f32),
            pltpu.VMEM((PLANES, ROWS, SUB, LANES), f32),
            pltpu.SemaphoreType.DMA((2, 2)),
            pltpu.SemaphoreType.DMA((2,)),
        ],
        compiler_params=pltpu.CompilerParams(vmem_limit_bytes=VMEM_BYTES),
    )(box_cost, flame_flag, *operands)


def shifted(x, axis, by):
    count = lax.axis_size(axis)
    return lax.ppermute(x, axis, [(i, (i + by) % count) for i in range(count)])


def per_device(
    state,
    masses,
    reciprocals,
    rate_scale,
    energy,
    reactants,
    products,
    heat_release,
    box_cost,
    box_owner,
    flame_flag,
):
    field, low, high, own, to_left, to_right, *constants = edges(
        state.reshape(FIELDS, PLANES * ROWS, LANES),
        masses.reshape(1, -1),
        reciprocals,
        rate_scale.reshape(1, -1),
        energy.reshape(1, -1),
        reactants.T,
        products.T,
    )
    below = shifted(high, "gx", 1)
    above = shifted(low, "gx", -1)
    left = shifted(to_right, "gy", 1)
    right = shifted(to_left, "gy", -1)
    message, coef = local_peak(box_cost, box_owner, field, constants[0], constants[1])
    total = first_divergence(
        field, coef, below, above, left, right, own, constants[0], constants[1]
    )
    gathered = lax.all_to_all(message, ("gx", "gy"), 0, 0, tiled=True)
    heat = jnp.pad(heat_release, (0, SUB - SPECIES))[:, None]
    heat = jnp.broadcast_to(heat, (1, SUB, LANES))
    constants[0] = jnp.concatenate([constants[0], heat], axis=0)
    return tuple(
        substep(
            box_cost,
            flame_flag,
            field,
            total,
            below,
            above,
            left,
            right,
            own,
            gathered,
            *constants,
        )
    )


def solution(mesh):
    split = P("gx", "gy")
    whole = P(None, None, "gx", "gy")
    return jax.shard_map(
        per_device,
        mesh=mesh,
        in_specs=(whole, P(), P(), P(), P(), P(), P(), P(), split, split, split),
        out_specs=(whole, split),
        check_vma=False,
    )
```
